32 devices in a mesh: row: 16 (over z, x, core), col: 2 (over y).
Axes of the slice: x: 2, y: 2, z: 4, core: 2. Of those that a mesh axis runs over, the one named last changes fastest.
Arguments:
- covariance: float32 [16384, 16384], P('row', 'col'), may hold values from -6 to 6
- lon_courant: float32 [128, 128], replicated, may hold values from 0.05 to 0.95
- lat_courant: float32 [128, 128], replicated, may hold values from 0.05 to 0.9
- zonal_upwind_sign: int32 [128, 128], replicated, may hold values 0 or 1
- lat_sign: int32 [128, 128], replicated, may hold values 0 or 1
- cycle_counts: int32 [128], replicated, may hold values from 1 to 4
Outputs:
- forecast: float32 [16384, 16384], P('row', 'col')
The draws below stay inside these ranges and needn't reach their ends.
Inputs may be any that keep to these rules, and one draw needn't show every extreme that they name: `zonal_upwind_sign`: 1 where the wind blows toward growing longitude, 0 otherwise. `lat_sign`: 1 where the wind blows toward growing latitude, 0 otherwise.
All inputs are finite; a program needn't handle non-finite values.
Results may differ from the reference program's by a relative error of at most 0.00002.
Values sent between devices are 32-bit elements; how exact they have to be, the bound alone decides.
No kernel may reach another device: no remote copies, remote signals or barrier semaphores. Data moves between devices by JAX's collectives and lax.ppermute only.
A program may use at most 320 MiB of HBM per device.

```python
import math
import jax
import jax.numpy as jnp
from jax import lax

NLAT = 128
NLON = 128
SUBCYCLES = 4
GRID_POINTS = 16384


def set_ends(entries, key, low, largest):
    longest = entries.shape.index(max(entries.shape))
    spots = []
    for shift in (0, 1):
        where = [jax.random.randint(jax.random.fold_in(key, axis), (), 0, length) for axis, length in enumerate(entries.shape)]
        where[longest] = (where[longest] + shift) % entries.shape[longest]
        spots.append(tuple(where))
    return entries.at[spots[0]].set(low).at[spots[1]].set(largest)


def shard_levels(own_key, extent, shards, least, largest):
    gain, own = 1.0, jax.random.fold_in(own_key, 6)
    for axis_at, parts in shards:
        draws = jnp.exp(jax.random.uniform(jax.random.fold_in(own, axis_at), (parts,), jnp.float32, least / len(shards), largest / len(shards)))
        gain = gain * jnp.repeat(draws, extent[axis_at] // parts).reshape([-1 if axis == axis_at else 1 for axis in range(len(extent))])
    return gain


def normal_values(stream_key, extent, scale, bound, pieces=(), kind=jnp.bfloat16):
    values = scale * jax.random.normal(stream_key, extent, jnp.float32)
    if pieces:
        values = values * shard_levels(stream_key, extent, pieces, -0.22, 0.18)
    return jnp.clip(values, -bound, bound).astype(kind)


def setup_inputs(seed: int = 0) -> dict:
    arg_keys = jax.random.split(jax.random.key(seed), 7)
    return {
        "covariance": normal_values(arg_keys[0], (GRID_POINTS, GRID_POINTS), 1.0, 6.0, ((0, 16), (1, 2)), jnp.float32),
        "lon_courant": jnp.clip(jnp.exp(jax.random.uniform(arg_keys[1], (NLAT, NLON), jnp.float32, math.log(0.05), math.log(0.95))), 0.05, 0.95),
        "lat_courant": jnp.clip(jnp.exp(jax.random.uniform(arg_keys[2], (NLAT, NLON), jnp.float32, math.log(0.05), math.log(0.9))), 0.05, 0.9),
        "zonal_upwind_sign": set_ends((jax.random.randint(arg_keys[3], (NLAT, NLON), 0, 2) < 1).astype(jnp.int32), jax.random.fold_in(arg_keys[3], 1), 0, 1),
        "lat_sign": set_ends((jax.random.randint(arg_keys[4], (NLAT, NLON), 0, 2) < 1).astype(jnp.int32), jax.random.fold_in(arg_keys[4], 1), 0, 1),
        "cycle_counts": set_ends(jax.random.randint(arg_keys[5], (NLAT,), 1, SUBCYCLES + 1), jax.random.fold_in(arg_keys[5], 1), 1, SUBCYCLES).astype(jnp.int32),
    }


def lat_step(values, courant, upwind_sign):
    zero_row = jnp.zeros_like(values[:1])
    below_cells = jnp.concatenate([zero_row, values[:-1]], axis=0)
    above_cells = jnp.concatenate([values[1:], zero_row], axis=0)
    nearby = jnp.where(upwind_sign == 1, below_cells, above_cells)
    return values - courant * (values - nearby)


def advance(values, lon_courant, lat_courant, zonal_upwind_sign, lat_sign, cycle_counts):
    lon_rate = lon_courant[:, :, None]
    lat_rate = lat_courant[:, :, None]
    zonal_heading = zonal_upwind_sign[:, :, None]
    lat_dir = lat_sign[:, :, None]
    counts = cycle_counts[:, None, None]
    values = lat_step(values, lat_rate, lat_dir)

    def subcycle(cycle_index, current):
        cell_rate = jnp.where(cycle_index < counts, lon_rate, jnp.zeros_like(lon_rate))
        western_neighbour = jnp.roll(current, 1, axis=1)
        east_cell = jnp.roll(current, -1, axis=1)
        nearby = jnp.where(zonal_heading == 1, western_neighbour, east_cell)
        return current - cell_rate * (current - nearby)

    values = lax.fori_loop(0, SUBCYCLES, subcycle, values)
    return lat_step(values, lat_rate, lat_dir)


def reference(covariance, lon_courant, lat_courant, zonal_upwind_sign, lat_sign, cycle_counts):
    block_count = 16
    block_width = GRID_POINTS // block_count

    def zonal_pass(block):
        return advance(block, lon_courant, lat_courant, zonal_upwind_sign, lat_sign, cycle_counts)

    col_blocks = covariance.reshape(NLAT, NLON, block_count, block_width).transpose(2, 0, 1, 3)
    advanced_blocks = lax.map(zonal_pass, col_blocks)
    advanced = advanced_blocks.transpose(1, 2, 0, 3).reshape(GRID_POINTS, GRID_POINTS)
    row_block_list = advanced.reshape(block_count, block_width, NLAT, NLON).transpose(0, 2, 3, 1)
    predicted_blocks = lax.map(zonal_pass, row_block_list)
    return predicted_blocks.transpose(0, 3, 1, 2).reshape(GRID_POINTS, GRID_POINTS)
```

```python
import functools

import jax
import jax.numpy as jnp
from jax import lax
from jax.experimental import pallas as pl
from jax.experimental.pallas import tpu as pltpu
from jax.sharding import PartitionSpec as P

SUBCYCLES = 4
F32, BF16 = jnp.float32, jnp.bfloat16
LON_RATE, LAT_RATE, ZONAL, HEADING, COUNTS = range(5)
VMEM_BYTES = 56 * 1024 * 1024
HIGHEST = lax.Precision.HIGHEST


def split(values):
    high = values.astype(BF16)
    return high, (values - high.astype(F32)).astype(BF16)


def dot(left, right):
    return jnp.dot(left, right, preferred_element_type=F32)


def exact_dot(left, right):
    return jnp.dot(left, right, preferred_element_type=F32, precision=HIGHEST)


def blend(center, rate, sign, below, above):
    return center - rate * (center - jnp.where(sign > 0.5, below, above))


def table_row(tables, which, at):
    return tables[which, pl.ds(at, 1), :]


def zonal_bands(rate, sign, count):
    lons = rate.shape[-1]
    zero = jnp.zeros_like(rate)
    bands = {0: jnp.ones_like(rate)}
    for cycle in range(SUBCYCLES):
        cell = jnp.where(count > cycle, rate, 0.0)
        west = {k - 1: pltpu.roll(band, 1, 1) for k, band in bands.items()}
        east = {k + 1: pltpu.roll(band, lons - 1, 1) for k, band in bands.items()}
        bands = {
            k: blend(bands.get(k, zero), cell, sign, west.get(k, zero), east.get(k, zero))
            for k in range(-cycle - 1, cycle + 2)
        }
    return bands


def zonal_matrix(bands, lat):
    lons = bands[0].shape[-1]
    reach = lax.broadcasted_iota(jnp.int32, (lons, lons), 0) - lax.broadcasted_iota(jnp.int32, (lons, lons), 1)
    reach = jnp.where(reach < 0, reach + lons, reach)
    field = jnp.zeros((lons, lons), F32)
    for k, band in bands.items():
        field = jnp.where(reach == k % lons, band[lat:lat + 1, :], field)
    return field


def column_tables_kernel(tables, out):
    lons = tables.shape[-1]
    bands = zonal_bands(tables[LON_RATE], tables[ZONAL], tables[COUNTS])
    for lat in range(out.shape[0]):
        high, low = split(zonal_matrix(bands, lat))
        out[lat, :lons, :lons] = high
        out[lat, :lons, lons:] = low
        out[lat, lons:, :lons] = high
        out[lat, lons:, lons:] = jnp.zeros_like(low)


def row_tables_kernel(kept, tables, mats, rates, signs, pack_up, pack_down, adders):
    lons = tables.shape[-1]
    lats = mats.shape[0] - 2
    square = (lons, lons)
    above_lanes = lax.broadcasted_iota(jnp.int32, square, 0)
    lanes = lax.broadcasted_iota(jnp.int32, square, 1)
    prefix = (above_lanes <= lanes).astype(BF16)

    def spread(which, at):
        return jnp.broadcast_to(table_row(tables, which, at), square).T

    low_mat = high_mat = None
    bands = zonal_bands(tables[LON_RATE], tables[ZONAL], tables[COUNTS])
    for lat in range(lats + 2):
        mat = zonal_matrix(bands, lat + 1).T
        if lat == 1:
            low_mat = mat
        if lat == lats:
            high_mat = mat
        high, low = split(mat)
        mats[lat, :lons, :lons] = high
        mats[lat, :lons, lons:] = high
        mats[lat, lons:, :lons] = low
        mats[lat, lons:, lons:] = jnp.zeros_like(low)
        rates[lat] = spread(LAT_RATE, lat + 1)
        signs[lat] = spread(HEADING, lat + 1)

    def picks(at, wanted):
        sign = jnp.broadcast_to(table_row(tables, HEADING, at), square)
        mask = (sign > 0.5) == wanted
        rank = dot(mask.astype(BF16), prefix)
        spot = above_lanes.astype(F32) + 1.0
        return jnp.where(mask & (rank == spot), 1.0, 0.0)

    def pack(out, picked, mat, own, own_first, wanted):
        moved = exact_dot(picked, mat)
        rate = table_row(tables, LAT_RATE, own)
        sign = table_row(tables, HEADING, own)
        inner = moved * jnp.where((sign > 0.5) == wanted, rate, 0.0)
        center = moved * (1.0 - rate)
        zero = jnp.zeros_like(picked)
        raw = [picked, zero] if own_first else [zero, picked]
        mixed = [center, inner] if own_first else [inner, center]
        whole = [jnp.concatenate([top[:kept], bottom[:kept]], axis=0) for top, bottom in zip(raw, mixed)]
        high, low = split(jnp.concatenate(whole, axis=1))
        span = 2 * lons
        out[:2 * kept, :span] = high
        out[:2 * kept, span:] = high
        out[2 * kept:, :span] = low[kept:]
        out[2 * kept:, span:] = jnp.zeros((kept, span), BF16)

    pack(pack_up, picks(lats + 2, True), high_mat, lats + 1, False, True)
    pack(pack_down, picks(1, False), low_mat, 2, True, False)

    def add(place, edge, inner, mat, wanted, edge_first):
        spot = picks(edge, wanted).T
        grown = exact_dot(mat * table_row(tables, LAT_RATE, edge), spot)
        rate = spread(LAT_RATE, edge)
        reach = jnp.where((spread(HEADING, inner) > 0.5) == wanted, spread(LAT_RATE, inner), 0.0)
        here = jnp.concatenate([((1.0 - rate) * grown)[:, :kept], (rate * spot)[:, :kept]], axis=1)
        next_in = jnp.concatenate([(reach * grown)[:, :kept], jnp.zeros((lons, kept), F32)], axis=1)
        both = [here, next_in] if edge_first else [next_in, here]
        high, low = split(jnp.concatenate(both, axis=0))
        adders[place, :2 * lons] = high
        adders[place, 2 * lons:] = low

    add(0, 2, 3, low_mat, True, True)
    add(1, lats + 1, lats, high_mat, False, False)


def sweep_columns(value, tables, first, mats, held, emit, group):
    lons = tables.shape[-1]

    def rate(k):
        return table_row(tables, LAT_RATE, first + 2 + k)

    def sign(k):
        return table_row(tables, HEADING, first + 2 + k)

    for k in range(-1, group + 1):
        start = blend(value(k), rate(k), sign(k), value(k - 1), value(k + 1))
        both = dot(jnp.concatenate(split(start), axis=1), mats(k + 1))
        held[:, (k + 1) * lons:(k + 2) * lons] = both[:, :lons] + both[:, lons:]
        if k >= 1:
            at = (k - 1) * lons
            below, center, above = (held[:, at + s * lons:at + (s + 1) * lons] for s in range(3))
            emit(k - 1, blend(center, rate(k - 1), sign(k - 1), below, above))


def edge_choice(step, first_step, last_step, halo_low, halo_high, rows):
    def take(k, group, lons, low, main, high):
        if k < 0:
            span = slice((k + 2) * lons, (k + 3) * lons)
            inside = low[rows, span]
            return inside if halo_low is None else jnp.where(step == first_step, halo_low[rows, span], inside)
        if k < group:
            return main[rows, k * lons:(k + 1) * lons]
        span = slice((k - group) * lons, (k - group + 1) * lons)
        inside = high[rows, span]
        return inside if halo_high is None else jnp.where(step == last_step, halo_high[rows, span], inside)

    return take


def pick_mats(main, first_extra, second_extra, group):
    def mats(at):
        if at < group:
            return main[at]
        return first_extra[0] if at == group else second_extra[0]

    return mats


def pack_kernel(group, place, steps_all, with_halo, tables, mats, mats_a, mats_b, pack_up, pack_down, *refs):
    bottom, top = refs[0:3], refs[3:6]
    at = 6
    halos = {False: (None, None), True: (None, None)}
    if with_halo:
        halos = {False: refs[6:8], True: refs[8:10]}
        at = 10
    up, down, held, moved = refs[at:at + 4]
    lons = tables.shape[-1]
    step = place(pl.program_id(0))
    everything = slice(None)
    for is_top, refs_here, packer, out in ((True, top, pack_up, up), (False, bottom, pack_down, down)):
        choose = edge_choice(step, 0, steps_all - 1, *halos[is_top], everything)
        low, main, high = refs_here

        def emit(k, values):
            moved[:, k * lons:(k + 1) * lons] = values

        sweep_columns(
            lambda k: choose(k, group, lons, low, main, high), tables, step * group,
            pick_mats(mats, mats_a, mats_b, group), held, emit, group,
        )
        sums = dot(packer[...], jnp.concatenate(split(moved[...]), axis=0))
        kept = out.shape[0] // 2
        out[:kept] = sums[:kept]
        out[kept:] = sums[kept:2 * kept] + sums[2 * kept:]


def local_kernel(group, steps_all, tables, mats, mats_a, mats_b, row_mats, rates, signs, low, main, high,
                 halo_low, halo_high, out, held, moved, stage):
    lons = tables.shape[-1]
    step = pl.program_id(0)
    lats = row_mats.shape[0] - 2
    part = held.shape[0]

    def one(block, carry):
        rows = pl.ds(pl.multiple_of(block * part, part), part)
        choose = edge_choice(step, 0, steps_all - 1, halo_low, halo_high, rows)

        def emit(k, values):
            moved[rows, k * lons:(k + 1) * lons] = values

        sweep_columns(
            lambda k: choose(k, group, lons, low, main, high), tables, step * group,
            pick_mats(mats, mats_a, mats_b, group), held, emit, group,
        )
        return carry

    lax.fori_loop(0, main.shape[0] // part, one, 0)

    def wide(ref, at):
        return jnp.concatenate([ref[at]] * group, axis=1)

    def lat_of(ref, lat):
        return ref[lat * lons:(lat + 1) * lons, :]

    zero = jnp.zeros((lons, group * lons), F32)
    for lat in range(-1, lats + 1):
        near = [lat_of(moved, at) if 0 <= at < lats else zero for at in (lat - 1, lat, lat + 1)]
        start = blend(near[1], wide(rates, lat + 1), wide(signs, lat + 1), near[0], near[2])
        both = dot(row_mats[lat + 1], jnp.concatenate(split(start), axis=0))
        stage[(lat + 1) * lons:(lat + 2) * lons, :] = both[:lons] + both[lons:]
        if lat >= 1:
            done = lat - 1
            below, center, above = (lat_of(stage, done + s) for s in range(3))
            out[done * lons:(done + 1) * lons, :] = blend(
                center, wide(rates, done + 1), wide(signs, done + 1), below, above
            )


def add_kernel(adder, from_below, from_above, before, after):
    side = after.shape[0]

    def one(received):
        high, low = split(received[...])
        both = dot(adder[0], high)
        after[...] = before[...] + (both[:side] + (both[side:] + dot(adder[0, :side], low)))

    @pl.when(pl.program_id(0) == 0)
    def _():
        one(from_below)

    @pl.when(pl.program_id(0) == 1)
    def _():
        one(from_above)


def params():
    return pltpu.CompilerParams(vmem_limit_bytes=VMEM_BYTES)


def whole_spec(shape):
    return pl.BlockSpec(shape, lambda *_: (0,) * len(shape))


def mats_specs(group, place, side):
    return [
        pl.BlockSpec((group, side, side), lambda g: (place(g), 0, 0)),
        pl.BlockSpec((1, side, side), lambda g: (place(g) * group + group, 0, 0)),
        pl.BlockSpec((1, side, side), lambda g: (place(g) * group + group + 1, 0, 0)),
    ]


def window_specs(rows, row_block, group, place, lons, col_blocks):
    half = group // 2
    return [
        pl.BlockSpec((rows, 2 * lons), lambda g: (row_block, jnp.maximum(place(g) * half - 1, 0))),
        pl.BlockSpec((rows, group * lons), lambda g: (row_block, place(g))),
        pl.BlockSpec((rows, 2 * lons), lambda g: (row_block, jnp.minimum((place(g) + 1) * half, col_blocks - 1))),
    ]


def largest_part(total, most):
    return max(part for part in range(1, most + 1) if total % part == 0)


def cost(flops, moved):
    return pl.CostEstimate(flops=flops, bytes_accessed=moved, transcendentals=0)


def column_tables(tables, lats, lons):
    total = tables.shape[1]
    return pl.pallas_call(
        column_tables_kernel,
        grid=(total // 8,),
        in_specs=[pl.BlockSpec((tables.shape[0], 8, lons), lambda g: (0, g, 0))],
        out_specs=pl.BlockSpec((8, 2 * lons, 2 * lons), lambda g: (g, 0, 0)),
        out_shape=jax.ShapeDtypeStruct((total, 2 * lons, 2 * lons), BF16),
        compiler_params=params(),
        cost_estimate=cost(0, total * 8 * lons * lons),
        name="column_tables",
    )(tables)


def row_tables(tables, lats, lons, kept):
    side = 2 * lons
    shapes = [
        jax.ShapeDtypeStruct((lats + 2, side, side), BF16),
        jax.ShapeDtypeStruct((lats + 2, lons, lons), F32),
        jax.ShapeDtypeStruct((lats + 2, lons, lons), F32),
        jax.ShapeDtypeStruct((3 * kept, 2 * side), BF16),
        jax.ShapeDtypeStruct((3 * kept, 2 * side), BF16),
        jax.ShapeDtypeStruct((2, 2 * side, 2 * kept), BF16),
    ]
    return pl.pallas_call(
        functools.partial(row_tables_kernel, kept),
        out_shape=shapes,
        compiler_params=params(),
        name="row_tables",
    )(tables)


def pack_call(covariance, tables, mats, pack_up, pack_down, halos, group, chunk, kept):
    rows, cols = covariance.shape
    lons = tables.shape[-1]
    side = 2 * lons
    steps_all = cols // (group * lons)
    first, stride, steps = chunk
    with_halo = halos is not None
    last = rows // side - 1

    def place(g):
        return first + stride * g

    specs = [whole_spec(tables.shape)] + mats_specs(group, place, side)
    specs += [whole_spec(pack_up.shape), whole_spec(pack_down.shape)]
    specs += window_specs(side, 0, group, place, lons, cols // side)
    specs += window_specs(side, last, group, place, lons, cols // side)
    args = [tables, mats, mats, mats, pack_up, pack_down] + [covariance] * 6
    if with_halo:
        for row_block in (0, last):
            specs += [pl.BlockSpec((side, side), functools.partial(lambda b, g: (b, 0), row_block))] * 2
            args += list(halos)
    width = steps * group * lons
    sent = jax.ShapeDtypeStruct((2 * kept, width), F32)
    return pl.pallas_call(
        functools.partial(pack_kernel, group, place, steps_all, with_halo),
        grid=(steps,),
        in_specs=specs,
        out_specs=[pl.BlockSpec((2 * kept, group * lons), lambda g: (0, g))] * 2,
        out_shape=[sent, sent],
        scratch_shapes=[pltpu.VMEM((side, (group + 2) * lons), F32), pltpu.VMEM((side, group * lons), F32)],
        compiler_params=params(),
        cost_estimate=cost(0, width * side * 16),
        name="pack_edges",
    )(*args)


def local_call(covariance, tables, mats, row_mats, rates, signs, halos, group):
    rows, cols = covariance.shape
    lons = tables.shape[-1]
    side = 2 * lons
    steps_all = cols // (group * lons)
    specs = [whole_spec(tables.shape)] + mats_specs(group, lambda g: g, side)
    specs += [whole_spec(row_mats.shape), whole_spec(rates.shape), whole_spec(signs.shape)]
    specs += window_specs(rows, 0, group, lambda g: g, lons, cols // side)
    specs += [whole_spec((rows, side))] * 2
    return pl.pallas_call(
        functools.partial(local_kernel, group, steps_all),
        grid=(steps_all,),
        in_specs=specs,
        out_specs=pl.BlockSpec((rows, group * lons), lambda g: (0, g)),
        out_shape=jax.ShapeDtypeStruct((rows, cols), F32),
        scratch_shapes=[
            pltpu.VMEM((side, (group + 2) * lons), F32),
            pltpu.VMEM((rows, group * lons), F32),
            pltpu.VMEM((rows + side, group * lons), F32),
        ],
        compiler_params=params(),
        cost_estimate=cost(0, rows * cols * 16),
        name="local_forecast",
    )(tables, mats, mats, mats, row_mats, rates, signs, covariance, covariance, covariance, *halos)


def add_call(forecast, adders, from_below, from_above, chunk, group):
    rows, cols = forecast.shape
    side = adders.shape[1] // 2
    lons = side // 2
    width = group * lons
    first, stride, steps = chunk
    last = rows // side - 1
    height = from_below.shape[0]
    spot = pl.BlockSpec((side, width), lambda s, g: (s * last, first + stride * g))
    return pl.pallas_call(
        add_kernel,
        grid=(2, steps),
        in_specs=[
            pl.BlockSpec((1,) + adders.shape[1:], lambda s, g: (s, 0, 0)),
            pl.BlockSpec((height, width), lambda s, g: (0, jnp.where(s == 0, g, steps - 1))),
            pl.BlockSpec((height, width), lambda s, g: (0, jnp.where(s == 1, g, 0))),
            spot,
        ],
        out_specs=spot,
        out_shape=jax.ShapeDtypeStruct(forecast.shape, F32),
        input_output_aliases={3: 0},
        compiler_params=params(),
        cost_estimate=cost(0, 4 * side * steps * width * 4),
        name="add_edges",
    )(adders, from_below, from_above, forecast)


def neighbours(axis):
    count = lax.axis_size(axis)
    up = [(i, i + 1) for i in range(count - 1)]
    return up, [(target, source) for source, target in up]


def chunks_of(steps_all):
    if steps_all < 4:
        return [(0, 1, steps_all)]
    inner = steps_all - 2
    half = inner // 2
    return [(1, 1, half), (1 + half, 1, inner - half), (0, steps_all - 1, 2)]


def forecast_with(kept, covariance, row_part, col_part, mat_part, tall_halos):
    rows, cols = covariance.shape
    lons = row_part.shape[-1]
    group = largest_part(cols // lons, 8)
    chunks = chunks_of(cols // (group * lons))
    up, down = neighbours("row")
    col_up, col_down = neighbours("col")
    halos = (lax.ppermute(tall_halos[0], "col", col_up), lax.ppermute(tall_halos[1], "col", col_down))
    mats = column_tables(mat_part, cols // lons, lons)
    row_mats, rates, signs, pack_up, pack_down, adders = row_tables(row_part, rows // lons, lons, kept)
    arrived = []
    for chunk in chunks:
        packed_up, packed_down = pack_call(
            covariance, col_part, mats, pack_up, pack_down, halos if chunk[0] == 0 else None, group, chunk, kept
        )
        arrived.append((lax.ppermute(packed_up, "row", up), lax.ppermute(packed_down, "row", down)))
    forecast = local_call(covariance, col_part, mats, row_mats, rates, signs, halos, group)
    for chunk, (from_below, from_above) in zip(chunks, arrived):
        forecast = add_call(forecast, adders, from_below, from_above, chunk, group)
    return forecast


def per_device(covariance, lon_courant, lat_courant, zonal_upwind_sign, lat_sign, cycle_counts):
    rows, cols = covariance.shape
    lons = lon_courant.shape[1]
    row_lats, col_lats = rows // lons, cols // lons
    counts = jnp.broadcast_to(cycle_counts[:, None], lon_courant.shape)
    tables = jnp.stack(
        [t.astype(F32) for t in (lon_courant, lat_courant, zonal_upwind_sign, lat_sign, counts)]
    )
    tables = jnp.pad(tables, ((0, 0), (2, 8), (0, 0)))
    row_first = lax.axis_index("row") * row_lats
    col_first = lax.axis_index("col") * col_lats
    row_part = lax.dynamic_slice_in_dim(tables, row_first, row_lats + 4, 1)
    col_part = lax.dynamic_slice_in_dim(tables, col_first, col_lats + 4, 1)
    mat_part = lax.dynamic_slice_in_dim(tables, col_first + 1, -(-(col_lats + 2) // 8) * 8, 1)
    from_below = jnp.sum(lat_sign[row_lats::row_lats] == 1, axis=1)
    from_above = jnp.sum(lat_sign[row_lats - 1:-1:row_lats] != 1, axis=1)
    most = jnp.maximum(jnp.max(from_below), jnp.max(from_above))
    sizes = [lons * part // 16 for part in (9, 10, 11, 13, 16)]
    branch = sum((most > size).astype(jnp.int32) for size in sizes[:-1])
    tall_halos = (covariance[:, cols - 2 * lons:], covariance[:, :2 * lons])
    return lax.switch(
        branch, [functools.partial(forecast_with, size) for size in sizes],
        covariance, row_part, col_part, mat_part, tall_halos,
    )


def solution(mesh):
    placed = (P("row", "col"), P(), P(), P(), P(), P())
    return jax.shard_map(
        per_device, mesh=mesh, in_specs=placed, out_specs=P("row", "col"), check_vma=False
    )
```

```python
import functools

import jax
import jax.numpy as jnp
from jax import lax
from jax.experimental import pallas as pl
from jax.experimental.pallas import tpu as pltpu
from jax.sharding import PartitionSpec as P

SUBCYCLES = 4
F32, BF16 = jnp.float32, jnp.bfloat16
LON_RATE, LAT_RATE, ZONAL, HEADING, COUNTS = range(5)
VMEM_BYTES = 56 * 1024 * 1024
HIGHEST = lax.Precision.HIGHEST


def split(values):
    high = values.astype(BF16)
    return high, (values - high.astype(F32)).astype(BF16)


def dot(left, right):
    return jnp.dot(left, right, preferred_element_type=F32)


def exact_dot(left, right):
    return jnp.dot(left, right, preferred_element_type=F32, precision=HIGHEST)


def blend(center, rate, sign, below, above):
    return center - rate * (center - jnp.where(sign > 0.5, below, above))


def table_row(tables, which, at):
    return tables[which, pl.ds(at, 1), :]


def zonal_bands(rate, sign, count):
    lons = rate.shape[-1]
    zero = jnp.zeros_like(rate)
    bands = {0: jnp.ones_like(rate)}
    for cycle in range(SUBCYCLES):
        cell = jnp.where(count > cycle, rate, 0.0)
        west = {k - 1: pltpu.roll(band, 1, 1) for k, band in bands.items()}
        east = {k + 1: pltpu.roll(band, lons - 1, 1) for k, band in bands.items()}
        bands = {
            k: blend(bands.get(k, zero), cell, sign, west.get(k, zero), east.get(k, zero))
            for k in range(-cycle - 1, cycle + 2)
        }
    return bands


def zonal_matrix(bands, lat):
    lons = bands[0].shape[-1]
    reach = lax.broadcasted_iota(jnp.int32, (lons, lons), 0) - lax.broadcasted_iota(jnp.int32, (lons, lons), 1)
    reach = jnp.where(reach < 0, reach + lons, reach)
    field = jnp.zeros((lons, lons), F32)
    for k, band in bands.items():
        field = jnp.where(reach == k % lons, band[lat:lat + 1, :], field)
    return field


def column_tables_kernel(tables, out):
    lons = tables.shape[-1]
    bands = zonal_bands(tables[LON_RATE], tables[ZONAL], tables[COUNTS])
    for lat in range(out.shape[0]):
        high, low = split(zonal_matrix(bands, lat))
        out[lat, :lons, :lons] = high
        out[lat, :lons, lons:] = low
        out[lat, lons:, :lons] = high
        out[lat, lons:, lons:] = jnp.zeros_like(low)


def padded(count, least):
    return -(-count // least) * least


def prepare_kernel(firsts, *refs):
    sources, (row_part, col_part, first_part, mat_part, most, wide) = refs[:5], refs[5:]
    lats, lons = sources[0].shape
    wide[...] = jnp.zeros_like(wide)
    for which, source in enumerate(sources):
        wide[which, 8:8 + lats, :] = jnp.broadcast_to(source[...].astype(F32), (lats, lons))
    row_lats = row_part.shape[1] - 4
    for which in range(5):
        for out, first in ((row_part, firsts[0] + 6), (col_part, firsts[1] + 6), (first_part, firsts[2] + 7),
                           (mat_part, firsts[1] + 7)):
            out[which] = wide[which, pl.ds(first, out.shape[1]), :]
    heading = (sources[HEADING][...] == 1).astype(F32)
    upward = jnp.sum(heading, axis=1, keepdims=True)
    lat = lax.broadcasted_iota(jnp.int32, (lats, 1), 0)
    place = lat % (2 * row_lats)
    low = (place == 0) & (lat > 0)
    high = (place == 2 * row_lats - 1) & (lat < lats - 1)
    needed = jnp.where(low, upward, jnp.where(high, lons - upward, 0.0))
    most[0] = jnp.max(needed).astype(jnp.int32)


def row_tables_kernel(kept, blocks, tables, mats, rates, signs, pack_cross, pack_chip, add_cross, add_chip):
    lons = tables.shape[-1]
    lats = mats.shape[0] - 2
    square = (lons, lons)
    down = lax.broadcasted_iota(jnp.int32, square, 0)
    across = lax.broadcasted_iota(jnp.int32, square, 1)

    def spread(which, at):
        return jnp.broadcast_to(table_row(tables, which, at), square).T

    low_mat = high_mat = None
    bands = zonal_bands(tables[LON_RATE], tables[ZONAL], tables[COUNTS])
    for lat in range(lats + 2):
        mat = zonal_matrix(bands, lat + 1).T
        if lat == 1:
            low_mat = mat
        if lat == lats:
            high_mat = mat
        high, low = split(mat)
        mats[lat, :lons, :lons] = high
        mats[lat, :lons, lons:] = high
        mats[lat, lons:, :lons] = low
        mats[lat, lons:, lons:] = jnp.zeros_like(low)
        rates[lat] = spread(LAT_RATE, lat + 1)
        signs[lat] = spread(HEADING, lat + 1)

    def packer(out, size, is_low):
        edge, beyond = (2, 1) if is_low else (lats + 1, lats + 2)
        mat = low_mat if is_low else high_mat
        wanted = not is_low
        rows = padded(2 * size, 16)
        sign = jnp.broadcast_to(table_row(tables, HEADING, beyond), square)
        mask = (sign > 0.5) == wanted
        rank = dot(mask.astype(BF16), (down <= across).astype(BF16))
        rank = jnp.where(mask, rank, 0.0)[:1]
        spot = lax.broadcasted_iota(jnp.int32, (rows, lons), 0)
        first = jnp.where(spot < size, spot, -2).astype(F32) + 1.0
        second = jnp.where((spot >= size) & (spot < 2 * size), spot - size, -2).astype(F32) + 1.0
        moved = exact_dot(jnp.where(rank == first, 1.0, 0.0), mat)
        raw = jnp.where(rank == second, 1.0, 0.0)
        rate = table_row(tables, LAT_RATE, edge)
        toward = (table_row(tables, HEADING, edge) > 0.5) == wanted
        own = moved * (1.0 - rate) + raw
        inner = moved * jnp.where(toward, rate, 0.0)
        high, low = split(jnp.concatenate([own, inner] if is_low else [inner, own], axis=1))
        span = 2 * lons
        extra = padded(size, 16)
        out[:rows, :span] = high
        out[:rows, span:] = high
        out[rows:, :span] = jnp.where(spot_below(size, extra, span), low[:extra].astype(F32), 0.0).astype(BF16)
        out[rows:, span:] = jnp.zeros((extra, span), BF16)

    def spot_below(size, extra, span):
        return lax.broadcasted_iota(jnp.int32, (extra, span), 0) < size

    def adder(out, size, is_low):
        edge, inner = (2, 3) if is_low else (lats + 1, lats)
        mat = low_mat if is_low else high_mat
        columns = padded(2 * size, 16)

        def wide(which, at):
            tile = spread(which, at)
            return jnp.concatenate([tile, tile], axis=1)[:, :columns]

        mask = (wide(HEADING, edge) > 0.5) == is_low
        rank = jnp.where(mask, dot((across <= down).astype(BF16), mask.astype(BF16)), 0.0)
        spot = lax.broadcasted_iota(jnp.int32, (lons, columns), 1)
        first = jnp.where(spot < size, spot, -2).astype(F32) + 1.0
        second = jnp.where((spot >= size) & (spot < 2 * size), spot - size, -2).astype(F32) + 1.0
        partial = jnp.where(rank == first, 1.0, 0.0)
        raw = jnp.where(rank == second, 1.0, 0.0)
        grown = exact_dot(mat * table_row(tables, LAT_RATE, edge), raw)
        rate = wide(LAT_RATE, edge)
        here = (1.0 - rate) * grown + rate * partial
        next_in = jnp.where((wide(HEADING, inner) > 0.5) == is_low, wide(LAT_RATE, inner), 0.0) * grown
        high, low = split(jnp.concatenate([here, next_in] if is_low else [next_in, here], axis=0))
        out[:2 * lons] = high
        out[2 * lons:] = low

    def sides(cross_low):
        packer(pack_cross, kept, cross_low)
        packer(pack_chip, lons, not cross_low)
        adder(add_cross, kept, cross_low)
        adder(add_chip, lons, not cross_low)

    pl.when(blocks[0] == 0)(lambda: sides(True))
    pl.when(blocks[0] != 0)(lambda: sides(False))


def sweep_columns(value, tables, first, mats, held, emit, group):
    lons = tables.shape[-1]

    def rate(k):
        return table_row(tables, LAT_RATE, first + 2 + k)

    def sign(k):
        return table_row(tables, HEADING, first + 2 + k)

    for k in range(-1, group + 1):
        start = blend(value(k), rate(k), sign(k), value(k - 1), value(k + 1))
        both = dot(jnp.concatenate(split(start), axis=1), mats(k + 1))
        held[:, (k + 1) * lons:(k + 2) * lons] = both[:, :lons] + both[:, lons:]
        if k >= 1:
            at = (k - 1) * lons
            below, center, above = (held[:, at + s * lons:at + (s + 1) * lons] for s in range(3))
            emit(k - 1, blend(center, rate(k - 1), sign(k - 1), below, above))


def edge_choice(step, first_step, last_step, halo_low, halo_high, rows):
    def take(k, group, lons, low, main, high):
        if k < 0:
            span = slice((k + 2) * lons, (k + 3) * lons)
            inside = low[rows, span]
            return inside if halo_low is None else jnp.where(step == first_step, halo_low[rows, span], inside)
        if k < group:
            return main[rows, k * lons:(k + 1) * lons]
        span = slice((k - group) * lons, (k - group + 1) * lons)
        inside = high[rows, span]
        return inside if halo_high is None else jnp.where(step == last_step, halo_high[rows, span], inside)

    return take


def pick_mats(main, first_extra, second_extra, group):
    def mats(at):
        if at < group:
            return main[at]
        return first_extra[0] if at == group else second_extra[0]

    return mats


def pack_kernel(group, place, steps_all, with_halo, blocks, tables, mats, mats_a, mats_b, pack_cross, pack_chip, *refs):
    cross, chip = refs[0:3], refs[3:6]
    at = 10 if with_halo else 6
    halos = (refs[6:8], refs[8:10]) if with_halo else ((None, None), (None, None))
    out_cross, out_chip, held, moved = refs[at:at + 4]
    lons = tables.shape[-1]
    side = 2 * lons
    step = place(pl.program_id(0))
    chosen = [edge_choice(step, 0, steps_all - 1, *halo, slice(None)) for halo in halos]

    def value(k):
        return jnp.concatenate(
            [choose(k, group, lons, *parts) for choose, parts in zip(chosen, (cross, chip))], axis=0
        )

    def emit(k, values):
        moved[:, k * lons:(k + 1) * lons] = values

    sweep_columns(value, tables, step * group, pick_mats(mats, mats_a, mats_b, group), held, emit, group)
    for part, (packer, out) in enumerate(((pack_cross, out_cross), (pack_chip, out_chip))):
        sums = dot(packer[...], jnp.concatenate(split(moved[part * side:(part + 1) * side]), axis=0))
        count = out.shape[0]
        rows = padded(count, 16)
        extra = padded(count // 2, 16)
        out[:extra] = sums[:extra] + sums[rows:]
        out[extra:] = sums[extra:count]


def local_kernel(group, steps_all, tables, mats, mats_a, mats_b, row_mats, rates, signs, low, main, high,
                 halo_low, halo_high, out, held, moved, stage):
    lons = tables.shape[-1]
    step = pl.program_id(0)
    lats = row_mats.shape[0] - 2
    part = held.shape[0]

    def one(block, carry):
        rows = pl.ds(pl.multiple_of(block * part, part), part)
        choose = edge_choice(step, 0, steps_all - 1, halo_low, halo_high, rows)

        def emit(k, values):
            moved[rows, k * lons:(k + 1) * lons] = values

        sweep_columns(
            lambda k: choose(k, group, lons, low, main, high), tables, step * group,
            pick_mats(mats, mats_a, mats_b, group), held, emit, group,
        )
        return carry

    lax.fori_loop(0, main.shape[0] // part, one, 0)

    def wide(ref, at):
        return jnp.concatenate([ref[at]] * group, axis=1)

    def lat_of(ref, lat):
        return ref[lat * lons:(lat + 1) * lons, :]

    zero = jnp.zeros((lons, group * lons), F32)
    for lat in range(-1, lats + 1):
        near = [lat_of(moved, at) if 0 <= at < lats else zero for at in (lat - 1, lat, lat + 1)]
        start = blend(near[1], wide(rates, lat + 1), wide(signs, lat + 1), near[0], near[2])
        both = dot(row_mats[lat + 1], jnp.concatenate(split(start), axis=0))
        stage[(lat + 1) * lons:(lat + 2) * lons, :] = both[:lons] + both[lons:]
        if lat >= 1:
            done = lat - 1
            below, center, above = (lat_of(stage, done + s) for s in range(3))
            out[done * lons:(done + 1) * lons, :] = blend(
                center, wide(rates, done + 1), wide(signs, done + 1), below, above
            )


def add_kernel(blocks, adder, received, before, after):
    side = after.shape[0]
    columns = adder.shape[1]
    values = received[...]
    if values.shape[0] < columns:
        rest = jnp.zeros((columns - values.shape[0], values.shape[1]), F32)
        values = jnp.concatenate([values, rest], axis=0)
    high, low = split(values)
    both = dot(adder[...], high)
    after[...] = before[...] + (both[:side] + (both[side:] + dot(adder[:side], low)))


def params():
    return pltpu.CompilerParams(vmem_limit_bytes=VMEM_BYTES)


def whole_spec(shape):
    return pl.BlockSpec(shape, lambda *_: (0,) * len(shape))


def mats_specs(group, place, side):
    return [
        pl.BlockSpec((group, side, side), lambda g, *_: (place(g), 0, 0)),
        pl.BlockSpec((1, side, side), lambda g, *_: (place(g) * group + group, 0, 0)),
        pl.BlockSpec((1, side, side), lambda g, *_: (place(g) * group + group + 1, 0, 0)),
    ]


def window_specs(rows, row_block, group, place, lons, col_blocks):
    half = group // 2
    return [
        pl.BlockSpec((rows, 2 * lons), lambda g, *_: (row_block(*_), jnp.maximum(place(g) * half - 1, 0))),
        pl.BlockSpec((rows, group * lons), lambda g, *_: (row_block(*_), place(g))),
        pl.BlockSpec((rows, 2 * lons), lambda g, *_: (row_block(*_), jnp.minimum((place(g) + 1) * half, col_blocks - 1))),
    ]


def largest_part(total, most):
    return max(part for part in range(1, most + 1) if total % part == 0)


def cost(flops, moved):
    return pl.CostEstimate(flops=flops, bytes_accessed=moved, transcendentals=0)


def cost(flops, moved):
    return pl.CostEstimate(flops=flops, bytes_accessed=moved, transcendentals=0)


def prepare(firsts, sources, counts):
    lats, lons = sources[0].shape
    shapes = [jax.ShapeDtypeStruct((5, count, lons), F32) for count in counts]
    return pl.pallas_call(
        prepare_kernel,
        in_specs=[pl.BlockSpec(memory_space=pltpu.SMEM)] + [whole_spec(t.shape) for t in sources],
        out_specs=[whole_spec(shape.shape) for shape in shapes] + [pl.BlockSpec(memory_space=pltpu.SMEM)],
        out_shape=shapes + [jax.ShapeDtypeStruct((1,), jnp.int32)],
        scratch_shapes=[pltpu.VMEM((5, lats + 24, lons), F32)],
        compiler_params=params(),
        name="prepare",
    )(firsts, *sources)


def column_tables(tables, lons):
    total = tables.shape[1]
    return pl.pallas_call(
        column_tables_kernel,
        grid=(total // 8,),
        in_specs=[pl.BlockSpec((tables.shape[0], 8, lons), lambda g: (0, g, 0))],
        out_specs=pl.BlockSpec((8, 2 * lons, 2 * lons), lambda g: (g, 0, 0)),
        out_shape=jax.ShapeDtypeStruct((total, 2 * lons, 2 * lons), BF16),
        compiler_params=params(),
        cost_estimate=cost(0, total * 16 * lons * lons),
        name="column_tables",
    )(tables)


def row_tables(blocks, tables, lats, lons, kept):
    side = 2 * lons
    shapes = [
        jax.ShapeDtypeStruct((lats + 2, side, side), BF16),
        jax.ShapeDtypeStruct((lats + 2, lons, lons), F32),
        jax.ShapeDtypeStruct((lats + 2, lons, lons), F32),
    ]
    for size in (kept, lons):
        shapes.append(jax.ShapeDtypeStruct((padded(2 * size, 16) + padded(size, 16), 2 * side), BF16))
    for size in (kept, lons):
        shapes.append(jax.ShapeDtypeStruct((2 * side, padded(2 * size, 16)), BF16))
    return pl.pallas_call(
        functools.partial(row_tables_kernel, kept),
        in_specs=[pl.BlockSpec(memory_space=pltpu.SMEM), whole_spec(tables.shape)],
        out_specs=[whole_spec(shape.shape) for shape in shapes],
        out_shape=shapes,
        compiler_params=params(),
        name="row_tables",
    )(blocks, tables)


def pack_call(blocks, covariance, tables, mats, mats_first, packers, halos, group, chunk, kept):
    rows, cols = covariance.shape
    lons = tables.shape[-1]
    side = 2 * lons
    steps_all = cols // (group * lons)
    first, stride, steps = chunk
    with_halo = halos is not None

    def place(g):
        return first + stride * g

    def mats_place(g):
        return place(g) - mats_first

    specs = [whole_spec(tables.shape)] + mats_specs(group, mats_place, side)
    specs += [whole_spec(packer.shape) for packer in packers]
    for which in (0, 1):
        specs += window_specs(side, lambda b, w=which: b[w], group, place, lons, cols // side)
    args = [blocks, tables, mats, mats, mats, *packers] + [covariance] * 6
    if with_halo:
        for which in (0, 1):
            specs += [pl.BlockSpec((side, side), lambda g, b, w=which: (b[w], 0))] * 2
            args += list(halos)
    width = steps * group * lons
    sent = [jax.ShapeDtypeStruct((2 * size, width), F32) for size in (kept, lons)]
    return pl.pallas_call(
        functools.partial(pack_kernel, group, place, steps_all, with_halo),
        grid_spec=pltpu.PrefetchScalarGridSpec(
            num_scalar_prefetch=1,
            grid=(steps,),
            in_specs=specs,
            out_specs=[pl.BlockSpec((2 * size, group * lons), lambda g, *_: (0, g)) for size in (kept, lons)],
            scratch_shapes=[
                pltpu.VMEM((2 * side, (group + 2) * lons), F32),
                pltpu.VMEM((2 * side, group * lons), F32),
            ],
        ),
        out_shape=sent,
        compiler_params=params(),
        cost_estimate=cost(0, width * side * 16),
        name="pack_edges",
    )(*args)


def local_call(covariance, tables, mats, row_mats, rates, signs, halos, group):
    rows, cols = covariance.shape
    lons = tables.shape[-1]
    side = 2 * lons
    steps_all = cols // (group * lons)
    specs = [whole_spec(tables.shape)] + mats_specs(group, lambda g: g, side)
    specs += [whole_spec(row_mats.shape), whole_spec(rates.shape), whole_spec(signs.shape)]
    specs += window_specs(rows, lambda: 0, group, lambda g: g, lons, cols // side)
    specs += [whole_spec((rows, side))] * 2
    return pl.pallas_call(
        functools.partial(local_kernel, group, steps_all),
        grid=(steps_all,),
        in_specs=specs,
        out_specs=pl.BlockSpec((rows, group * lons), lambda g: (0, g)),
        out_shape=jax.ShapeDtypeStruct((rows, cols), F32),
        scratch_shapes=[
            pltpu.VMEM((side, (group + 2) * lons), F32),
            pltpu.VMEM((rows, group * lons), F32),
            pltpu.VMEM((rows + side, group * lons), F32),
        ],
        compiler_params=params(),
        cost_estimate=cost(0, rows * cols * 16),
        name="local_forecast",
    )(tables, mats, mats, mats, row_mats, rates, signs, covariance, covariance, covariance, *halos)


def add_call(blocks, which, forecast, adder, received, chunk, group):
    side = adder.shape[0] // 2
    width = group * side // 2
    first, stride, steps = chunk
    spot = pl.BlockSpec((side, width), lambda g, b: (b[which], first + stride * g))
    return pl.pallas_call(
        add_kernel,
        grid_spec=pltpu.PrefetchScalarGridSpec(
            num_scalar_prefetch=1,
            grid=(steps,),
            in_specs=[
                whole_spec(adder.shape),
                pl.BlockSpec((received.shape[0], width), lambda g, b: (0, g)),
                spot,
            ],
            out_specs=spot,
        ),
        out_shape=jax.ShapeDtypeStruct(forecast.shape, F32),
        input_output_aliases={3: 0},
        compiler_params=params(),
        cost_estimate=cost(0, 2 * side * steps * width * 4),
        name="add_edges",
    )(blocks, adder, received, forecast)


def neighbours(axis):
    count = lax.axis_size(axis)
    up = [(i, i + 1) for i in range(count - 1)]
    return up, [(target, source) for source, target in up]


def chunks_of(steps_all):
    if steps_all < 4:
        return [(0, 1, steps_all)]
    inner = steps_all - 2
    start = max(1, inner // 3)
    return [(1, 1, start), (1 + start, 1, inner - start), (0, steps_all - 1, 2)]


def swaps(axis, start):
    count = lax.axis_size(axis)
    pairs = [(i, i + 1) for i in range(start, count - 1, 2)]
    return pairs + [(b, a) for a, b in pairs]


def forecast_with(kept, covariance, blocks, row_part, col_part, first_part, mat_part, tall_halos):
    rows, cols = covariance.shape
    lons = row_part.shape[-1]
    group = largest_part(cols // lons, 8)
    chunks = chunks_of(cols // (group * lons))
    cross, chip = swaps("row", 1), swaps("row", 0)
    col_up, col_down = neighbours("col")
    halos = (lax.ppermute(tall_halos[0], "col", col_up), lax.ppermute(tall_halos[1], "col", col_down))
    row_mats, rates, signs, pack_cross, pack_chip, add_cross, add_chip = row_tables(
        blocks, row_part, rows // lons, lons, kept
    )
    packers = (pack_cross, pack_chip)
    early, late = (chunks[0], 1) if len(chunks) > 1 else (None, 0)
    arrived = []

    def send(chunk, mats, mats_first, packers, halos):
        to_cross, to_chip = pack_call(
            blocks, covariance, col_part, mats, mats_first, packers, halos, group, chunk, kept
        )
        arrived.append((lax.ppermute(to_cross, "row", cross), lax.ppermute(to_chip, "row", chip)))

    if early:
        send(early, column_tables(first_part, lons), early[0], packers, None)
    mats = column_tables(mat_part, lons)
    for chunk in chunks[late:-1]:
        send(chunk, mats, 0, packers, None)
    forecast = local_call(covariance, col_part, mats, row_mats, rates, signs, halos, group)
    forecast, packers = lax.optimization_barrier((forecast, packers))
    send(chunks[-1], mats, 0, packers, halos)
    for which, adder in ((1, add_chip), (0, add_cross)):
        for chunk, received in zip(chunks, arrived):
            forecast = add_call(blocks, which, forecast, adder, received[which], chunk, group)
    return forecast


def per_device(covariance, lon_courant, lat_courant, zonal_upwind_sign, lat_sign, cycle_counts):
    rows, cols = covariance.shape
    lons = lon_courant.shape[1]
    row_lats, col_lats = rows // lons, cols // lons
    group = largest_part(col_lats, 8)
    chunk = chunks_of(col_lats // group)[0]
    row = lax.axis_index("row")
    col_first = lax.axis_index("col") * col_lats
    firsts = jnp.stack([row * row_lats, col_first, col_first + chunk[0] * group]).astype(jnp.int32)
    last = rows // (2 * lons) - 1
    blocks = jnp.where(row % 2 == 0, jnp.array([0, last]), jnp.array([last, 0])).astype(jnp.int32)
    counts = (row_lats + 4, col_lats + 4, padded(chunk[2] * group + 2, 8), padded(col_lats + 2, 8))
    sources = (lon_courant, lat_courant, zonal_upwind_sign, lat_sign, cycle_counts[:, None])
    *parts, most = prepare(firsts, sources, counts)
    sizes = [lons * part // 32 for part in (19, 22, 32)]
    branch = sum((most[0] > size).astype(jnp.int32) for size in sizes[:-1])
    tall_halos = (covariance[:, cols - 2 * lons:], covariance[:, :2 * lons])
    return lax.switch(
        branch, [functools.partial(forecast_with, size) for size in sizes],
        covariance, blocks, *parts, tall_halos,
    )


def solution(mesh):
    placed = (P("row", "col"), P(), P(), P(), P(), P())
    return jax.shard_map(
        per_device, mesh=mesh, in_specs=placed, out_specs=P("row", "col"), check_vma=False
    )
```

```python
import functools

import jax
import jax.numpy as jnp
from jax import lax
from jax.experimental import pallas as pl
from jax.experimental.pallas import tpu as pltpu
from jax.sharding import PartitionSpec as P

SUBCYCLES = 4
F32, BF16 = jnp.float32, jnp.bfloat16
LON_RATE, LAT_RATE, ZONAL, HEADING, COUNTS = range(5)
VMEM_BYTES = 56 * 1024 * 1024
HIGHEST = lax.Precision.HIGHEST


def split(values):
    high = values.astype(BF16)
    return high, (values - high.astype(F32)).astype(BF16)


def dot(left, right):
    return jnp.dot(left, right, preferred_element_type=F32)


def exact_dot(left, right):
    return jnp.dot(left, right, preferred_element_type=F32, precision=HIGHEST)


def blend(center, rate, sign, below, above):
    return center - rate * (center - jnp.where(sign > 0.5, below, above))


def table_row(tables, which, at):
    return tables[which, pl.ds(at, 1), :]


def zonal_bands(rate, sign, count):
    lons = rate.shape[-1]
    zero = jnp.zeros_like(rate)
    bands = {0: jnp.ones_like(rate)}
    for cycle in range(SUBCYCLES):
        cell = jnp.where(count > cycle, rate, 0.0)
        west = {k - 1: pltpu.roll(band, 1, 1) for k, band in bands.items()}
        east = {k + 1: pltpu.roll(band, lons - 1, 1) for k, band in bands.items()}
        bands = {
            k: blend(bands.get(k, zero), cell, sign, west.get(k, zero), east.get(k, zero))
            for k in range(-cycle - 1, cycle + 2)
        }
    return bands


def zonal_matrix(bands, lat):
    lons = bands[0].shape[-1]
    reach = lax.broadcasted_iota(jnp.int32, (lons, lons), 0) - lax.broadcasted_iota(jnp.int32, (lons, lons), 1)
    reach = jnp.where(reach < 0, reach + lons, reach)
    field = jnp.zeros((lons, lons), F32)
    for k, band in bands.items():
        field = jnp.where(reach == k % lons, band[lat:lat + 1, :], field)
    return field


def column_tables_kernel(tables, out):
    lons = tables.shape[-1]
    bands = zonal_bands(tables[LON_RATE], tables[ZONAL], tables[COUNTS])
    for lat in range(out.shape[0]):
        high, low = split(zonal_matrix(bands, lat))
        out[lat, :lons, :lons] = high
        out[lat, :lons, lons:] = low
        out[lat, lons:, :lons] = high
        out[lat, lons:, lons:] = jnp.zeros_like(low)


def padded(count, least):
    return -(-count // least) * least


def prepare_kernel(firsts, *refs):
    sources, (row_part, col_part, first_part, mat_part, most, wide) = refs[:5], refs[5:]
    lats, lons = sources[0].shape
    wide[...] = jnp.zeros_like(wide)
    for which, source in enumerate(sources):
        wide[which, 8:8 + lats, :] = jnp.broadcast_to(source[...].astype(F32), (lats, lons))
    row_lats = row_part.shape[1] - 4
    for which in range(5):
        for out, first in ((row_part, firsts[0] + 6), (col_part, firsts[1] + 6), (first_part, firsts[2] + 7),
                           (mat_part, firsts[1] + 7)):
            out[which] = wide[which, pl.ds(first, out.shape[1]), :]
    heading = (sources[HEADING][...] == 1).astype(F32)
    upward = jnp.sum(heading, axis=1, keepdims=True)
    lat = lax.broadcasted_iota(jnp.int32, (lats, 1), 0)
    place = lat % (2 * row_lats)
    low = (place == 0) & (lat > 0)
    high = (place == 2 * row_lats - 1) & (lat < lats - 1)
    needed = jnp.where(low, upward, jnp.where(high, lons - upward, 0.0))
    most[0] = jnp.max(needed).astype(jnp.int32)


def row_tables_kernel(kept, blocks, tables, mats, rates, signs, pack_cross, add_cross):
    lons = tables.shape[-1]
    lats = mats.shape[0] - 2
    square = (lons, lons)
    down = lax.broadcasted_iota(jnp.int32, square, 0)
    across = lax.broadcasted_iota(jnp.int32, square, 1)

    def spread(which, at):
        return jnp.broadcast_to(table_row(tables, which, at), square).T

    low_mat = high_mat = None
    bands = zonal_bands(tables[LON_RATE], tables[ZONAL], tables[COUNTS])
    for lat in range(lats + 2):
        mat = zonal_matrix(bands, lat + 1).T
        if lat == 1:
            low_mat = mat
        if lat == lats:
            high_mat = mat
        high, low = split(mat)
        mats[lat, :lons, :lons] = high
        mats[lat, :lons, lons:] = high
        mats[lat, lons:, :lons] = low
        mats[lat, lons:, lons:] = jnp.zeros_like(low)
        rates[lat] = spread(LAT_RATE, lat + 1)
        signs[lat] = spread(HEADING, lat + 1)

    def packer(out, size, is_low):
        edge, beyond = (2, 1) if is_low else (lats + 1, lats + 2)
        mat = low_mat if is_low else high_mat
        wanted = not is_low
        rows = padded(2 * size, 16)
        sign = jnp.broadcast_to(table_row(tables, HEADING, beyond), square)
        mask = (sign > 0.5) == wanted
        rank = dot(mask.astype(BF16), (down <= across).astype(BF16))
        rank = jnp.where(mask, rank, 0.0)[:1]
        spot = lax.broadcasted_iota(jnp.int32, (rows, lons), 0)
        first = jnp.where(spot < size, spot, -2).astype(F32) + 1.0
        second = jnp.where((spot >= size) & (spot < 2 * size), spot - size, -2).astype(F32) + 1.0
        moved = exact_dot(jnp.where(rank == first, 1.0, 0.0), mat)
        raw = jnp.where(rank == second, 1.0, 0.0)
        rate = table_row(tables, LAT_RATE, edge)
        toward = (table_row(tables, HEADING, edge) > 0.5) == wanted
        own = moved * (1.0 - rate) + raw
        inner = moved * jnp.where(toward, rate, 0.0)
        high, low = split(jnp.concatenate([own, inner] if is_low else [inner, own], axis=1))
        span = 2 * lons
        extra = padded(size, 16)
        out[:rows, :span] = high
        out[:rows, span:] = high
        out[rows:, :span] = jnp.where(spot_below(size, extra, span), low[:extra].astype(F32), 0.0).astype(BF16)
        out[rows:, span:] = jnp.zeros((extra, span), BF16)

    def spot_below(size, extra, span):
        return lax.broadcasted_iota(jnp.int32, (extra, span), 0) < size

    def adder(out, size, is_low):
        edge, inner = (2, 3) if is_low else (lats + 1, lats)
        mat = low_mat if is_low else high_mat
        columns = padded(2 * size, 16)

        def wide(which, at):
            tile = spread(which, at)
            return jnp.concatenate([tile, tile], axis=1)[:, :columns]

        mask = (wide(HEADING, edge) > 0.5) == is_low
        rank = jnp.where(mask, dot((across <= down).astype(BF16), mask.astype(BF16)), 0.0)
        spot = lax.broadcasted_iota(jnp.int32, (lons, columns), 1)
        first = jnp.where(spot < size, spot, -2).astype(F32) + 1.0
        second = jnp.where((spot >= size) & (spot < 2 * size), spot - size, -2).astype(F32) + 1.0
        partial = jnp.where(rank == first, 1.0, 0.0)
        raw = jnp.where(rank == second, 1.0, 0.0)
        grown = exact_dot(mat * table_row(tables, LAT_RATE, edge), raw)
        rate = wide(LAT_RATE, edge)
        here = (1.0 - rate) * grown + rate * partial
        next_in = jnp.where((wide(HEADING, inner) > 0.5) == is_low, wide(LAT_RATE, inner), 0.0) * grown
        high, low = split(jnp.concatenate([here, next_in] if is_low else [next_in, here], axis=0))
        out[:2 * lons] = high
        out[2 * lons:] = low

    def sides(cross_low):
        packer(pack_cross, kept, cross_low)
        adder(add_cross, kept, cross_low)

    pl.when(blocks[0] == 0)(lambda: sides(True))
    pl.when(blocks[0] != 0)(lambda: sides(False))


def sweep_columns(value, tables, first, mats, held, emit, group):
    lons = tables.shape[-1]

    def rate(k):
        return table_row(tables, LAT_RATE, first + 2 + k)

    def sign(k):
        return table_row(tables, HEADING, first + 2 + k)

    for k in range(-1, group + 1):
        start = blend(value(k), rate(k), sign(k), value(k - 1), value(k + 1))
        both = dot(jnp.concatenate(split(start), axis=1), mats(k + 1))
        held[:, (k + 1) * lons:(k + 2) * lons] = both[:, :lons] + both[:, lons:]
        if k >= 1:
            at = (k - 1) * lons
            below, center, above = (held[:, at + s * lons:at + (s + 1) * lons] for s in range(3))
            emit(k - 1, blend(center, rate(k - 1), sign(k - 1), below, above))


def edge_choice(step, first_step, last_step, halo_low, halo_high, rows):
    def take(k, group, lons, low, main, high):
        if k < 0:
            span = slice((k + 2) * lons, (k + 3) * lons)
            inside = low[rows, span]
            return inside if halo_low is None else jnp.where(step == first_step, halo_low[rows, span], inside)
        if k < group:
            return main[rows, k * lons:(k + 1) * lons]
        span = slice((k - group) * lons, (k - group + 1) * lons)
        inside = high[rows, span]
        return inside if halo_high is None else jnp.where(step == last_step, halo_high[rows, span], inside)

    return take


def pick_mats(main, first_extra, second_extra, group):
    def mats(at):
        if at < group:
            return main[at]
        return first_extra[0] if at == group else second_extra[0]

    return mats


def pack_kernel(group, place, steps_all, blocks, tables, mats, mats_a, mats_b, packer, low, main, high, *refs):
    halos = refs[:2] if len(refs) == 5 else (None, None)
    out, held, moved = refs[-3:]
    lons = tables.shape[-1]
    step = place(pl.program_id(0))
    choose = edge_choice(step, 0, steps_all - 1, *halos, slice(None))

    def emit(k, values):
        moved[:, k * lons:(k + 1) * lons] = values

    sweep_columns(
        lambda k: choose(k, group, lons, low, main, high), tables, step * group,
        pick_mats(mats, mats_a, mats_b, group), held, emit, group,
    )
    sums = dot(packer[...], jnp.concatenate(split(moved[...]), axis=0))
    count = out.shape[0]
    rows = padded(count, 16)
    extra = padded(count // 2, 16)
    out[:extra] = sums[:extra] + sums[rows:]
    out[extra:] = sums[extra:count]


def local_kernel(group, steps_all, blocks, tables, mats, mats_a, mats_b, row_mats, rates, signs, low, main, high,
                 halo_low, halo_high, chip_low, chip_main, chip_high, chip_halos, out, held, moved, stage):
    lons = tables.shape[-1]
    side = 2 * lons
    step = pl.program_id(0)
    lats = row_mats.shape[0] - 2
    part = held.shape[0]
    weights = pick_mats(mats, mats_a, mats_b, group)
    chip_above = blocks[1] > 0
    top = (lats + 2) * lons

    @pl.when(step == 0)
    def _():
        moved[pl.ds(pl.multiple_of(jnp.where(chip_above, 0, top), lons), side), :] = jnp.zeros(
            (side, group * lons), F32
        )

    def sweep(value, held_here, first_row, count):
        def emit(k, values):
            moved[pl.ds(first_row, count), k * lons:(k + 1) * lons] = values

        sweep_columns(value, tables, step * group, weights, held_here, emit, group)

    def one(block, carry):
        first_row = pl.multiple_of(block * part, part)
        choose = edge_choice(step, 0, steps_all - 1, halo_low, halo_high, pl.ds(first_row, part))
        sweep(
            lambda k: choose(k, group, lons, low, main, high), held,
            pl.multiple_of(first_row + side, side), part,
        )
        return carry

    lax.fori_loop(0, main.shape[0] // part, one, 0)
    choose_chip = edge_choice(
        step, 0, steps_all - 1, chip_halos.at[:, :side], chip_halos.at[:, side:], slice(None)
    )
    sweep(
        lambda k: choose_chip(k, group, lons, chip_low, chip_main, chip_high), held.at[:side],
        pl.multiple_of(jnp.where(chip_above, top, 0), lons), side,
    )

    def wide(ref, at):
        return jnp.concatenate([ref[at]] * group, axis=1)

    def lat_of(ref, at):
        return ref[at * lons:(at + 1) * lons, :]

    for lat in range(-1, lats + 1):
        near = [lat_of(moved, at) for at in (lat + 1, lat + 2, lat + 3)]
        start = blend(near[1], wide(rates, lat + 1), wide(signs, lat + 1), near[0], near[2])
        both = dot(row_mats[lat + 1], jnp.concatenate(split(start), axis=0))
        stage[(lat + 1) * lons:(lat + 2) * lons, :] = both[:lons] + both[lons:]
        if lat >= 1:
            done = lat - 1
            below, center, above = (lat_of(stage, done + s) for s in range(3))
            out[done * lons:(done + 1) * lons, :] = blend(
                center, wide(rates, done + 1), wide(signs, done + 1), below, above
            )


def add_kernel(blocks, adder, received, before, after):
    side = after.shape[0]
    columns = adder.shape[1]
    values = received[...]
    if values.shape[0] < columns:
        rest = jnp.zeros((columns - values.shape[0], values.shape[1]), F32)
        values = jnp.concatenate([values, rest], axis=0)
    high, low = split(values)
    both = dot(adder[...], high)
    after[...] = before[...] + (both[:side] + (both[side:] + dot(adder[:side], low)))


def params():
    return pltpu.CompilerParams(vmem_limit_bytes=VMEM_BYTES)


def whole_spec(shape):
    return pl.BlockSpec(shape, lambda *_: (0,) * len(shape))


def mats_specs(group, place, side):
    return [
        pl.BlockSpec((group, side, side), lambda g, *_: (place(g), 0, 0)),
        pl.BlockSpec((1, side, side), lambda g, *_: (place(g) * group + group, 0, 0)),
        pl.BlockSpec((1, side, side), lambda g, *_: (place(g) * group + group + 1, 0, 0)),
    ]


def window_specs(rows, row_block, group, place, lons, col_blocks):
    half = group // 2
    return [
        pl.BlockSpec((rows, 2 * lons), lambda g, *_: (row_block(*_), jnp.maximum(place(g) * half - 1, 0))),
        pl.BlockSpec((rows, group * lons), lambda g, *_: (row_block(*_), place(g))),
        pl.BlockSpec((rows, 2 * lons), lambda g, *_: (row_block(*_), jnp.minimum((place(g) + 1) * half, col_blocks - 1))),
    ]


def largest_part(total, most):
    return max(part for part in range(1, most + 1) if total % part == 0)


def prepare(firsts, sources, counts):
    lats, lons = sources[0].shape
    shapes = [jax.ShapeDtypeStruct((5, count, lons), F32) for count in counts]
    return pl.pallas_call(
        prepare_kernel,
        in_specs=[pl.BlockSpec(memory_space=pltpu.SMEM)] + [whole_spec(t.shape) for t in sources],
        out_specs=[whole_spec(shape.shape) for shape in shapes] + [pl.BlockSpec(memory_space=pltpu.SMEM)],
        out_shape=shapes + [jax.ShapeDtypeStruct((1,), jnp.int32)],
        scratch_shapes=[pltpu.VMEM((5, lats + 24, lons), F32)],
        compiler_params=params(),
        name="prepare",
    )(firsts, *sources)


def column_tables(tables, lons):
    total = tables.shape[1]
    return pl.pallas_call(
        column_tables_kernel,
        grid=(total // 8,),
        in_specs=[pl.BlockSpec((tables.shape[0], 8, lons), lambda g: (0, g, 0))],
        out_specs=pl.BlockSpec((8, 2 * lons, 2 * lons), lambda g: (g, 0, 0)),
        out_shape=jax.ShapeDtypeStruct((total, 2 * lons, 2 * lons), BF16),
        compiler_params=params(),
        name="column_tables",
    )(tables)


def row_tables(blocks, tables, lats, lons, kept):
    side = 2 * lons
    shapes = [
        jax.ShapeDtypeStruct((lats + 2, side, side), BF16),
        jax.ShapeDtypeStruct((lats + 2, lons, lons), F32),
        jax.ShapeDtypeStruct((lats + 2, lons, lons), F32),
    ]
    shapes.append(jax.ShapeDtypeStruct((padded(2 * kept, 16) + padded(kept, 16), 2 * side), BF16))
    shapes.append(jax.ShapeDtypeStruct((2 * side, padded(2 * kept, 16)), BF16))
    return pl.pallas_call(
        functools.partial(row_tables_kernel, kept),
        in_specs=[pl.BlockSpec(memory_space=pltpu.SMEM), whole_spec(tables.shape)],
        out_specs=[whole_spec(shape.shape) for shape in shapes],
        out_shape=shapes,
        compiler_params=params(),
        name="row_tables",
    )(blocks, tables)


def pack_call(blocks, covariance, tables, mats, mats_first, packer, halos, group, chunk, kept):
    rows, cols = covariance.shape
    lons = tables.shape[-1]
    side = 2 * lons
    steps_all = cols // (group * lons)
    first, stride, steps = chunk

    def place(g):
        return first + stride * g

    def mats_place(g):
        return place(g) - mats_first

    specs = [whole_spec(tables.shape)] + mats_specs(group, mats_place, side) + [whole_spec(packer.shape)]
    specs += window_specs(side, lambda b: b[0], group, place, lons, cols // side)
    args = [blocks, tables, mats, mats, mats, packer] + [covariance] * 3
    if halos is not None:
        specs += [pl.BlockSpec((side, side), lambda g, b: (b[0], 0))] * 2
        args += list(halos)
    return pl.pallas_call(
        functools.partial(pack_kernel, group, place, steps_all),
        grid_spec=pltpu.PrefetchScalarGridSpec(
            num_scalar_prefetch=1,
            grid=(steps,),
            in_specs=specs,
            out_specs=pl.BlockSpec((2 * kept, group * lons), lambda g, *_: (0, g)),
            scratch_shapes=[
                pltpu.VMEM((side, (group + 2) * lons), F32),
                pltpu.VMEM((side, group * lons), F32),
            ],
        ),
        out_shape=jax.ShapeDtypeStruct((2 * kept, steps * group * lons), F32),
        compiler_params=params(),
        name="pack_edges",
    )(*args)


def local_call(blocks, covariance, tables, mats, row_mats, rates, signs, halos, chip_rows, chip_halos, group):
    rows, cols = covariance.shape
    lons = tables.shape[-1]
    side = 2 * lons
    steps_all = cols // (group * lons)
    part = largest_part(rows // side, 2) * side
    specs = [whole_spec(tables.shape)] + mats_specs(group, lambda g: g, side)
    specs += [whole_spec(row_mats.shape), whole_spec(rates.shape), whole_spec(signs.shape)]
    specs += window_specs(rows, lambda *_: 0, group, lambda g: g, lons, cols // side)
    specs += [whole_spec((rows, side))] * 2
    specs += window_specs(side, lambda *_: 0, group, lambda g: g, lons, cols // side)
    specs += [whole_spec(chip_halos.shape)]
    return pl.pallas_call(
        functools.partial(local_kernel, group, steps_all),
        grid_spec=pltpu.PrefetchScalarGridSpec(
            num_scalar_prefetch=1,
            grid=(steps_all,),
            in_specs=specs,
            out_specs=pl.BlockSpec((rows, group * lons), lambda g, *_: (0, g)),
            scratch_shapes=[
                pltpu.VMEM((part, (group + 2) * lons), F32),
                pltpu.VMEM((rows + 2 * side, group * lons), F32),
                pltpu.VMEM((rows + side, group * lons), F32),
            ],
        ),
        out_shape=jax.ShapeDtypeStruct((rows, cols), F32),
        compiler_params=params(),
        name="local_forecast",
    )(
        blocks, tables, mats, mats, mats, row_mats, rates, signs, covariance, covariance, covariance, *halos,
        chip_rows, chip_rows, chip_rows, chip_halos,
    )


def add_call(blocks, forecast, adder, received, chunk, group):
    side = adder.shape[0] // 2
    width = group * side // 2
    first, stride, steps = chunk
    spot = pl.BlockSpec((side, width), lambda g, b: (b[0], first + stride * g))
    return pl.pallas_call(
        add_kernel,
        grid_spec=pltpu.PrefetchScalarGridSpec(
            num_scalar_prefetch=1,
            grid=(steps,),
            in_specs=[
                whole_spec(adder.shape),
                pl.BlockSpec((received.shape[0], width), lambda g, b: (0, g)),
                spot,
            ],
            out_specs=spot,
        ),
        out_shape=jax.ShapeDtypeStruct(forecast.shape, F32),
        input_output_aliases={3: 0},
        compiler_params=params(),
        name="add_edges",
    )(blocks, adder, received, forecast)


def neighbours(axis):
    count = lax.axis_size(axis)
    up = [(i, i + 1) for i in range(count - 1)]
    return up, [(target, source) for source, target in up]


def chunks_of(steps_all):
    if steps_all < 4:
        return [(0, 1, steps_all)]
    inner = steps_all - 2
    start = max(1, inner // 3)
    return [(1, 1, start), (1 + start, 1, inner - start), (0, steps_all - 1, 2)]


def swaps(axis, start):
    count = lax.axis_size(axis)
    pairs = [(i, i + 1) for i in range(start, count - 1, 2)]
    return pairs + [(b, a) for a, b in pairs]


def forecast_with(kept, covariance, blocks, spots, row_part, col_part, first_part, mat_part):
    rows, cols = covariance.shape
    lons = row_part.shape[-1]
    side = 2 * lons
    group = largest_part(cols // lons, 8)
    chunks = chunks_of(cols // (group * lons))
    cross, chip = swaps("row", 1), swaps("row", 0)
    col_up, col_down = neighbours("col")
    row_mats, rates, signs, packer, adder = row_tables(blocks, row_part, rows // lons, lons, kept)
    arrived = []

    def pack(chunk, mats, mats_first, halos):
        return pack_call(blocks, covariance, col_part, mats, mats_first, packer, halos, group, chunk, kept)

    def send(packed):
        arrived.append(lax.ppermute(packed, "row", cross))

    early = len(chunks) > 1
    if early:
        packed = pack(chunks[0], column_tables(first_part, lons), chunks[0][0], None)
        packed, mat_part, spots = lax.optimization_barrier((packed, mat_part, spots))
        send(packed)
    tall_low = lax.dynamic_slice(covariance, (spots[0], spots[0] + cols - side), (rows, side))
    tall_high = lax.dynamic_slice(covariance, (spots[0], spots[0]), (rows, side))
    halos = (lax.ppermute(tall_low, "col", col_up), lax.ppermute(tall_high, "col", col_down))
    chip_rows = lax.ppermute(lax.dynamic_slice(covariance, (spots[1], spots[0]), (side, cols)), "row", chip)
    mats = column_tables(mat_part, lons)
    for chunk in chunks[early:-1]:
        packed, arrived[0], halos = lax.optimization_barrier((pack(chunk, mats, 0, None), arrived[0], halos))
        send(packed)
    near = [lax.dynamic_slice(halo, (spots[1], spots[0]), (side, side)) for halo in halos]
    chip_halos = lax.ppermute(jnp.concatenate(near, axis=1), "row", chip)
    packed = pack(chunks[-1], mats, 0, halos)
    packed, row_mats = lax.optimization_barrier((packed, row_mats))
    send(packed)
    forecast = local_call(
        blocks, covariance, col_part, mats, row_mats, rates, signs, halos, chip_rows, chip_halos, group
    )
    order = [0, 2, 1] if len(chunks) == 3 else range(len(chunks))
    for at in order:
        forecast = add_call(blocks, forecast, adder, arrived[at], chunks[at], group)
    return forecast


def per_device(covariance, lon_courant, lat_courant, zonal_upwind_sign, lat_sign, cycle_counts):
    rows, cols = covariance.shape
    lons = lon_courant.shape[1]
    row_lats, col_lats = rows // lons, cols // lons
    group = largest_part(col_lats, 8)
    chunk = chunks_of(col_lats // group)[0]
    row = lax.axis_index("row")
    col_first = lax.axis_index("col") * col_lats
    firsts = jnp.stack([row * row_lats, col_first, col_first + chunk[0] * group]).astype(jnp.int32)
    last = rows // (2 * lons) - 1
    blocks = jnp.where(row % 2 == 0, jnp.array([0, last]), jnp.array([last, 0])).astype(jnp.int32)
    counts = (row_lats + 4, col_lats + 4, padded(chunk[2] * group + 2, 8), padded(col_lats + 2, 8))
    sources = (lon_courant, lat_courant, zonal_upwind_sign, lat_sign, cycle_counts[:, None])
    *parts, most = prepare(firsts, sources, counts)
    sizes = [lons * part // 32 for part in (19, 22, 32)]
    branch = sum((most[0] > size).astype(jnp.int32) for size in sizes[:-1])
    spots = jnp.stack([jnp.zeros_like(row), blocks[1] * 2 * lons]).astype(jnp.int32)
    return lax.switch(
        branch, [functools.partial(forecast_with, size) for size in sizes],
        covariance, blocks, spots, *parts,
    )


def solution(mesh):
    placed = (P("row", "col"), P(), P(), P(), P(), P())
    return jax.shard_map(
        per_device, mesh=mesh, in_specs=placed, out_specs=P("row", "col"), check_vma=False
    )
```

```python
import functools

import jax
import jax.numpy as jnp
from jax import lax
from jax.experimental import pallas as pl
from jax.experimental.pallas import tpu as pltpu
from jax.sharding import PartitionSpec as P

SUBCYCLES = 4
F32, BF16 = jnp.float32, jnp.bfloat16
LON_RATE, LAT_RATE, ZONAL, HEADING, COUNTS = range(5)
VMEM_BYTES = 56 * 1024 * 1024
HIGHEST = lax.Precision.HIGHEST


def split(values):
    high = values.astype(BF16)
    return high, (values - high.astype(F32)).astype(BF16)


def dot(left, right):
    return jnp.dot(left, right, preferred_element_type=F32)


def exact_dot(left, right):
    return jnp.dot(left, right, preferred_element_type=F32, precision=HIGHEST)


def blend(center, rate, sign, below, above):
    return center - rate * (center - jnp.where(sign > 0.5, below, above))


def table_row(tables, which, at):
    return tables[which, pl.ds(at, 1), :]


def zonal_bands(rate, sign, count):
    lons = rate.shape[-1]
    zero = jnp.zeros_like(rate)
    bands = {0: jnp.ones_like(rate)}
    for cycle in range(SUBCYCLES):
        cell = jnp.where(count > cycle, rate, 0.0)
        west = {k - 1: pltpu.roll(band, 1, 1) for k, band in bands.items()}
        east = {k + 1: pltpu.roll(band, lons - 1, 1) for k, band in bands.items()}
        bands = {
            k: blend(bands.get(k, zero), cell, sign, west.get(k, zero), east.get(k, zero))
            for k in range(-cycle - 1, cycle + 2)
        }
    return bands


def zonal_matrix(bands, lat):
    lons = bands[0].shape[-1]
    reach = lax.broadcasted_iota(jnp.int32, (lons, lons), 0) - lax.broadcasted_iota(jnp.int32, (lons, lons), 1)
    reach = jnp.where(reach < 0, reach + lons, reach)
    field = jnp.zeros((lons, lons), F32)
    for k, band in bands.items():
        field = jnp.where(reach == k % lons, band[lat:lat + 1, :], field)
    return field


def column_tables_kernel(tables, out):
    lons = tables.shape[-1]
    bands = zonal_bands(tables[LON_RATE], tables[ZONAL], tables[COUNTS])
    for lat in range(out.shape[0]):
        high, low = split(zonal_matrix(bands, lat))
        out[lat, :lons, :lons] = high
        out[lat, :lons, lons:] = low
        out[lat, lons:, :lons] = high
        out[lat, lons:, lons:] = jnp.zeros_like(low)


def padded(count, least):
    return -(-count // least) * least


def prepare_kernel(first_mat, blocks_last, *refs):
    sources, (row_part, col_part, first_part, mat_part, most, blocks, wide) = refs[:5], refs[5:]
    lats, lons = sources[0].shape
    wide[...] = jnp.zeros_like(wide)
    for which, source in enumerate(sources):
        values = source[...].astype(F32)
        if which == COUNTS:
            values = jnp.broadcast_to(values, (lons, lats)).T
        wide[which, 8:8 + lats, :] = values
    row_lats = row_part.shape[1] - 4
    col_lats = col_part.shape[1] - 4
    row = lax.axis_index("row")
    col_first = lax.axis_index("col") * col_lats
    odd = row % 2
    blocks[0] = odd * blocks_last
    blocks[1] = (1 - odd) * blocks_last
    for which in range(5):
        for out, first in ((row_part, row * row_lats + 6), (col_part, col_first + 6),
                           (first_part, col_first + first_mat + 7), (mat_part, col_first + 7)):
            out[which] = wide[which, pl.ds(first, out.shape[1]), :]
    heading = (sources[HEADING][...] == 1).astype(F32)
    upward = jnp.sum(heading, axis=1, keepdims=True)
    lat = lax.broadcasted_iota(jnp.int32, (lats, 1), 0)
    place = lat % (2 * row_lats)
    low = (place == 0) & (lat > 0)
    high = (place == 2 * row_lats - 1) & (lat < lats - 1)
    needed = jnp.where(low, upward, jnp.where(high, lons - upward, 0.0))
    most[0] = jnp.max(needed).astype(jnp.int32)


def row_tables_kernel(kept, blocks, tables, covariance, mats, rates, signs, pack_cross, add_cross, tall_low, tall_high, done):
    lons = tables.shape[-1]
    side = 2 * lons
    cols = covariance.shape[1]
    copies = [
        pltpu.make_async_copy(covariance.at[:, cols - side:], tall_low, done.at[0]),
        pltpu.make_async_copy(covariance.at[:, :side], tall_high, done.at[1]),
    ]
    for copy in copies:
        copy.start()
    lats = mats.shape[0] - 2
    square = (lons, lons)
    down = lax.broadcasted_iota(jnp.int32, square, 0)
    across = lax.broadcasted_iota(jnp.int32, square, 1)

    def spread(which, at):
        return jnp.broadcast_to(table_row(tables, which, at), square).T

    low_mat = high_mat = None
    bands = zonal_bands(tables[LON_RATE], tables[ZONAL], tables[COUNTS])
    for lat in range(lats + 2):
        mat = zonal_matrix(bands, lat + 1).T
        if lat == 1:
            low_mat = mat
        if lat == lats:
            high_mat = mat
        high, low = split(mat)
        mats[lat, :lons, :lons] = high
        mats[lat, :lons, lons:] = high
        mats[lat, lons:, :lons] = low
        mats[lat, lons:, lons:] = jnp.zeros_like(low)
        rates[lat] = spread(LAT_RATE, lat + 1)
        signs[lat] = spread(HEADING, lat + 1)

    def packer(out, size, is_low):
        edge, beyond = (2, 1) if is_low else (lats + 1, lats + 2)
        mat = low_mat if is_low else high_mat
        wanted = not is_low
        rows = padded(2 * size, 16)
        sign = jnp.broadcast_to(table_row(tables, HEADING, beyond), square)
        mask = (sign > 0.5) == wanted
        rank = dot(mask.astype(BF16), (down <= across).astype(BF16))
        rank = jnp.where(mask, rank, 0.0)[:1]
        spot = lax.broadcasted_iota(jnp.int32, (rows, lons), 0)
        first = jnp.where(spot < size, spot, -2).astype(F32) + 1.0
        second = jnp.where((spot >= size) & (spot < 2 * size), spot - size, -2).astype(F32) + 1.0
        moved = exact_dot(jnp.where(rank == first, 1.0, 0.0), mat)
        raw = jnp.where(rank == second, 1.0, 0.0)
        rate = table_row(tables, LAT_RATE, edge)
        toward = (table_row(tables, HEADING, edge) > 0.5) == wanted
        own = moved * (1.0 - rate) + raw
        inner = moved * jnp.where(toward, rate, 0.0)
        high, low = split(jnp.concatenate([own, inner] if is_low else [inner, own], axis=1))
        span = 2 * lons
        extra = padded(size, 16)
        out[:rows, :span] = high
        out[:rows, span:] = high
        out[rows:, :span] = jnp.where(spot_below(size, extra, span), low[:extra].astype(F32), 0.0).astype(BF16)
        out[rows:, span:] = jnp.zeros((extra, span), BF16)

    def spot_below(size, extra, span):
        return lax.broadcasted_iota(jnp.int32, (extra, span), 0) < size

    def adder(out, size, is_low):
        edge, inner = (2, 3) if is_low else (lats + 1, lats)
        mat = low_mat if is_low else high_mat
        columns = padded(2 * size, 16)
        total = 3 * columns

        def wide(which, at):
            tile = spread(which, at)
            return jnp.concatenate([tile] * (-(-total // lons)), axis=1)[:, :total]

        mask = (wide(HEADING, edge) > 0.5) == is_low
        rank = jnp.where(mask, dot((across <= down).astype(BF16), mask.astype(BF16)), 0.0)
        place = lax.broadcasted_iota(jnp.int32, (lons, total), 1)
        spot = jnp.where(place >= columns, place - columns, place)
        spot = jnp.where(spot >= columns, spot - columns, spot)
        first = jnp.where(spot < size, spot, -2).astype(F32) + 1.0
        second = jnp.where((spot >= size) & (spot < 2 * size), spot - size, -2).astype(F32) + 1.0
        partial = jnp.where(rank == first, 1.0, 0.0)
        raw = jnp.where(rank == second, 1.0, 0.0)
        grown = exact_dot(mat * table_row(tables, LAT_RATE, edge), raw)
        rate = wide(LAT_RATE, edge)
        here = (1.0 - rate) * grown + rate * partial
        next_in = jnp.where((wide(HEADING, inner) > 0.5) == is_low, wide(LAT_RATE, inner), 0.0) * grown
        whole = jnp.concatenate([here, next_in] if is_low else [next_in, here], axis=0)
        high = whole.astype(BF16).astype(F32)
        place = lax.broadcasted_iota(jnp.int32, whole.shape, 1)
        middle = (place >= columns) & (place < 2 * columns)
        out[...] = jnp.where(middle, whole - high, high).astype(BF16)

    def sides(cross_low):
        packer(pack_cross, kept, cross_low)
        adder(add_cross, kept, cross_low)

    pl.when(blocks[0] == 0)(lambda: sides(True))
    pl.when(blocks[0] != 0)(lambda: sides(False))
    for copy in copies:
        copy.wait()


def sweep_columns(value, tables, first, mats, held, emit, group):
    lons = tables.shape[-1]

    def rate(k):
        return table_row(tables, LAT_RATE, first + 2 + k)

    def sign(k):
        return table_row(tables, HEADING, first + 2 + k)

    for k in range(-1, group + 1):
        start = blend(value(k), rate(k), sign(k), value(k - 1), value(k + 1))
        both = dot(jnp.concatenate(split(start), axis=1), mats(k + 1))
        held[:, (k + 1) * lons:(k + 2) * lons] = both[:, :lons] + both[:, lons:]
        if k >= 1:
            at = (k - 1) * lons
            below, center, above = (held[:, at + s * lons:at + (s + 1) * lons] for s in range(3))
            emit(k - 1, blend(center, rate(k - 1), sign(k - 1), below, above))


def edge_choice(step, first_step, last_step, halo_low, halo_high, rows):
    def take(k, group, lons, low, main, high):
        if k < 0:
            span = slice((k + 2) * lons, (k + 3) * lons)
            inside = low[rows, span]
            return inside if halo_low is None else jnp.where(step == first_step, halo_low[rows, span], inside)
        if k < group:
            return main[rows, k * lons:(k + 1) * lons]
        span = slice((k - group) * lons, (k - group + 1) * lons)
        inside = high[rows, span]
        return inside if halo_high is None else jnp.where(step == last_step, halo_high[rows, span], inside)

    return take


def pick_mats(main, first_extra, second_extra, group):
    def mats(at):
        if at < group:
            return main[at]
        return first_extra[0] if at == group else second_extra[0]

    return mats


def pack_kernel(group, place, steps_all, copies, blocks, tables, mats, mats_a, mats_b, packer, low, main, high, *refs):
    halos = (None, None)
    if copies:
        source, out, chip_rows, held, moved, done = refs
        side = chip_rows.shape[0]
        copy = pltpu.make_async_copy(
            source.at[pl.ds(pl.multiple_of(blocks[1] * side, side), side), :], chip_rows, done
        )
        pl.when(pl.program_id(0) == 0)(copy.start)
    else:
        halos = refs[:2] if len(refs) == 5 else halos
        out, held, moved = refs[-3:]
    lons = tables.shape[-1]
    step = place(pl.program_id(0))
    choose = edge_choice(step, 0, steps_all - 1, *halos, slice(None))

    def emit(k, values):
        moved[:, k * lons:(k + 1) * lons] = values

    sweep_columns(
        lambda k: choose(k, group, lons, low, main, high), tables, step * group,
        pick_mats(mats, mats_a, mats_b, group), held, emit, group,
    )
    sums = dot(packer[...], jnp.concatenate(split(moved[...]), axis=0))
    count = out.shape[0]
    rows = padded(count, 16)
    extra = padded(count // 2, 16)
    out[:extra] = sums[:extra] + sums[rows:]
    out[extra:] = sums[extra:count]
    if copies:
        pl.when(pl.program_id(0) == pl.num_programs(0) - 1)(copy.wait)


def local_kernel(group, steps_all, blocks, tables, mats, mats_a, mats_b, row_mats, rates, signs, low, main, high,
                 halo_low, halo_high, chip_low, chip_main, chip_high, chip_halos, out, held, moved, stage):
    lons = tables.shape[-1]
    side = 2 * lons
    step = pl.program_id(0)
    lats = row_mats.shape[0] - 2
    part = held.shape[0]
    weights = pick_mats(mats, mats_a, mats_b, group)
    chip_above = blocks[1] > 0
    top = (lats + 2) * lons

    @pl.when(step == 0)
    def _():
        moved[pl.ds(pl.multiple_of(jnp.where(chip_above, 0, top), lons), side), :] = jnp.zeros(
            (side, group * lons), F32
        )

    def sweep(value, held_here, first_row, count):
        def emit(k, values):
            moved[pl.ds(first_row, count), k * lons:(k + 1) * lons] = values

        sweep_columns(value, tables, step * group, weights, held_here, emit, group)

    def one(block, carry):
        first_row = pl.multiple_of(block * part, part)
        choose = edge_choice(step, 0, steps_all - 1, halo_low, halo_high, pl.ds(first_row, part))
        sweep(
            lambda k: choose(k, group, lons, low, main, high), held,
            pl.multiple_of(first_row + side, side), part,
        )
        return carry

    lax.fori_loop(0, main.shape[0] // part, one, 0)
    choose_chip = edge_choice(
        step, 0, steps_all - 1, chip_halos.at[:, :side], chip_halos.at[:, side:], slice(None)
    )
    sweep(
        lambda k: choose_chip(k, group, lons, chip_low, chip_main, chip_high), held.at[:side],
        pl.multiple_of(jnp.where(chip_above, top, 0), lons), side,
    )

    def wide(ref, at):
        return jnp.concatenate([ref[at]] * group, axis=1)

    def lat_of(ref, at):
        return ref[at * lons:(at + 1) * lons, :]

    for lat in range(-1, lats + 1):
        near = [lat_of(moved, at) for at in (lat + 1, lat + 2, lat + 3)]
        start = blend(near[1], wide(rates, lat + 1), wide(signs, lat + 1), near[0], near[2])
        both = dot(row_mats[lat + 1], jnp.concatenate(split(start), axis=0))
        stage[(lat + 1) * lons:(lat + 2) * lons, :] = both[:lons] + both[lons:]
        if lat >= 1:
            done = lat - 1
            below, center, above = (lat_of(stage, done + s) for s in range(3))
            out[done * lons:(done + 1) * lons, :] = blend(
                center, wide(rates, done + 1), wide(signs, done + 1), below, above
            )


def add_kernel(blocks, adder, received, before, after):
    columns = adder.shape[1] // 3
    values = received[...]
    if values.shape[0] < columns:
        rest = jnp.zeros((columns - values.shape[0], values.shape[1]), F32)
        values = jnp.concatenate([values, rest], axis=0)
    high, low = split(values)
    after[...] = before[...] + dot(adder[...], jnp.concatenate([high, high, low], axis=0))


def params():
    return pltpu.CompilerParams(vmem_limit_bytes=VMEM_BYTES)


def whole_spec(shape):
    return pl.BlockSpec(shape, lambda *_: (0,) * len(shape))


def mats_specs(group, place, side):
    return [
        pl.BlockSpec((group, side, side), lambda g, *_: (place(g), 0, 0)),
        pl.BlockSpec((1, side, side), lambda g, *_: (place(g) * group + group, 0, 0)),
        pl.BlockSpec((1, side, side), lambda g, *_: (place(g) * group + group + 1, 0, 0)),
    ]


def window_specs(rows, row_block, group, place, lons, col_blocks):
    half = group // 2
    return [
        pl.BlockSpec((rows, 2 * lons), lambda g, *_: (row_block(*_), jnp.maximum(place(g) * half - 1, 0))),
        pl.BlockSpec((rows, group * lons), lambda g, *_: (row_block(*_), place(g))),
        pl.BlockSpec((rows, 2 * lons), lambda g, *_: (row_block(*_), jnp.minimum((place(g) + 1) * half, col_blocks - 1))),
    ]


def largest_part(total, most):
    return max(part for part in range(1, most + 1) if total % part == 0)


def prepare(sources, counts, first_mat, blocks_last):
    lats, lons = sources[0].shape
    shapes = [jax.ShapeDtypeStruct((5, count, lons), F32) for count in counts]
    scalars = [jax.ShapeDtypeStruct((1,), jnp.int32), jax.ShapeDtypeStruct((2,), jnp.int32)]
    return pl.pallas_call(
        functools.partial(prepare_kernel, first_mat, blocks_last),
        in_specs=[whole_spec(t.shape) for t in sources],
        out_specs=[whole_spec(shape.shape) for shape in shapes] + [pl.BlockSpec(memory_space=pltpu.SMEM)] * 2,
        out_shape=shapes + scalars,
        scratch_shapes=[pltpu.VMEM((5, lats + 24, lons), F32)],
        compiler_params=params(),
        name="prepare",
    )(*sources)


def column_tables(tables, lons):
    total = tables.shape[1]
    return pl.pallas_call(
        column_tables_kernel,
        grid=(total // 8,),
        in_specs=[pl.BlockSpec((tables.shape[0], 8, lons), lambda g: (0, g, 0))],
        out_specs=pl.BlockSpec((8, 2 * lons, 2 * lons), lambda g: (g, 0, 0)),
        out_shape=jax.ShapeDtypeStruct((total, 2 * lons, 2 * lons), BF16),
        compiler_params=params(),
        name="column_tables",
    )(tables)


def row_tables(blocks, tables, covariance, kept):
    rows = covariance.shape[0]
    lons = tables.shape[-1]
    lats = rows // lons
    side = 2 * lons
    shapes = [
        jax.ShapeDtypeStruct((lats + 2, side, side), BF16),
        jax.ShapeDtypeStruct((lats + 2, lons, lons), F32),
        jax.ShapeDtypeStruct((lats + 2, lons, lons), F32),
        jax.ShapeDtypeStruct((padded(2 * kept, 16) + padded(kept, 16), 2 * side), BF16),
        jax.ShapeDtypeStruct((side, 3 * padded(2 * kept, 16)), BF16),
    ]
    tall = jax.ShapeDtypeStruct((rows, side), F32)
    here = pl.BlockSpec(memory_space=pl.ANY)
    return pl.pallas_call(
        functools.partial(row_tables_kernel, kept),
        in_specs=[pl.BlockSpec(memory_space=pltpu.SMEM), whole_spec(tables.shape), here],
        out_specs=[whole_spec(shape.shape) for shape in shapes] + [here, here],
        out_shape=shapes + [tall, tall],
        scratch_shapes=[pltpu.SemaphoreType.DMA((2,))],
        compiler_params=params(),
        name="row_tables",
    )(blocks, tables, covariance)


def pack_call(blocks, covariance, tables, mats, mats_first, packer, halos, copies, group, chunk, kept):
    rows, cols = covariance.shape
    lons = tables.shape[-1]
    side = 2 * lons
    steps_all = cols // (group * lons)
    first, stride, steps = chunk

    def place(g):
        return first + stride * g

    def mats_place(g):
        return place(g) - mats_first

    here = pl.BlockSpec(memory_space=pl.ANY)
    specs = [whole_spec(tables.shape)] + mats_specs(group, mats_place, side) + [whole_spec(packer.shape)]
    specs += window_specs(side, lambda b: b[0], group, place, lons, cols // side)
    args = [blocks, tables, mats, mats, mats, packer] + [covariance] * 3
    outs = [pl.BlockSpec((2 * kept, group * lons), lambda g, *_: (0, g))]
    shapes = [jax.ShapeDtypeStruct((2 * kept, steps * group * lons), F32)]
    scratch = [pltpu.VMEM((side, (group + 2) * lons), F32), pltpu.VMEM((side, group * lons), F32)]
    if copies:
        specs.append(here)
        args.append(covariance)
        outs.append(here)
        shapes.append(jax.ShapeDtypeStruct((side, cols), F32))
        scratch.append(pltpu.SemaphoreType.DMA)
    elif halos is not None:
        specs += [pl.BlockSpec((side, side), lambda g, b: (b[0], 0))] * 2
        args += list(halos)
    return pl.pallas_call(
        functools.partial(pack_kernel, group, place, steps_all, copies),
        grid_spec=pltpu.PrefetchScalarGridSpec(
            num_scalar_prefetch=1, grid=(steps,), in_specs=specs, out_specs=outs, scratch_shapes=scratch,
        ),
        out_shape=shapes,
        compiler_params=params(),
        name="pack_edges",
    )(*args)


def local_call(blocks, covariance, tables, mats, row_mats, rates, signs, halos, chip_rows, chip_halos, group):
    rows, cols = covariance.shape
    lons = tables.shape[-1]
    side = 2 * lons
    steps_all = cols // (group * lons)
    part = largest_part(rows // side, 2) * side
    specs = [whole_spec(tables.shape)] + mats_specs(group, lambda g: g, side)
    specs += [whole_spec(row_mats.shape), whole_spec(rates.shape), whole_spec(signs.shape)]
    specs += window_specs(rows, lambda *_: 0, group, lambda g: g, lons, cols // side)
    specs += [whole_spec((rows, side))] * 2
    specs += window_specs(side, lambda *_: 0, group, lambda g: g, lons, cols // side)
    specs += [whole_spec(chip_halos.shape)]
    return pl.pallas_call(
        functools.partial(local_kernel, group, steps_all),
        grid_spec=pltpu.PrefetchScalarGridSpec(
            num_scalar_prefetch=1,
            grid=(steps_all,),
            in_specs=specs,
            out_specs=pl.BlockSpec((rows, group * lons), lambda g, *_: (0, g)),
            scratch_shapes=[
                pltpu.VMEM((part, (group + 2) * lons), F32),
                pltpu.VMEM((rows + 2 * side, group * lons), F32),
                pltpu.VMEM((rows + side, group * lons), F32),
            ],
        ),
        out_shape=jax.ShapeDtypeStruct((rows, cols), F32),
        compiler_params=params(),
        name="local_forecast",
    )(
        blocks, tables, mats, mats, mats, row_mats, rates, signs, covariance, covariance, covariance, *halos,
        chip_rows, chip_rows, chip_rows, chip_halos,
    )


def add_call(blocks, forecast, adder, received, chunk, group):
    side = adder.shape[0]
    width = group * side // 2
    first, stride, steps = chunk
    spot = pl.BlockSpec((side, width), lambda g, b: (b[0], first + stride * g))
    return pl.pallas_call(
        add_kernel,
        grid_spec=pltpu.PrefetchScalarGridSpec(
            num_scalar_prefetch=1,
            grid=(steps,),
            in_specs=[
                whole_spec(adder.shape),
                pl.BlockSpec((received.shape[0], width), lambda g, b: (0, g)),
                spot,
            ],
            out_specs=spot,
        ),
        out_shape=jax.ShapeDtypeStruct(forecast.shape, F32),
        input_output_aliases={3: 0},
        compiler_params=params(),
        name="add_edges",
    )(blocks, adder, received, forecast)


def neighbours(axis):
    count = lax.axis_size(axis)
    up = [(i, i + 1) for i in range(count - 1)]
    return up, [(target, source) for source, target in up]


def chunks_of(steps_all):
    if steps_all < 4:
        return [(0, 1, steps_all)]
    inner = steps_all - 2
    start = max(1, inner // 3)
    return [(1, 1, start), (1 + start, 1, inner - start), (0, steps_all - 1, 2)]


def swaps(axis, start):
    count = lax.axis_size(axis)
    pairs = [(i, i + 1) for i in range(start, count - 1, 2)]
    return pairs + [(b, a) for a, b in pairs]


def forecast_with(kept, covariance, blocks, row_part, col_part, first_part, mat_part):
    rows, cols = covariance.shape
    lons = row_part.shape[-1]
    side = 2 * lons
    group = largest_part(cols // lons, 8)
    chunks = chunks_of(cols // (group * lons))
    cross, chip = swaps("row", 1), swaps("row", 0)
    col_up, col_down = neighbours("col")
    row_mats, rates, signs, packer, adder, tall_low, tall_high = row_tables(blocks, row_part, covariance, kept)
    arrived = []

    def pack(chunk, mats, mats_first, halos=None, copies=False):
        return pack_call(blocks, covariance, col_part, mats, mats_first, packer, halos, copies, group, chunk, kept)

    def send(packed):
        arrived.append(lax.ppermute(packed, "row", cross))

    early = len(chunks) > 1
    if early:
        packed, chip_rows = pack(chunks[0], column_tables(first_part, lons), chunks[0][0], copies=True)
        packed, chip_rows, mat_part, tall_low, tall_high = lax.optimization_barrier(
            (packed, chip_rows, mat_part, tall_low, tall_high)
        )
        send(packed)
    else:
        chip_rows = lax.dynamic_slice_in_dim(covariance, blocks[1] * side, side, 0)
    chip_rows = lax.ppermute(chip_rows, "row", chip)
    halos = (lax.ppermute(tall_low, "col", col_up), lax.ppermute(tall_high, "col", col_down))
    mats = column_tables(mat_part, lons)
    for chunk in chunks[early:-1]:
        packed, arrived[0], halos = lax.optimization_barrier((pack(chunk, mats, 0)[0], arrived[0], halos))
        send(packed)
    near = [lax.dynamic_slice_in_dim(halo, blocks[1] * side, side, 0) for halo in halos]
    chip_halos = lax.ppermute(jnp.concatenate(near, axis=1), "row", chip)
    packed, row_mats = lax.optimization_barrier((pack(chunks[-1], mats, 0, halos)[0], row_mats))
    send(packed)
    forecast = local_call(
        blocks, covariance, col_part, mats, row_mats, rates, signs, halos, chip_rows, chip_halos, group
    )
    order = [0, 2, 1] if len(chunks) == 3 else range(len(chunks))
    for at in order:
        forecast = add_call(blocks, forecast, adder, arrived[at], chunks[at], group)
    return forecast


def per_device(covariance, lon_courant, lat_courant, zonal_upwind_sign, lat_sign, cycle_counts):
    rows, cols = covariance.shape
    lons = lon_courant.shape[1]
    row_lats, col_lats = rows // lons, cols // lons
    group = largest_part(col_lats, 8)
    chunk = chunks_of(col_lats // group)[0]
    counts = (row_lats + 4, col_lats + 4, padded(chunk[2] * group + 2, 8), padded(col_lats + 2, 8))
    sources = (lon_courant, lat_courant, zonal_upwind_sign, lat_sign, cycle_counts[None, :])
    *parts, most, blocks = prepare(sources, counts, chunk[0] * group, rows // (2 * lons) - 1)
    sizes = [lons * part // 32 for part in (19, 22, 32)]
    branch = sum((most[0] > size).astype(jnp.int32) for size in sizes[:-1])
    return lax.switch(
        branch, [functools.partial(forecast_with, size) for size in sizes],
        covariance, blocks, *parts,
    )


def solution(mesh):
    placed = (P("row", "col"), P(), P(), P(), P(), P())
    return jax.shard_map(
        per_device, mesh=mesh, in_specs=placed, out_specs=P("row", "col"), check_vma=False
    )
```

```python
import functools

import jax
import jax.numpy as jnp
from jax import lax
from jax.experimental import pallas as pl
from jax.experimental.pallas import tpu as pltpu
from jax.sharding import PartitionSpec as P

SUBCYCLES = 4
F32, BF16 = jnp.float32, jnp.bfloat16
LON_RATE, LAT_RATE, ZONAL, HEADING, COUNTS = range(5)
VMEM_BYTES = 56 * 1024 * 1024
HIGHEST = lax.Precision.HIGHEST


def split(values):
    high = values.astype(BF16)
    return high, (values - high.astype(F32)).astype(BF16)


def dot(left, right):
    return jnp.dot(left, right, preferred_element_type=F32)


def exact_dot(left, right):
    return jnp.dot(left, right, preferred_element_type=F32, precision=HIGHEST)


def blend(center, rate, sign, below, above):
    return center - rate * (center - jnp.where(sign > 0.5, below, above))


def table_row(tables, which, at):
    return tables[which, pl.ds(at, 1), :]


def zonal_bands(rate, sign, count):
    lons = rate.shape[-1]
    zero = jnp.zeros_like(rate)
    bands = {0: jnp.ones_like(rate)}
    for cycle in range(SUBCYCLES):
        cell = jnp.where(count > cycle, rate, 0.0)
        west = {k - 1: pltpu.roll(band, 1, 1) for k, band in bands.items()}
        east = {k + 1: pltpu.roll(band, lons - 1, 1) for k, band in bands.items()}
        bands = {
            k: blend(bands.get(k, zero), cell, sign, west.get(k, zero), east.get(k, zero))
            for k in range(-cycle - 1, cycle + 2)
        }
    return bands


def zonal_matrix(bands, lat):
    lons = bands[0].shape[-1]
    reach = lax.broadcasted_iota(jnp.int32, (lons, lons), 0) - lax.broadcasted_iota(jnp.int32, (lons, lons), 1)
    reach = jnp.where(reach < 0, reach + lons, reach)
    field = jnp.zeros((lons, lons), F32)
    for k, band in bands.items():
        field = jnp.where(reach == k % lons, band[lat:lat + 1, :], field)
    return field


def column_tables_kernel(tables, out):
    lons = tables.shape[-1]
    bands = zonal_bands(tables[LON_RATE], tables[ZONAL], tables[COUNTS])
    for lat in range(out.shape[0]):
        high, low = split(zonal_matrix(bands, lat))
        out[lat, :lons, :lons] = high
        out[lat, :lons, lons:] = low
        out[lat, lons:, :lons] = high
        out[lat, lons:, lons:] = jnp.zeros_like(low)


def padded(count, least):
    return -(-count // least) * least


def prepare_kernel(first_mat, blocks_last, *refs):
    sources, (row_part, col_part, first_part, mat_part, most, blocks, wide) = refs[:5], refs[5:]
    lats, lons = sources[0].shape
    wide[...] = jnp.zeros_like(wide)
    for which, source in enumerate(sources):
        values = source[...].astype(F32)
        if which == COUNTS:
            values = jnp.broadcast_to(values, (lons, lats)).T
        wide[which, 8:8 + lats, :] = values
    row_lats = row_part.shape[1] - 4
    col_lats = col_part.shape[1] - 4
    row = lax.axis_index("row")
    col_first = lax.axis_index("col") * col_lats
    odd = row % 2
    blocks[0] = odd * blocks_last
    blocks[1] = (1 - odd) * blocks_last
    blocks[2] = lax.axis_index("col") % 2
    for which in range(5):
        for out, first in ((row_part, row * row_lats + 6), (col_part, col_first + 6),
                           (first_part, col_first + first_mat + 7), (mat_part, col_first + 7)):
            out[which] = wide[which, pl.ds(first, out.shape[1]), :]
    heading = (sources[HEADING][...] == 1).astype(F32)
    upward = jnp.sum(heading, axis=1, keepdims=True)
    lat = lax.broadcasted_iota(jnp.int32, (lats, 1), 0)
    place = lat % (2 * row_lats)
    low = (place == 0) & (lat > 0)
    high = (place == 2 * row_lats - 1) & (lat < lats - 1)
    needed = jnp.where(low, upward, jnp.where(high, lons - upward, 0.0))
    most[0] = jnp.max(needed).astype(jnp.int32)


def row_tables_kernel(kept, blocks, tables, covariance, mats, rates, signs, pack_cross, add_cross, *refs):
    lons = tables.shape[-1]
    side = 2 * lons
    cols = covariance.shape[1]
    *sent, held, done = refs
    edges = [jnp.where(blocks[2] == at, cols - side, 0) for at in range(len(sent))]
    loads = [
        pltpu.make_async_copy(covariance.at[:, pl.ds(pl.multiple_of(edge, side), side)], held.at[at], done.at[0, at])
        for at, edge in enumerate(edges)
    ]
    stores = [pltpu.make_async_copy(held.at[at], out, done.at[1, at]) for at, out in enumerate(sent)]
    for copy in loads:
        copy.start()
    lats = mats.shape[0] - 2
    square = (lons, lons)
    down = lax.broadcasted_iota(jnp.int32, square, 0)
    across = lax.broadcasted_iota(jnp.int32, square, 1)

    def spread(which, at):
        return jnp.broadcast_to(table_row(tables, which, at), square).T

    low_mat = high_mat = None
    bands = zonal_bands(tables[LON_RATE], tables[ZONAL], tables[COUNTS])
    for lat in range(lats + 2):
        mat = zonal_matrix(bands, lat + 1).T
        if lat == 1:
            low_mat = mat
        if lat == lats:
            high_mat = mat
        high, low = split(mat)
        mats[lat, :lons, :lons] = high
        mats[lat, :lons, lons:] = high
        mats[lat, lons:, :lons] = low
        mats[lat, lons:, lons:] = jnp.zeros_like(low)
        rates[lat] = spread(LAT_RATE, lat + 1)
        signs[lat] = spread(HEADING, lat + 1)

    def packer(out, size, is_low):
        edge, beyond = (2, 1) if is_low else (lats + 1, lats + 2)
        mat = low_mat if is_low else high_mat
        wanted = not is_low
        rows = padded(2 * size, 16)
        sign = jnp.broadcast_to(table_row(tables, HEADING, beyond), square)
        mask = (sign > 0.5) == wanted
        rank = dot(mask.astype(BF16), (down <= across).astype(BF16))
        rank = jnp.where(mask, rank, 0.0)[:1]
        spot = lax.broadcasted_iota(jnp.int32, (rows, lons), 0)
        first = jnp.where(spot < size, spot, -2).astype(F32) + 1.0
        second = jnp.where((spot >= size) & (spot < 2 * size), spot - size, -2).astype(F32) + 1.0
        moved = exact_dot(jnp.where(rank == first, 1.0, 0.0), mat)
        raw = jnp.where(rank == second, 1.0, 0.0)
        rate = table_row(tables, LAT_RATE, edge)
        toward = (table_row(tables, HEADING, edge) > 0.5) == wanted
        own = moved * (1.0 - rate) + raw
        inner = moved * jnp.where(toward, rate, 0.0)
        high, low = split(jnp.concatenate([own, inner] if is_low else [inner, own], axis=1))
        span = 2 * lons
        extra = padded(size, 16)
        out[:rows, :span] = high
        out[:rows, span:] = high
        out[rows:, :span] = jnp.where(spot_below(size, extra, span), low[:extra].astype(F32), 0.0).astype(BF16)
        out[rows:, span:] = jnp.zeros((extra, span), BF16)

    def spot_below(size, extra, span):
        return lax.broadcasted_iota(jnp.int32, (extra, span), 0) < size

    def adder(out, size, is_low):
        edge, inner = (2, 3) if is_low else (lats + 1, lats)
        mat = low_mat if is_low else high_mat
        columns = padded(2 * size, 16)
        total = 3 * columns

        def wide(which, at):
            tile = spread(which, at)
            return jnp.concatenate([tile] * (-(-total // lons)), axis=1)[:, :total]

        mask = (wide(HEADING, edge) > 0.5) == is_low
        rank = jnp.where(mask, dot((across <= down).astype(BF16), mask.astype(BF16)), 0.0)
        place = lax.broadcasted_iota(jnp.int32, (lons, total), 1)
        spot = jnp.where(place >= columns, place - columns, place)
        spot = jnp.where(spot >= columns, spot - columns, spot)
        first = jnp.where(spot < size, spot, -2).astype(F32) + 1.0
        second = jnp.where((spot >= size) & (spot < 2 * size), spot - size, -2).astype(F32) + 1.0
        partial = jnp.where(rank == first, 1.0, 0.0)
        raw = jnp.where(rank == second, 1.0, 0.0)
        grown = exact_dot(mat * table_row(tables, LAT_RATE, edge), raw)
        rate = wide(LAT_RATE, edge)
        here = (1.0 - rate) * grown + rate * partial
        next_in = jnp.where((wide(HEADING, inner) > 0.5) == is_low, wide(LAT_RATE, inner), 0.0) * grown
        whole = jnp.concatenate([here, next_in] if is_low else [next_in, here], axis=0)
        high = whole.astype(BF16).astype(F32)
        place = lax.broadcasted_iota(jnp.int32, whole.shape, 1)
        middle = (place >= columns) & (place < 2 * columns)
        out[...] = jnp.where(middle, whole - high, high).astype(BF16)

    def sides(cross_low):
        packer(pack_cross, kept, cross_low)
        adder(add_cross, kept, cross_low)

    for load, store in zip(loads, stores):
        load.wait()
        store.start()
    pl.when(blocks[0] == 0)(lambda: sides(True))
    pl.when(blocks[0] != 0)(lambda: sides(False))
    for copy in stores:
        copy.wait()


def sweep_columns(value, tables, first, mats, held, emit, group):
    lons = tables.shape[-1]

    def rate(k):
        return table_row(tables, LAT_RATE, first + 2 + k)

    def sign(k):
        return table_row(tables, HEADING, first + 2 + k)

    for k in range(-1, group + 1):
        start = blend(value(k), rate(k), sign(k), value(k - 1), value(k + 1))
        both = dot(jnp.concatenate(split(start), axis=1), mats(k + 1))
        held[:, (k + 1) * lons:(k + 2) * lons] = both[:, :lons] + both[:, lons:]
        if k >= 1:
            at = (k - 1) * lons
            below, center, above = (held[:, at + s * lons:at + (s + 1) * lons] for s in range(3))
            emit(k - 1, blend(center, rate(k - 1), sign(k - 1), below, above))


def edge_choice(step, last_step, halos, odd, rows):
    def outside(span, from_pair):
        pair = halos[0][rows, span]
        other = halos[1][rows, span] if len(halos) > 1 else jnp.zeros_like(pair)
        return jnp.where(from_pair, pair, other)

    def take(k, group, lons, low, main, high):
        if k < 0:
            span = slice((k + 2) * lons, (k + 3) * lons)
            inside = low[rows, span]
            return jnp.where(step == 0, outside(span, odd == 1), inside) if halos else inside
        if k < group:
            return main[rows, k * lons:(k + 1) * lons]
        span = slice((k - group) * lons, (k - group + 1) * lons)
        inside = high[rows, span]
        return jnp.where(step == last_step, outside(span, odd == 0), inside) if halos else inside

    return take


def pick_mats(main, first_extra, second_extra, group):
    def mats(at):
        if at < group:
            return main[at]
        return first_extra[0] if at == group else second_extra[0]

    return mats


def pack_kernel(group, place, steps_all, count, copies, blocks, tables, mats, mats_a, mats_b, packer, low, main, high, *refs):
    halos = refs[:count]
    if copies:
        source, out, chip_rows, held, moved, passed, loaded, stored = refs[count:]
        side, cols = chip_rows.shape
        from_row = pl.multiple_of(blocks[1] * side, side)
        width = cols // 4
        loads, stores = [], []
        for at in range(4):
            span = slice(at * width, (at + 1) * width)
            loads.append(pltpu.make_async_copy(
                source.at[pl.ds(from_row, side), span], passed.at[:, span], loaded.at[at]
            ))
            stores.append(pltpu.make_async_copy(passed.at[:, span], chip_rows.at[:, span], stored.at[at]))

        @pl.when(pl.program_id(0) == 0)
        def _():
            for load in loads:
                load.start()
    else:
        out, held, moved = refs[count:]
    lons = tables.shape[-1]
    step = place(pl.program_id(0))
    choose = edge_choice(step, steps_all - 1, halos, blocks[2], slice(None))

    def emit(k, values):
        moved[:, k * lons:(k + 1) * lons] = values

    sweep_columns(
        lambda k: choose(k, group, lons, low, main, high), tables, step * group,
        pick_mats(mats, mats_a, mats_b, group), held, emit, group,
    )
    sums = dot(packer[...], jnp.concatenate(split(moved[...]), axis=0))
    count = out.shape[0]
    rows = padded(count, 16)
    extra = padded(count // 2, 16)
    out[:extra] = sums[:extra] + sums[rows:]
    out[extra:] = sums[extra:count]
    if copies:
        @pl.when(pl.program_id(0) == 0)
        def _():
            for load, store in zip(loads[:3], stores[:3]):
                load.wait()
                store.start()

        @pl.when(pl.program_id(0) == pl.num_programs(0) - 1)
        def _():
            loads[3].wait()
            stores[3].start()
            for store in stores:
                store.wait()


def local_kernel(group, offset, steps_all, count, blocks, tables, mats, mats_a, mats_b, row_mats, rates, signs, low, main, high,
                 chip_low, chip_main, chip_high, chip_halos, *refs):
    halos = refs[:count]
    out, held, moved, stage = refs[-4:]
    lons = tables.shape[-1]
    side = 2 * lons
    step = pl.program_id(0) + offset
    lats = row_mats.shape[0] - 2
    part = held.shape[0]
    weights = pick_mats(mats, mats_a, mats_b, group)
    chip_above = blocks[1] > 0
    top = (lats + 2) * lons

    @pl.when(pl.program_id(0) == 0)
    def _():
        moved[pl.ds(pl.multiple_of(jnp.where(chip_above, 0, top), lons), side), :] = jnp.zeros(
            (side, group * lons), F32
        )

    def sweep(value, held_here, first_row, count):
        def emit(k, values):
            moved[pl.ds(first_row, count), k * lons:(k + 1) * lons] = values

        sweep_columns(value, tables, step * group, weights, held_here, emit, group)

    def one(block, carry):
        first_row = pl.multiple_of(block * part, part)
        choose = edge_choice(step, steps_all - 1, halos, blocks[2], pl.ds(first_row, part))
        sweep(
            lambda k: choose(k, group, lons, low, main, high), held,
            pl.multiple_of(first_row + side, side), part,
        )
        return carry

    lax.fori_loop(0, main.shape[0] // part, one, 0)
    chip_sides = [chip_halos.at[:, at * side:(at + 1) * side] for at in range(count)]
    choose_chip = edge_choice(step, steps_all - 1, chip_sides, blocks[2], slice(None))
    sweep(
        lambda k: choose_chip(k, group, lons, chip_low, chip_main, chip_high), held.at[:side],
        pl.multiple_of(jnp.where(chip_above, top, 0), lons), side,
    )

    def wide(ref, at):
        return jnp.concatenate([ref[at]] * group, axis=1)

    def lat_of(ref, at):
        return ref[at * lons:(at + 1) * lons, :]

    for lat in range(-1, lats + 1):
        near = [lat_of(moved, at) for at in (lat + 1, lat + 2, lat + 3)]
        start = blend(near[1], wide(rates, lat + 1), wide(signs, lat + 1), near[0], near[2])
        both = dot(row_mats[lat + 1], jnp.concatenate(split(start), axis=0))
        stage[(lat + 1) * lons:(lat + 2) * lons, :] = both[:lons] + both[lons:]
        if lat >= 1:
            done = lat - 1
            below, center, above = (lat_of(stage, done + s) for s in range(3))
            out[done * lons:(done + 1) * lons, :] = blend(
                center, wide(rates, done + 1), wide(signs, done + 1), below, above
            )


def add_kernel(blocks, adder, received, before, after):
    columns = adder.shape[1] // 3
    values = received[...]
    if values.shape[0] < columns:
        rest = jnp.zeros((columns - values.shape[0], values.shape[1]), F32)
        values = jnp.concatenate([values, rest], axis=0)
    high, low = split(values)
    after[...] = before[...] + dot(adder[...], jnp.concatenate([high, high, low], axis=0))


def params():
    return pltpu.CompilerParams(vmem_limit_bytes=VMEM_BYTES)


def whole_spec(shape):
    return pl.BlockSpec(shape, lambda *_: (0,) * len(shape))


def mats_specs(group, place, side):
    return [
        pl.BlockSpec((group, side, side), lambda g, *_: (place(g), 0, 0)),
        pl.BlockSpec((1, side, side), lambda g, *_: (place(g) * group + group, 0, 0)),
        pl.BlockSpec((1, side, side), lambda g, *_: (place(g) * group + group + 1, 0, 0)),
    ]


def window_specs(rows, row_block, group, place, lons, col_blocks):
    half = group // 2
    return [
        pl.BlockSpec((rows, 2 * lons), lambda g, *_: (row_block(*_), jnp.maximum(place(g) * half - 1, 0))),
        pl.BlockSpec((rows, group * lons), lambda g, *_: (row_block(*_), place(g))),
        pl.BlockSpec((rows, 2 * lons), lambda g, *_: (row_block(*_), jnp.minimum((place(g) + 1) * half, col_blocks - 1))),
    ]


def largest_part(total, most):
    return max(part for part in range(1, most + 1) if total % part == 0)


def prepare(sources, counts, first_mat, blocks_last):
    lats, lons = sources[0].shape
    shapes = [jax.ShapeDtypeStruct((5, count, lons), F32) for count in counts]
    scalars = [jax.ShapeDtypeStruct((1,), jnp.int32), jax.ShapeDtypeStruct((3,), jnp.int32)]
    return pl.pallas_call(
        functools.partial(prepare_kernel, first_mat, blocks_last),
        in_specs=[whole_spec(t.shape) for t in sources],
        out_specs=[whole_spec(shape.shape) for shape in shapes] + [pl.BlockSpec(memory_space=pltpu.SMEM)] * 2,
        out_shape=shapes + scalars,
        scratch_shapes=[pltpu.VMEM((5, lats + 24, lons), F32)],
        compiler_params=params(),
        name="prepare",
    )(*sources)


def column_tables(tables, lons):
    total = tables.shape[1]
    return pl.pallas_call(
        column_tables_kernel,
        grid=(total // 8,),
        in_specs=[pl.BlockSpec((tables.shape[0], 8, lons), lambda g: (0, g, 0))],
        out_specs=pl.BlockSpec((8, 2 * lons, 2 * lons), lambda g: (g, 0, 0)),
        out_shape=jax.ShapeDtypeStruct((total, 2 * lons, 2 * lons), BF16),
        compiler_params=params(),
        name="column_tables",
    )(tables)


def row_tables(blocks, tables, covariance, kept, count):
    rows = covariance.shape[0]
    lons = tables.shape[-1]
    lats = rows // lons
    side = 2 * lons
    shapes = [
        jax.ShapeDtypeStruct((lats + 2, side, side), BF16),
        jax.ShapeDtypeStruct((lats + 2, lons, lons), F32),
        jax.ShapeDtypeStruct((lats + 2, lons, lons), F32),
        jax.ShapeDtypeStruct((padded(2 * kept, 16) + padded(kept, 16), 2 * side), BF16),
        jax.ShapeDtypeStruct((side, 3 * padded(2 * kept, 16)), BF16),
    ]
    tall = jax.ShapeDtypeStruct((rows, side), F32)
    here = pl.BlockSpec(memory_space=pl.ANY)
    return pl.pallas_call(
        functools.partial(row_tables_kernel, kept),
        in_specs=[pl.BlockSpec(memory_space=pltpu.SMEM), whole_spec(tables.shape), here],
        out_specs=[whole_spec(shape.shape) for shape in shapes] + [here] * count,
        out_shape=shapes + [tall] * count,
        scratch_shapes=[pltpu.VMEM((count, rows, side), F32), pltpu.SemaphoreType.DMA((2, count))],
        compiler_params=params(),
        name="row_tables",
    )(blocks, tables, covariance)


def pack_call(blocks, covariance, tables, mats, mats_first, packer, halos, copies, group, chunk, kept):
    rows, cols = covariance.shape
    lons = tables.shape[-1]
    side = 2 * lons
    steps_all = cols // (group * lons)
    first, stride, steps = chunk

    def place(g):
        return first + stride * g

    def mats_place(g):
        return place(g) - mats_first

    here = pl.BlockSpec(memory_space=pl.ANY)
    specs = [whole_spec(tables.shape)] + mats_specs(group, mats_place, side) + [whole_spec(packer.shape)]
    specs += window_specs(side, lambda b: b[0], group, place, lons, cols // side)
    args = [blocks, tables, mats, mats, mats, packer] + [covariance] * 3
    specs += [pl.BlockSpec((side, side), lambda g, b: (b[0], 0))] * len(halos)
    args += list(halos)
    outs = [pl.BlockSpec((2 * kept, group * lons), lambda g, *_: (0, g))]
    shapes = [jax.ShapeDtypeStruct((2 * kept, steps * group * lons), F32)]
    scratch = [pltpu.VMEM((side, (group + 2) * lons), F32), pltpu.VMEM((side, group * lons), F32)]
    if copies:
        specs.append(here)
        args.append(covariance)
        outs.append(here)
        shapes.append(jax.ShapeDtypeStruct((side, cols), F32))
        scratch.append(pltpu.VMEM((side, cols), F32))
        scratch += [pltpu.SemaphoreType.DMA((4,))] * 2
    return pl.pallas_call(
        functools.partial(pack_kernel, group, place, steps_all, len(halos), copies),
        grid_spec=pltpu.PrefetchScalarGridSpec(
            num_scalar_prefetch=1, grid=(steps,), in_specs=specs, out_specs=outs, scratch_shapes=scratch,
        ),
        out_shape=shapes,
        compiler_params=params(),
        name="pack_edges",
    )(*args)


def local_call(blocks, covariance, tables, mats, row_mats, rates, signs, halos, chip_rows, chip_halos, before, group,
               offset, steps):
    rows, cols = covariance.shape
    lons = tables.shape[-1]
    side = 2 * lons
    part = largest_part(rows // side, 2) * side

    def place(g):
        return g + offset

    specs = [whole_spec(tables.shape)] + mats_specs(group, place, side)
    specs += [whole_spec(row_mats.shape), whole_spec(rates.shape), whole_spec(signs.shape)]
    specs += window_specs(rows, lambda *_: 0, group, place, lons, cols // side)
    specs += window_specs(side, lambda *_: 0, group, place, lons, cols // side)
    specs += [whole_spec(chip_halos.shape)] + [whole_spec((rows, side))] * len(halos)
    args = [blocks, tables, mats, mats, mats, row_mats, rates, signs, covariance, covariance, covariance]
    args += [chip_rows, chip_rows, chip_rows, chip_halos, *halos]
    aliases = {}
    if before is not None:
        aliases = {len(args): 0}
        specs.append(pl.BlockSpec(memory_space=pl.ANY))
        args.append(before)
    return pl.pallas_call(
        functools.partial(local_kernel, group, offset, cols // (group * lons), len(halos)),
        grid_spec=pltpu.PrefetchScalarGridSpec(
            num_scalar_prefetch=1,
            grid=(steps,),
            in_specs=specs,
            out_specs=pl.BlockSpec((rows, group * lons), lambda g, *_: (0, place(g))),
            scratch_shapes=[
                pltpu.VMEM((part, (group + 2) * lons), F32),
                pltpu.VMEM((rows + 2 * side, group * lons), F32),
                pltpu.VMEM((rows + side, group * lons), F32),
            ],
        ),
        out_shape=jax.ShapeDtypeStruct((rows, cols), F32),
        input_output_aliases=aliases,
        compiler_params=params(),
        name="local_forecast",
    )(*args)


def add_call(blocks, forecast, adder, received, chunk, group):
    side = adder.shape[0]
    width = group * side // 2
    first, stride, steps = chunk
    spot = pl.BlockSpec((side, width), lambda g, b: (b[0], first + stride * g))
    return pl.pallas_call(
        add_kernel,
        grid_spec=pltpu.PrefetchScalarGridSpec(
            num_scalar_prefetch=1,
            grid=(steps,),
            in_specs=[
                whole_spec(adder.shape),
                pl.BlockSpec((received.shape[0], width), lambda g, b: (0, g)),
                spot,
            ],
            out_specs=spot,
        ),
        out_shape=jax.ShapeDtypeStruct(forecast.shape, F32),
        input_output_aliases={3: 0},
        compiler_params=params(),
        name="add_edges",
    )(blocks, adder, received, forecast)


def chunks_of(steps_all):
    if steps_all < 4:
        return [(0, 1, steps_all)]
    inner = steps_all - 2
    start = max(1, inner // 3)
    return [(1, 1, start), (1 + start, 1, inner - start), (0, steps_all - 1, 2)]


def swaps(axis, start):
    count = lax.axis_size(axis)
    pairs = [(i, i + 1) for i in range(start, count - 1, 2)]
    return pairs + [(b, a) for a, b in pairs]


def forecast_with(kept, covariance, blocks, row_part, col_part, first_part, mat_part):
    rows, cols = covariance.shape
    lons = row_part.shape[-1]
    side = 2 * lons
    group = largest_part(cols // lons, 8)
    steps_all = cols // (group * lons)
    chunks = chunks_of(steps_all)
    cross, chip = swaps("row", 1), swaps("row", 0)
    col_swaps = [pairs for pairs in (swaps("col", 0), swaps("col", 1)) if pairs]
    row_mats, rates, signs, packer, adder, *sides = row_tables(blocks, row_part, covariance, kept, len(col_swaps))
    halos = [lax.ppermute(sent, "col", pairs) for sent, pairs in zip(sides, col_swaps)]
    arrived = []

    def pack(chunk, mats, mats_first, halos=(), copies=False):
        return pack_call(blocks, covariance, col_part, mats, mats_first, packer, halos, copies, group, chunk, kept)

    def send(packed):
        arrived.append(lax.ppermute(packed, "row", cross))

    early = len(chunks) > 1
    if early:
        packed, chip_rows = pack(chunks[0], column_tables(first_part, lons), chunks[0][0], copies=True)
        packed, chip_rows, mat_part = lax.optimization_barrier((packed, chip_rows, mat_part))
        send(packed)
    else:
        chip_rows = lax.dynamic_slice_in_dim(covariance, blocks[1] * side, side, 0)
    chip_rows = lax.ppermute(chip_rows, "row", chip)
    mats = column_tables(mat_part, lons)
    for chunk in chunks[early:-1]:
        packed, arrived[0], halos = lax.optimization_barrier((pack(chunk, mats, 0)[0], arrived[0], halos))
        send(packed)
    near = [lax.dynamic_slice_in_dim(halo, blocks[1] * side, side, 0) for halo in halos]
    chip_halos = lax.ppermute(jnp.concatenate(near, axis=1), "row", chip)
    packed, row_mats = lax.optimization_barrier((pack(chunks[-1], mats, 0, halos)[0], row_mats))
    parts = 2 if steps_all >= 4 and steps_all % 2 == 0 else 1
    steps = steps_all // parts
    forecast = None
    for at in range(parts):
        forecast = local_call(
            blocks, covariance, col_part, mats, row_mats, rates, signs, halos, chip_rows, chip_halos, forecast, group,
            at * steps, steps,
        )
        if at == 0:
            packed, forecast = lax.optimization_barrier((packed, forecast))
            send(packed)
    for chunk, received in zip(chunks, arrived):
        forecast = add_call(blocks, forecast, adder, received, chunk, group)
    return forecast


def per_device(covariance, lon_courant, lat_courant, zonal_upwind_sign, lat_sign, cycle_counts):
    rows, cols = covariance.shape
    lons = lon_courant.shape[1]
    row_lats, col_lats = rows // lons, cols // lons
    group = largest_part(col_lats, 8)
    chunk = chunks_of(col_lats // group)[0]
    counts = (row_lats + 4, col_lats + 4, padded(chunk[2] * group + 2, 8), padded(col_lats + 2, 8))
    sources = (lon_courant, lat_courant, zonal_upwind_sign, lat_sign, cycle_counts[None, :])
    *parts, most, blocks = prepare(sources, counts, chunk[0] * group, rows // (2 * lons) - 1)
    sizes = [lons * part // 32 for part in (19, 22, 32)]
    branch = sum((most[0] > size).astype(jnp.int32) for size in sizes[:-1])
    return lax.switch(
        branch, [functools.partial(forecast_with, size) for size in sizes],
        covariance, blocks, *parts,
    )


def solution(mesh):
    placed = (P("row", "col"), P(), P(), P(), P(), P())
    return jax.shard_map(
        per_device, mesh=mesh, in_specs=placed, out_specs=P("row", "col"), check_vma=False
    )
```

```python
import functools

import jax
import jax.numpy as jnp
from jax import lax
from jax.experimental import pallas as pl
from jax.experimental.pallas import tpu as pltpu
from jax.sharding import PartitionSpec as P

SUBCYCLES = 4
F32, BF16 = jnp.float32, jnp.bfloat16
LON_RATE, LAT_RATE, ZONAL, HEADING, COUNTS = range(5)
VMEM_BYTES = 56 * 1024 * 1024
HIGHEST = lax.Precision.HIGHEST


def split(values):
    high = values.astype(BF16)
    return high, (values - high.astype(F32)).astype(BF16)


def dot(left, right):
    return jnp.dot(left, right, preferred_element_type=F32)


def exact_dot(left, right):
    return jnp.dot(left, right, preferred_element_type=F32, precision=HIGHEST)


def blend(center, rate, sign, below, above):
    return center - rate * (center - jnp.where(sign > 0.5, below, above))


def table_row(tables, which, at):
    return tables[which, pl.ds(at, 1), :]


def zonal_bands(rate, sign, count):
    lons = rate.shape[-1]
    zero = jnp.zeros_like(rate)
    bands = {0: jnp.ones_like(rate)}
    for cycle in range(SUBCYCLES):
        cell = jnp.where(count > cycle, rate, 0.0)
        west = {k - 1: pltpu.roll(band, 1, 1) for k, band in bands.items()}
        east = {k + 1: pltpu.roll(band, lons - 1, 1) for k, band in bands.items()}
        bands = {
            k: blend(bands.get(k, zero), cell, sign, west.get(k, zero), east.get(k, zero))
            for k in range(-cycle - 1, cycle + 2)
        }
    return bands


def zonal_matrix(bands, lat):
    lons = bands[0].shape[-1]
    reach = lax.broadcasted_iota(jnp.int32, (lons, lons), 0) - lax.broadcasted_iota(jnp.int32, (lons, lons), 1)
    reach = jnp.where(reach < 0, reach + lons, reach)
    field = jnp.zeros((lons, lons), F32)
    for k, band in bands.items():
        field = jnp.where(reach == k % lons, band[lat:lat + 1, :], field)
    return field


def store_column_mats(bands, out, first, count):
    lons = bands[0].shape[-1]
    for lat in range(count):
        high, low = split(zonal_matrix(bands, lat))
        out[first + lat, :lons, :lons] = high
        out[first + lat, :lons, lons:] = low
        out[first + lat, lons:, :lons] = high
        out[first + lat, lons:, lons:] = jnp.zeros_like(low)


def column_tables_kernel(tables, out):
    bands = zonal_bands(tables[LON_RATE], tables[ZONAL], tables[COUNTS])
    store_column_mats(bands, out, 0, out.shape[0])


def padded(count, least):
    return -(-count // least) * least


def prepare_kernel(first_mat, blocks_last, *refs):
    sources, (row_part, col_part, first_part, mat_part, most, blocks, wide) = refs[:5], refs[5:]
    lats, lons = sources[0].shape
    wide[...] = jnp.zeros_like(wide)
    for which, source in enumerate(sources):
        values = source[...].astype(F32)
        if which == COUNTS:
            values = jnp.broadcast_to(values, (lons, lats)).T
        wide[which, 8:8 + lats, :] = values
    row_lats = row_part.shape[1] - 4
    col_lats = col_part.shape[1] - 4
    row = lax.axis_index("row")
    col_first = lax.axis_index("col") * col_lats
    odd = row % 2
    blocks[0] = odd * blocks_last
    blocks[1] = (1 - odd) * blocks_last
    blocks[2] = lax.axis_index("col") % 2
    for which in range(5):
        for out, first in ((row_part, row * row_lats + 6), (col_part, col_first + 6),
                           (first_part, col_first + first_mat + 7), (mat_part, col_first + 7)):
            out[which] = wide[which, pl.ds(first, out.shape[1]), :]
    heading = (sources[HEADING][...] == 1).astype(F32)
    upward = jnp.sum(heading, axis=1, keepdims=True)
    lat = lax.broadcasted_iota(jnp.int32, (lats, 1), 0)
    place = lat % (2 * row_lats)
    low = (place == 0) & (lat > 0)
    high = (place == 2 * row_lats - 1) & (lat < lats - 1)
    needed = jnp.where(low, upward, jnp.where(high, lons - upward, 0.0))
    most[0] = jnp.max(needed).astype(jnp.int32)


def early_tables_kernel(kept, blocks, tables, col_tables, covariance, col_mats, mats, rates, signs, pack_cross, add_cross,
                        chip_rows, *refs):
    lons = tables.shape[-1]
    side = 2 * lons
    cols = covariance.shape[1]
    *sent, passed, held, done = refs
    from_row = pl.multiple_of(blocks[1] * side, side)
    edges = [jnp.where(blocks[2] == at, cols - side, 0) for at in range(len(sent))]
    places = [(covariance.at[pl.ds(from_row, side), :], passed, chip_rows)]
    for at, edge in enumerate(edges):
        places.append((covariance.at[:, pl.ds(pl.multiple_of(edge, side), side)], held.at[at], sent[at]))
    loads = [pltpu.make_async_copy(source, spot, done.at[0, at]) for at, (source, spot, _) in enumerate(places)]
    stores = [pltpu.make_async_copy(spot, out, done.at[1, at]) for at, (_, spot, out) in enumerate(places)]
    for copy in loads:
        copy.start()

    def one(block, carry):
        first = pl.multiple_of(block * 8, 8)
        rows_here = [col_tables[which, pl.ds(first, 8), :] for which in (LON_RATE, ZONAL, COUNTS)]
        store_column_mats(zonal_bands(*rows_here), col_mats, first, 8)
        return carry

    lax.fori_loop(0, col_mats.shape[0] // 8, one, 0)
    for load, store in zip(loads, stores):
        load.wait()
        store.start()
    lats = mats.shape[0] - 2
    square = (lons, lons)
    down = lax.broadcasted_iota(jnp.int32, square, 0)
    across = lax.broadcasted_iota(jnp.int32, square, 1)

    def spread(which, at):
        return jnp.broadcast_to(table_row(tables, which, at), square).T

    low_mat = high_mat = None
    bands = zonal_bands(tables[LON_RATE], tables[ZONAL], tables[COUNTS])
    for lat in range(lats + 2):
        mat = zonal_matrix(bands, lat + 1).T
        if lat == 1:
            low_mat = mat
        if lat == lats:
            high_mat = mat
        high, low = split(mat)
        mats[lat, :lons, :lons] = high
        mats[lat, :lons, lons:] = high
        mats[lat, lons:, :lons] = low
        mats[lat, lons:, lons:] = jnp.zeros_like(low)
        rates[lat] = spread(LAT_RATE, lat + 1)
        signs[lat] = spread(HEADING, lat + 1)

    def packer(out, size, is_low):
        edge, beyond = (2, 1) if is_low else (lats + 1, lats + 2)
        mat = low_mat if is_low else high_mat
        wanted = not is_low
        rows = padded(2 * size, 16)
        sign = jnp.broadcast_to(table_row(tables, HEADING, beyond), square)
        mask = (sign > 0.5) == wanted
        rank = dot(mask.astype(BF16), (down <= across).astype(BF16))
        rank = jnp.where(mask, rank, 0.0)[:1]
        spot = lax.broadcasted_iota(jnp.int32, (rows, lons), 0)
        first = jnp.where(spot < size, spot, -2).astype(F32) + 1.0
        second = jnp.where((spot >= size) & (spot < 2 * size), spot - size, -2).astype(F32) + 1.0
        moved = exact_dot(jnp.where(rank == first, 1.0, 0.0), mat)
        raw = jnp.where(rank == second, 1.0, 0.0)
        rate = table_row(tables, LAT_RATE, edge)
        toward = (table_row(tables, HEADING, edge) > 0.5) == wanted
        own = moved * (1.0 - rate) + raw
        inner = moved * jnp.where(toward, rate, 0.0)
        high, low = split(jnp.concatenate([own, inner] if is_low else [inner, own], axis=1))
        span = 2 * lons
        extra = padded(size, 16)
        out[:rows, :span] = high
        out[:rows, span:] = high
        out[rows:, :span] = jnp.where(spot_below(size, extra, span), low[:extra].astype(F32), 0.0).astype(BF16)
        out[rows:, span:] = jnp.zeros((extra, span), BF16)

    def spot_below(size, extra, span):
        return lax.broadcasted_iota(jnp.int32, (extra, span), 0) < size

    def adder(out, size, is_low):
        edge, inner = (2, 3) if is_low else (lats + 1, lats)
        mat = low_mat if is_low else high_mat
        columns = padded(2 * size, 16)
        total = 3 * columns

        def wide(which, at):
            tile = spread(which, at)
            return jnp.concatenate([tile] * (-(-total // lons)), axis=1)[:, :total]

        mask = (wide(HEADING, edge) > 0.5) == is_low
        rank = jnp.where(mask, dot((across <= down).astype(BF16), mask.astype(BF16)), 0.0)
        place = lax.broadcasted_iota(jnp.int32, (lons, total), 1)
        spot = jnp.where(place >= columns, place - columns, place)
        spot = jnp.where(spot >= columns, spot - columns, spot)
        first = jnp.where(spot < size, spot, -2).astype(F32) + 1.0
        second = jnp.where((spot >= size) & (spot < 2 * size), spot - size, -2).astype(F32) + 1.0
        partial = jnp.where(rank == first, 1.0, 0.0)
        raw = jnp.where(rank == second, 1.0, 0.0)
        grown = exact_dot(mat * table_row(tables, LAT_RATE, edge), raw)
        rate = wide(LAT_RATE, edge)
        here = (1.0 - rate) * grown + rate * partial
        next_in = jnp.where((wide(HEADING, inner) > 0.5) == is_low, wide(LAT_RATE, inner), 0.0) * grown
        whole = jnp.concatenate([here, next_in] if is_low else [next_in, here], axis=0)
        high = whole.astype(BF16).astype(F32)
        place = lax.broadcasted_iota(jnp.int32, whole.shape, 1)
        middle = (place >= columns) & (place < 2 * columns)
        out[...] = jnp.where(middle, whole - high, high).astype(BF16)

    def sides(cross_low):
        packer(pack_cross, kept, cross_low)
        adder(add_cross, kept, cross_low)

    pl.when(blocks[0] == 0)(lambda: sides(True))
    pl.when(blocks[0] != 0)(lambda: sides(False))
    for copy in stores:
        copy.wait()


def sweep_columns(value, tables, first, mats, held, emit, group):
    lons = tables.shape[-1]

    def rate(k):
        return table_row(tables, LAT_RATE, first + 2 + k)

    def sign(k):
        return table_row(tables, HEADING, first + 2 + k)

    for k in range(-1, group + 1):
        start = blend(value(k), rate(k), sign(k), value(k - 1), value(k + 1))
        both = dot(jnp.concatenate(split(start), axis=1), mats(k + 1))
        held[:, (k + 1) * lons:(k + 2) * lons] = both[:, :lons] + both[:, lons:]
        if k >= 1:
            at = (k - 1) * lons
            below, center, above = (held[:, at + s * lons:at + (s + 1) * lons] for s in range(3))
            emit(k - 1, blend(center, rate(k - 1), sign(k - 1), below, above))


def edge_choice(step, last_step, halos, odd, rows):
    def outside(span, from_pair):
        pair = halos[0][rows, span]
        other = halos[1][rows, span] if len(halos) > 1 else jnp.zeros_like(pair)
        return jnp.where(from_pair, pair, other)

    def take(k, group, lons, low, main, high):
        if k < 0:
            span = slice((k + 2) * lons, (k + 3) * lons)
            inside = low[rows, span]
            return jnp.where(step == 0, outside(span, odd == 1), inside) if halos else inside
        if k < group:
            return main[rows, k * lons:(k + 1) * lons]
        span = slice((k - group) * lons, (k - group + 1) * lons)
        inside = high[rows, span]
        return jnp.where(step == last_step, outside(span, odd == 0), inside) if halos else inside

    return take


def pick_mats(main, first_extra, second_extra, group):
    def mats(at):
        if at < group:
            return main[at]
        return first_extra[0] if at == group else second_extra[0]

    return mats


def pack_kernel(group, place, steps_all, count, blocks, tables, mats, mats_a, mats_b, packer, low, main, high, *refs):
    halos = refs[:count]
    out, held, moved = refs[count:]
    lons = tables.shape[-1]
    step = place(pl.program_id(0))
    choose = edge_choice(step, steps_all - 1, halos, blocks[2], slice(None))

    def emit(k, values):
        moved[:, k * lons:(k + 1) * lons] = values

    sweep_columns(
        lambda k: choose(k, group, lons, low, main, high), tables, step * group,
        pick_mats(mats, mats_a, mats_b, group), held, emit, group,
    )
    sums = dot(packer[...], jnp.concatenate(split(moved[...]), axis=0))
    count = out.shape[0]
    rows = padded(count, 16)
    extra = padded(count // 2, 16)
    out[:extra] = sums[:extra] + sums[rows:]
    out[extra:] = sums[extra:count]


def local_kernel(group, steps_all, count, blocks, tables, mats, mats_a, mats_b, row_mats, rates, signs, low, main, high,
                 chip_low, chip_main, chip_high, chip_halos, *refs):
    halos = refs[:count]
    out, held, moved, stage = refs[-4:]
    lons = tables.shape[-1]
    side = 2 * lons
    step = pl.program_id(0)
    lats = row_mats.shape[0] - 2
    part = held.shape[0]
    weights = pick_mats(mats, mats_a, mats_b, group)
    chip_above = blocks[1] > 0
    top = (lats + 2) * lons

    @pl.when(pl.program_id(0) == 0)
    def _():
        moved[pl.ds(pl.multiple_of(jnp.where(chip_above, 0, top), lons), side), :] = jnp.zeros(
            (side, group * lons), F32
        )

    def sweep(value, held_here, first_row, count):
        def emit(k, values):
            moved[pl.ds(first_row, count), k * lons:(k + 1) * lons] = values

        sweep_columns(value, tables, step * group, weights, held_here, emit, group)

    def one(block, carry):
        first_row = pl.multiple_of(block * part, part)
        choose = edge_choice(step, steps_all - 1, halos, blocks[2], pl.ds(first_row, part))
        sweep(
            lambda k: choose(k, group, lons, low, main, high), held,
            pl.multiple_of(first_row + side, side), part,
        )
        return carry

    lax.fori_loop(0, main.shape[0] // part, one, 0)
    chip_sides = [chip_halos.at[:, at * side:(at + 1) * side] for at in range(count)]
    choose_chip = edge_choice(step, steps_all - 1, chip_sides, blocks[2], slice(None))
    sweep(
        lambda k: choose_chip(k, group, lons, chip_low, chip_main, chip_high), held.at[:side],
        pl.multiple_of(jnp.where(chip_above, top, 0), lons), side,
    )

    def wide(ref, at):
        return jnp.concatenate([ref[at]] * group, axis=1)

    def lat_of(ref, at):
        return ref[at * lons:(at + 1) * lons, :]

    for lat in range(-1, lats + 1):
        near = [lat_of(moved, at) for at in (lat + 1, lat + 2, lat + 3)]
        start = blend(near[1], wide(rates, lat + 1), wide(signs, lat + 1), near[0], near[2])
        both = dot(row_mats[lat + 1], jnp.concatenate(split(start), axis=0))
        stage[(lat + 1) * lons:(lat + 2) * lons, :] = both[:lons] + both[lons:]
        if lat >= 1:
            done = lat - 1
            below, center, above = (lat_of(stage, done + s) for s in range(3))
            out[done * lons:(done + 1) * lons, :] = blend(
                center, wide(rates, done + 1), wide(signs, done + 1), below, above
            )


def add_kernel(blocks, adder, received, before, after):
    columns = adder.shape[1] // 3
    values = received[...]
    if values.shape[0] < columns:
        rest = jnp.zeros((columns - values.shape[0], values.shape[1]), F32)
        values = jnp.concatenate([values, rest], axis=0)
    high, low = split(values)
    after[...] = before[...] + dot(adder[...], jnp.concatenate([high, high, low], axis=0))


def params():
    return pltpu.CompilerParams(vmem_limit_bytes=VMEM_BYTES)


def whole_spec(shape):
    return pl.BlockSpec(shape, lambda *_: (0,) * len(shape))


def mats_specs(group, place, side):
    return [
        pl.BlockSpec((group, side, side), lambda g, *_: (place(g), 0, 0)),
        pl.BlockSpec((1, side, side), lambda g, *_: (place(g) * group + group, 0, 0)),
        pl.BlockSpec((1, side, side), lambda g, *_: (place(g) * group + group + 1, 0, 0)),
    ]


def window_specs(rows, row_block, group, place, lons, col_blocks):
    half = group // 2
    return [
        pl.BlockSpec((rows, 2 * lons), lambda g, *_: (row_block(*_), jnp.maximum(place(g) * half - 1, 0))),
        pl.BlockSpec((rows, group * lons), lambda g, *_: (row_block(*_), place(g))),
        pl.BlockSpec((rows, 2 * lons), lambda g, *_: (row_block(*_), jnp.minimum((place(g) + 1) * half, col_blocks - 1))),
    ]


def largest_part(total, most):
    return max(part for part in range(1, most + 1) if total % part == 0)


def prepare(sources, counts, first_mat, blocks_last):
    lats, lons = sources[0].shape
    shapes = [jax.ShapeDtypeStruct((5, count, lons), F32) for count in counts]
    scalars = [jax.ShapeDtypeStruct((1,), jnp.int32), jax.ShapeDtypeStruct((3,), jnp.int32)]
    return pl.pallas_call(
        functools.partial(prepare_kernel, first_mat, blocks_last),
        in_specs=[whole_spec(t.shape) for t in sources],
        out_specs=[whole_spec(shape.shape) for shape in shapes] + [pl.BlockSpec(memory_space=pltpu.SMEM)] * 2,
        out_shape=shapes + scalars,
        scratch_shapes=[pltpu.VMEM((5, lats + 24, lons), F32)],
        compiler_params=params(),
        name="prepare",
    )(*sources)


def column_tables(tables, lons):
    total = tables.shape[1]
    return pl.pallas_call(
        column_tables_kernel,
        grid=(total // 8,),
        in_specs=[pl.BlockSpec((tables.shape[0], 8, lons), lambda g: (0, g, 0))],
        out_specs=pl.BlockSpec((8, 2 * lons, 2 * lons), lambda g: (g, 0, 0)),
        out_shape=jax.ShapeDtypeStruct((total, 2 * lons, 2 * lons), BF16),
        compiler_params=params(),
        name="column_tables",
    )(tables)


def early_tables(blocks, tables, col_tables, covariance, kept, count):
    rows, cols = covariance.shape
    lons = tables.shape[-1]
    lats = rows // lons
    side = 2 * lons
    shapes = [
        jax.ShapeDtypeStruct((col_tables.shape[1], side, side), BF16),
        jax.ShapeDtypeStruct((lats + 2, side, side), BF16),
        jax.ShapeDtypeStruct((lats + 2, lons, lons), F32),
        jax.ShapeDtypeStruct((lats + 2, lons, lons), F32),
        jax.ShapeDtypeStruct((padded(2 * kept, 16) + padded(kept, 16), 2 * side), BF16),
        jax.ShapeDtypeStruct((side, 3 * padded(2 * kept, 16)), BF16),
    ]
    copied = [jax.ShapeDtypeStruct((side, cols), F32)] + [jax.ShapeDtypeStruct((rows, side), F32)] * count
    here = pl.BlockSpec(memory_space=pl.ANY)
    return pl.pallas_call(
        functools.partial(early_tables_kernel, kept),
        in_specs=[
            pl.BlockSpec(memory_space=pltpu.SMEM), whole_spec(tables.shape), whole_spec(col_tables.shape), here,
        ],
        out_specs=[whole_spec(shape.shape) for shape in shapes] + [here] * len(copied),
        out_shape=shapes + copied,
        scratch_shapes=[
            pltpu.VMEM((side, cols), F32),
            pltpu.VMEM((count, rows, side), F32),
            pltpu.SemaphoreType.DMA((2, count + 1)),
        ],
        compiler_params=params(),
        name="early_tables",
    )(blocks, tables, col_tables, covariance)


def pack_call(blocks, covariance, tables, mats, mats_first, packer, halos, group, chunk, kept):
    rows, cols = covariance.shape
    lons = tables.shape[-1]
    side = 2 * lons
    steps_all = cols // (group * lons)
    first, steps = chunk

    def place(g):
        return lax.rem(first + g, steps_all)

    def mats_place(g):
        return place(g) - mats_first

    specs = [whole_spec(tables.shape)] + mats_specs(group, mats_place, side) + [whole_spec(packer.shape)]
    specs += window_specs(side, lambda b: b[0], group, place, lons, cols // side)
    specs += [pl.BlockSpec((side, side), lambda g, b: (b[0], 0))] * len(halos)
    return pl.pallas_call(
        functools.partial(pack_kernel, group, place, steps_all, len(halos)),
        grid_spec=pltpu.PrefetchScalarGridSpec(
            num_scalar_prefetch=1,
            grid=(steps,),
            in_specs=specs,
            out_specs=pl.BlockSpec((2 * kept, group * lons), lambda g, *_: (0, g)),
            scratch_shapes=[pltpu.VMEM((side, (group + 2) * lons), F32), pltpu.VMEM((side, group * lons), F32)],
        ),
        out_shape=jax.ShapeDtypeStruct((2 * kept, steps * group * lons), F32),
        compiler_params=params(),
        name="pack_edges",
    )(blocks, tables, mats, mats, mats, packer, covariance, covariance, covariance, *halos)


def local_call(blocks, covariance, tables, mats, row_mats, rates, signs, halos, chip_rows, chip_halos, group):
    rows, cols = covariance.shape
    lons = tables.shape[-1]
    side = 2 * lons
    part = largest_part(rows // side, 2) * side

    steps = cols // (group * lons)

    def place(g):
        return g

    specs = [whole_spec(tables.shape)] + mats_specs(group, place, side)
    specs += [whole_spec(row_mats.shape), whole_spec(rates.shape), whole_spec(signs.shape)]
    specs += window_specs(rows, lambda *_: 0, group, place, lons, cols // side)
    specs += window_specs(side, lambda *_: 0, group, place, lons, cols // side)
    specs += [whole_spec(chip_halos.shape)] + [whole_spec((rows, side))] * len(halos)
    args = [blocks, tables, mats, mats, mats, row_mats, rates, signs, covariance, covariance, covariance]
    args += [chip_rows, chip_rows, chip_rows, chip_halos, *halos]
    return pl.pallas_call(
        functools.partial(local_kernel, group, steps, len(halos)),
        grid_spec=pltpu.PrefetchScalarGridSpec(
            num_scalar_prefetch=1,
            grid=(steps,),
            in_specs=specs,
            out_specs=pl.BlockSpec((rows, group * lons), lambda g, *_: (0, place(g))),
            scratch_shapes=[
                pltpu.VMEM((part, (group + 2) * lons), F32),
                pltpu.VMEM((rows + 2 * side, group * lons), F32),
                pltpu.VMEM((rows + side, group * lons), F32),
            ],
        ),
        out_shape=jax.ShapeDtypeStruct((rows, cols), F32),
        compiler_params=params(),
        name="local_forecast",
    )(*args)


def add_call(blocks, forecast, adder, received, chunk, group):
    side = adder.shape[0]
    width = group * side // 2
    first, steps = chunk
    steps_all = forecast.shape[1] // width
    spot = pl.BlockSpec((side, width), lambda g, b: (b[0], lax.rem(first + g, steps_all)))
    return pl.pallas_call(
        add_kernel,
        grid_spec=pltpu.PrefetchScalarGridSpec(
            num_scalar_prefetch=1,
            grid=(steps,),
            in_specs=[
                whole_spec(adder.shape),
                pl.BlockSpec((received.shape[0], width), lambda g, b: (0, g)),
                spot,
            ],
            out_specs=spot,
        ),
        out_shape=jax.ShapeDtypeStruct(forecast.shape, F32),
        input_output_aliases={3: 0},
        compiler_params=params(),
        name="add_edges",
    )(blocks, adder, received, forecast)


def chunks_of(steps_all):
    if steps_all < 4:
        return [(0, steps_all)]
    start = max(1, (steps_all - 2) // 3)
    middle = steps_all - 2 - start
    return [(1, start), (1 + start, middle), (1 + start + middle, steps_all - start - middle)]


def swaps(axis, start):
    count = lax.axis_size(axis)
    pairs = [(i, i + 1) for i in range(start, count - 1, 2)]
    return pairs + [(b, a) for a, b in pairs]


def forecast_with(kept, covariance, blocks, row_part, col_part, first_part, mat_part):
    rows, cols = covariance.shape
    lons = row_part.shape[-1]
    side = 2 * lons
    group = largest_part(cols // lons, 8)
    steps_all = cols // (group * lons)
    chunks = chunks_of(steps_all)
    cross, chip = swaps("row", 1), swaps("row", 0)
    col_swaps = [pairs for pairs in (swaps("col", 0), swaps("col", 1)) if pairs]
    first_mats, row_mats, rates, signs, packer, adder, chip_rows, *sides = early_tables(
        blocks, row_part, first_part, covariance, kept, len(col_swaps)
    )
    halos = [lax.ppermute(sent, "col", pairs) for sent, pairs in zip(sides, col_swaps)]
    arrived = []

    def pack(chunk, mats, mats_first, halos=()):
        return pack_call(blocks, covariance, col_part, mats, mats_first, packer, halos, group, chunk, kept)

    def send(packed):
        arrived.append(lax.ppermute(packed, "row", cross))

    early = len(chunks) > 1
    if early:
        packed = pack(chunks[0], first_mats, chunks[0][0])
        packed, chip_rows, mat_part = lax.optimization_barrier((packed, chip_rows, mat_part))
        send(packed)
    chip_rows = lax.ppermute(chip_rows, "row", chip)
    mats = column_tables(mat_part, lons)
    for chunk in chunks[early:-1]:
        packed, arrived[0], halos = lax.optimization_barrier((pack(chunk, mats, 0), arrived[0], halos))
        send(packed)
    near = [lax.dynamic_slice_in_dim(halo, blocks[1] * side, side, 0) for halo in halos]
    chip_halos = lax.ppermute(jnp.concatenate(near, axis=1), "row", chip)
    packed, row_mats = lax.optimization_barrier((pack(chunks[-1], mats, 0, halos), row_mats))
    send(packed)
    forecast = local_call(
        blocks, covariance, col_part, mats, row_mats, rates, signs, halos, chip_rows, chip_halos, group
    )
    for at in [0, 2, 1] if len(chunks) == 3 else range(len(chunks)):
        forecast = add_call(blocks, forecast, adder, arrived[at], chunks[at], group)
    return forecast


def per_device(covariance, lon_courant, lat_courant, zonal_upwind_sign, lat_sign, cycle_counts):
    rows, cols = covariance.shape
    lons = lon_courant.shape[1]
    row_lats, col_lats = rows // lons, cols // lons
    group = largest_part(col_lats, 8)
    chunk = chunks_of(col_lats // group)[0]
    counts = (row_lats + 4, col_lats + 4, padded(chunk[1] * group + 2, 8), padded(col_lats + 2, 8))
    sources = (lon_courant, lat_courant, zonal_upwind_sign, lat_sign, cycle_counts[None, :])
    *parts, most, blocks = prepare(sources, counts, chunk[0] * group, rows // (2 * lons) - 1)
    sizes = [lons * part // 32 for part in (19, 22, 32)]
    branch = sum((most[0] > size).astype(jnp.int32) for size in sizes[:-1])
    return lax.switch(
        branch, [functools.partial(forecast_with, size) for size in sizes],
        covariance, blocks, *parts,
    )


def solution(mesh):
    placed = (P("row", "col"), P(), P(), P(), P(), P())
    return jax.shard_map(
        per_device, mesh=mesh, in_specs=placed, out_specs=P("row", "col"), check_vma=False
    )
```

```python
import functools

import jax
import jax.numpy as jnp
from jax import lax
from jax.experimental import pallas as pl
from jax.experimental.pallas import tpu as pltpu
from jax.sharding import PartitionSpec as P

SUBCYCLES = 4
F32, BF16 = jnp.float32, jnp.bfloat16
LON_RATE, LAT_RATE, ZONAL, HEADING, COUNTS = range(5)
VMEM_BYTES = 56 * 1024 * 1024
HIGHEST = lax.Precision.HIGHEST


def split(values):
    high = values.astype(BF16)
    return high, (values - high.astype(F32)).astype(BF16)


def dot(left, right):
    return jnp.dot(left, right, preferred_element_type=F32)


def exact_dot(left, right):
    return jnp.dot(left, right, preferred_element_type=F32, precision=HIGHEST)


def blend(center, rate, sign, below, above):
    return center - rate * (center - jnp.where(sign > 0.5, below, above))


def table_row(tables, which, at):
    return tables[which, pl.ds(at, 1), :]


def zonal_bands(rate, sign, count):
    lons = rate.shape[-1]
    zero = jnp.zeros_like(rate)
    bands = {0: jnp.ones_like(rate)}
    for cycle in range(SUBCYCLES):
        cell = jnp.where(count > cycle, rate, 0.0)
        west = {k - 1: pltpu.roll(band, 1, 1) for k, band in bands.items()}
        east = {k + 1: pltpu.roll(band, lons - 1, 1) for k, band in bands.items()}
        bands = {
            k: blend(bands.get(k, zero), cell, sign, west.get(k, zero), east.get(k, zero))
            for k in range(-cycle - 1, cycle + 2)
        }
    return bands


def zonal_matrix(bands, lat):
    lons = bands[0].shape[-1]
    reach = lax.broadcasted_iota(jnp.int32, (lons, lons), 0) - lax.broadcasted_iota(jnp.int32, (lons, lons), 1)
    reach = jnp.where(reach < 0, reach + lons, reach)
    field = jnp.zeros((lons, lons), F32)
    for k, band in bands.items():
        field = jnp.where(reach == k % lons, band[lat:lat + 1, :], field)
    return field


def store_column_mats(bands, out, first, count):
    lons = bands[0].shape[-1]
    for lat in range(count):
        high, low = split(zonal_matrix(bands, lat))
        out[first + lat, :lons, :lons] = high
        out[first + lat, :lons, lons:] = low
        out[first + lat, lons:, :lons] = high
        out[first + lat, lons:, lons:] = jnp.zeros_like(low)


def column_tables_kernel(tables, out):
    bands = zonal_bands(tables[LON_RATE], tables[ZONAL], tables[COUNTS])
    store_column_mats(bands, out, 0, out.shape[0])


def padded(count, least):
    return -(-count // least) * least


def prepare_kernel(first_mat, blocks_last, *refs):
    sources, (row_part, col_part, first_part, mat_part, most, blocks, wide) = refs[:5], refs[5:]
    lats, lons = sources[0].shape
    wide[...] = jnp.zeros_like(wide)
    for which, source in enumerate(sources):
        values = source[...].astype(F32)
        if which == COUNTS:
            values = jnp.broadcast_to(values, (lons, lats)).T
        wide[which, 8:8 + lats, :] = values
    row_lats = row_part.shape[1] - 4
    col_lats = col_part.shape[1] - 4
    row = lax.axis_index("row")
    col_first = lax.axis_index("col") * col_lats
    odd = row % 2
    blocks[0] = odd * blocks_last
    blocks[1] = (1 - odd) * blocks_last
    blocks[2] = lax.axis_index("col") % 2
    for which in range(5):
        for out, first in ((row_part, row * row_lats + 6), (col_part, col_first + 6),
                           (first_part, col_first + first_mat + 7), (mat_part, col_first + 7)):
            out[which] = wide[which, pl.ds(first, out.shape[1]), :]
    heading = (sources[HEADING][...] == 1).astype(F32)
    upward = jnp.sum(heading, axis=1, keepdims=True)
    lat = lax.broadcasted_iota(jnp.int32, (lats, 1), 0)
    place = lat % (2 * row_lats)
    low = (place == 0) & (lat > 0)
    high = (place == 2 * row_lats - 1) & (lat < lats - 1)
    needed = jnp.where(low, upward, jnp.where(high, lons - upward, 0.0))
    most[0] = jnp.max(needed).astype(jnp.int32)


def early_tables_kernel(kept, blocks, tables, col_tables, covariance, col_mats, mats, rates, signs, pack_cross, add_cross,
                        chip_rows, *refs):
    lons = tables.shape[-1]
    side = 2 * lons
    cols = covariance.shape[1]
    *sent, passed, held, done = refs
    from_row = pl.multiple_of(blocks[1] * side, side)
    edges = [jnp.where(blocks[2] == at, cols - side, 0) for at in range(len(sent))]
    places = [(covariance.at[pl.ds(from_row, side), :], passed, chip_rows)]
    for at, edge in enumerate(edges):
        places.append((covariance.at[:, pl.ds(pl.multiple_of(edge, side), side)], held.at[at], sent[at]))
    loads = [pltpu.make_async_copy(source, spot, done.at[0, at]) for at, (source, spot, _) in enumerate(places)]
    stores = [pltpu.make_async_copy(spot, out, done.at[1, at]) for at, (_, spot, out) in enumerate(places)]
    for copy in loads:
        copy.start()

    def one(block, carry):
        first = pl.multiple_of(block * 8, 8)
        rows_here = [col_tables[which, pl.ds(first, 8), :] for which in (LON_RATE, ZONAL, COUNTS)]
        store_column_mats(zonal_bands(*rows_here), col_mats, first, 8)
        return carry

    lax.fori_loop(0, col_mats.shape[0] // 8, one, 0)
    for load, store in zip(loads, stores):
        load.wait()
        store.start()
    lats = mats.shape[0] - 2
    square = (lons, lons)
    down = lax.broadcasted_iota(jnp.int32, square, 0)
    across = lax.broadcasted_iota(jnp.int32, square, 1)

    def spread(which, at):
        return jnp.broadcast_to(table_row(tables, which, at), square).T

    low_mat = high_mat = None
    bands = zonal_bands(tables[LON_RATE], tables[ZONAL], tables[COUNTS])
    for lat in range(lats + 2):
        mat = zonal_matrix(bands, lat + 1).T
        if lat == 1:
            low_mat = mat
        if lat == lats:
            high_mat = mat
        high, low = split(mat)
        mats[lat, :lons, :lons] = high
        mats[lat, :lons, lons:] = high
        mats[lat, lons:, :lons] = low
        mats[lat, lons:, lons:] = jnp.zeros_like(low)
        rates[lat] = spread(LAT_RATE, lat + 1)
        signs[lat] = spread(HEADING, lat + 1)

    def packer(out, size, is_low):
        edge, beyond = (2, 1) if is_low else (lats + 1, lats + 2)
        mat = low_mat if is_low else high_mat
        wanted = not is_low
        rows = padded(2 * size, 16)
        sign = jnp.broadcast_to(table_row(tables, HEADING, beyond), square)
        mask = (sign > 0.5) == wanted
        rank = dot(mask.astype(BF16), (down <= across).astype(BF16))
        rank = jnp.where(mask, rank, 0.0)[:1]
        spot = lax.broadcasted_iota(jnp.int32, (rows, lons), 0)
        first = jnp.where(spot < size, spot, -2).astype(F32) + 1.0
        second = jnp.where((spot >= size) & (spot < 2 * size), spot - size, -2).astype(F32) + 1.0
        moved = exact_dot(jnp.where(rank == first, 1.0, 0.0), mat)
        raw = jnp.where(rank == second, 1.0, 0.0)
        rate = table_row(tables, LAT_RATE, edge)
        toward = (table_row(tables, HEADING, edge) > 0.5) == wanted
        own = moved * (1.0 - rate) + raw
        inner = moved * jnp.where(toward, rate, 0.0)
        high, low = split(jnp.concatenate([own, inner] if is_low else [inner, own], axis=1))
        span = 2 * lons
        extra = padded(size, 16)
        out[:rows, :span] = high
        out[:rows, span:] = high
        out[rows:, :span] = jnp.where(spot_below(size, extra, span), low[:extra].astype(F32), 0.0).astype(BF16)
        out[rows:, span:] = jnp.zeros((extra, span), BF16)

    def spot_below(size, extra, span):
        return lax.broadcasted_iota(jnp.int32, (extra, span), 0) < size

    def adder(out, size, is_low):
        edge, inner = (2, 3) if is_low else (lats + 1, lats)
        mat = low_mat if is_low else high_mat
        columns = padded(2 * size, 16)
        total = 3 * columns

        def wide(which, at):
            tile = spread(which, at)
            return jnp.concatenate([tile] * (-(-total // lons)), axis=1)[:, :total]

        mask = (wide(HEADING, edge) > 0.5) == is_low
        rank = jnp.where(mask, dot((across <= down).astype(BF16), mask.astype(BF16)), 0.0)
        place = lax.broadcasted_iota(jnp.int32, (lons, total), 1)
        spot = jnp.where(place >= columns, place - columns, place)
        spot = jnp.where(spot >= columns, spot - columns, spot)
        first = jnp.where(spot < size, spot, -2).astype(F32) + 1.0
        second = jnp.where((spot >= size) & (spot < 2 * size), spot - size, -2).astype(F32) + 1.0
        partial = jnp.where(rank == first, 1.0, 0.0)
        raw = jnp.where(rank == second, 1.0, 0.0)
        grown = exact_dot(mat * table_row(tables, LAT_RATE, edge), raw)
        rate = wide(LAT_RATE, edge)
        here = (1.0 - rate) * grown + rate * partial
        next_in = jnp.where((wide(HEADING, inner) > 0.5) == is_low, wide(LAT_RATE, inner), 0.0) * grown
        whole = jnp.concatenate([here, next_in] if is_low else [next_in, here], axis=0)
        high = whole.astype(BF16).astype(F32)
        place = lax.broadcasted_iota(jnp.int32, whole.shape, 1)
        middle = (place >= columns) & (place < 2 * columns)
        out[...] = jnp.where(middle, whole - high, high).astype(BF16)

    def sides(cross_low):
        packer(pack_cross, kept, cross_low)
        adder(add_cross, kept, cross_low)

    pl.when(blocks[0] == 0)(lambda: sides(True))
    pl.when(blocks[0] != 0)(lambda: sides(False))
    for copy in stores:
        copy.wait()


def sweep_columns(value, tables, first, mats, held, emit, group):
    lons = tables.shape[-1]

    def rate(k):
        return table_row(tables, LAT_RATE, first + 2 + k)

    def sign(k):
        return table_row(tables, HEADING, first + 2 + k)

    for k in range(-1, group + 1):
        start = blend(value(k), rate(k), sign(k), value(k - 1), value(k + 1))
        both = dot(jnp.concatenate(split(start), axis=1), mats(k + 1))
        held[:, (k + 1) * lons:(k + 2) * lons] = both[:, :lons] + both[:, lons:]
        if k >= 1:
            at = (k - 1) * lons
            below, center, above = (held[:, at + s * lons:at + (s + 1) * lons] for s in range(3))
            emit(k - 1, blend(center, rate(k - 1), sign(k - 1), below, above))


def edge_choice(step, last_step, halos, odd, rows):
    def outside(span, from_pair):
        pair = halos[0][rows, span]
        other = halos[1][rows, span] if len(halos) > 1 else jnp.zeros_like(pair)
        return jnp.where(from_pair, pair, other)

    def take(k, group, lons, low, main, high):
        if k < 0:
            span = slice((k + 2) * lons, (k + 3) * lons)
            inside = low[rows, span]
            return jnp.where(step == 0, outside(span, odd == 1), inside) if halos else inside
        if k < group:
            return main[rows, k * lons:(k + 1) * lons]
        span = slice((k - group) * lons, (k - group + 1) * lons)
        inside = high[rows, span]
        return jnp.where(step == last_step, outside(span, odd == 0), inside) if halos else inside

    return take


def pick_mats(main, first_extra, second_extra, group):
    def mats(at):
        if at < group:
            return main[at]
        return first_extra[0] if at == group else second_extra[0]

    return mats


def pack_kernel(group, place, steps_all, count, blocks, tables, mats, mats_a, mats_b, packer, low, main, high, *refs):
    halos = refs[:count]
    out, held, moved = refs[count:]
    lons = tables.shape[-1]
    step = place(pl.program_id(0))
    choose = edge_choice(step, steps_all - 1, halos, blocks[2], slice(None))

    def emit(k, values):
        moved[:, k * lons:(k + 1) * lons] = values

    sweep_columns(
        lambda k: choose(k, group, lons, low, main, high), tables, step * group,
        pick_mats(mats, mats_a, mats_b, group), held, emit, group,
    )
    sums = dot(packer[...], jnp.concatenate(split(moved[...]), axis=0))
    count = out.shape[0]
    rows = padded(count, 16)
    extra = padded(count // 2, 16)
    out[:extra] = sums[:extra] + sums[rows:]
    out[extra:] = sums[extra:count]


def local_kernel(group, steps_all, count, blocks, tables, mats, mats_a, mats_b, row_mats, rates, signs, low, main, high,
                 chip_low, chip_main, chip_high, chip_halos, *refs):
    halos = refs[:count]
    out, held, moved, stage = refs[-4:]
    lons = tables.shape[-1]
    side = 2 * lons
    step = pl.program_id(0)
    lats = row_mats.shape[0] - 2
    part = held.shape[0]
    weights = pick_mats(mats, mats_a, mats_b, group)
    chip_above = blocks[1] > 0
    top = (lats + 2) * lons

    @pl.when(pl.program_id(0) == 0)
    def _():
        moved[pl.ds(pl.multiple_of(jnp.where(chip_above, 0, top), lons), side), :] = jnp.zeros(
            (side, group * lons), F32
        )

    def sweep(value, held_here, first_row, count):
        def emit(k, values):
            moved[pl.ds(first_row, count), k * lons:(k + 1) * lons] = values

        sweep_columns(value, tables, step * group, weights, held_here, emit, group)

    def one(block, carry):
        first_row = pl.multiple_of(block * part, part)
        choose = edge_choice(step, steps_all - 1, halos, blocks[2], pl.ds(first_row, part))
        sweep(
            lambda k: choose(k, group, lons, low, main, high), held,
            pl.multiple_of(first_row + side, side), part,
        )
        return carry

    lax.fori_loop(0, main.shape[0] // part, one, 0)
    chip_sides = [chip_halos.at[:, at * side:(at + 1) * side] for at in range(count)]
    choose_chip = edge_choice(step, steps_all - 1, chip_sides, blocks[2], slice(None))
    sweep(
        lambda k: choose_chip(k, group, lons, chip_low, chip_main, chip_high), held.at[:side],
        pl.multiple_of(jnp.where(chip_above, top, 0), lons), side,
    )

    def wide(ref, at):
        return jnp.concatenate([ref[at]] * group, axis=1)

    def lat_of(ref, at):
        return ref[at * lons:(at + 1) * lons, :]

    for lat in range(-1, lats + 1):
        near = [lat_of(moved, at) for at in (lat + 1, lat + 2, lat + 3)]
        start = blend(near[1], wide(rates, lat + 1), wide(signs, lat + 1), near[0], near[2])
        both = dot(row_mats[lat + 1], jnp.concatenate(split(start), axis=0))
        stage[(lat + 1) * lons:(lat + 2) * lons, :] = both[:lons] + both[lons:]
        if lat >= 1:
            done = lat - 1
            below, center, above = (lat_of(stage, done + s) for s in range(3))
            out[done * lons:(done + 1) * lons, :] = blend(
                center, wide(rates, done + 1), wide(signs, done + 1), below, above
            )


def add_kernel(blocks, adder, received, before, after):
    columns = adder.shape[1] // 3
    values = received[...]
    if values.shape[0] < columns:
        rest = jnp.zeros((columns - values.shape[0], values.shape[1]), F32)
        values = jnp.concatenate([values, rest], axis=0)
    high, low = split(values)
    after[...] = before[...] + dot(adder[...], jnp.concatenate([high, high, low], axis=0))


def params():
    return pltpu.CompilerParams(vmem_limit_bytes=VMEM_BYTES)


def whole_spec(shape):
    return pl.BlockSpec(shape, lambda *_: (0,) * len(shape))


def mats_specs(group, place, side):
    return [
        pl.BlockSpec((group, side, side), lambda g, *_: (place(g), 0, 0)),
        pl.BlockSpec((1, side, side), lambda g, *_: (place(g) * group + group, 0, 0)),
        pl.BlockSpec((1, side, side), lambda g, *_: (place(g) * group + group + 1, 0, 0)),
    ]


def window_specs(rows, row_block, group, place, lons, col_blocks):
    half = group // 2
    return [
        pl.BlockSpec((rows, 2 * lons), lambda g, *_: (row_block(*_), jnp.maximum(place(g) * half - 1, 0))),
        pl.BlockSpec((rows, group * lons), lambda g, *_: (row_block(*_), place(g))),
        pl.BlockSpec((rows, 2 * lons), lambda g, *_: (row_block(*_), jnp.minimum((place(g) + 1) * half, col_blocks - 1))),
    ]


def largest_part(total, most):
    return max(part for part in range(1, most + 1) if total % part == 0)


def prepare(sources, counts, first_mat, blocks_last):
    lats, lons = sources[0].shape
    shapes = [jax.ShapeDtypeStruct((5, count, lons), F32) for count in counts]
    scalars = [jax.ShapeDtypeStruct((1,), jnp.int32), jax.ShapeDtypeStruct((3,), jnp.int32)]
    return pl.pallas_call(
        functools.partial(prepare_kernel, first_mat, blocks_last),
        in_specs=[whole_spec(t.shape) for t in sources],
        out_specs=[whole_spec(shape.shape) for shape in shapes] + [pl.BlockSpec(memory_space=pltpu.SMEM)] * 2,
        out_shape=shapes + scalars,
        scratch_shapes=[pltpu.VMEM((5, lats + 24, lons), F32)],
        compiler_params=params(),
        name="prepare",
    )(*sources)


def column_tables(tables, lons):
    total = tables.shape[1]
    return pl.pallas_call(
        column_tables_kernel,
        grid=(total // 8,),
        in_specs=[pl.BlockSpec((tables.shape[0], 8, lons), lambda g: (0, g, 0))],
        out_specs=pl.BlockSpec((8, 2 * lons, 2 * lons), lambda g: (g, 0, 0)),
        out_shape=jax.ShapeDtypeStruct((total, 2 * lons, 2 * lons), BF16),
        compiler_params=params(),
        name="column_tables",
    )(tables)


def early_tables(blocks, tables, col_tables, covariance, kept, count):
    rows, cols = covariance.shape
    lons = tables.shape[-1]
    lats = rows // lons
    side = 2 * lons
    shapes = [
        jax.ShapeDtypeStruct((col_tables.shape[1], side, side), BF16),
        jax.ShapeDtypeStruct((lats + 2, side, side), BF16),
        jax.ShapeDtypeStruct((lats + 2, lons, lons), F32),
        jax.ShapeDtypeStruct((lats + 2, lons, lons), F32),
        jax.ShapeDtypeStruct((padded(2 * kept, 16) + padded(kept, 16), 2 * side), BF16),
        jax.ShapeDtypeStruct((side, 3 * padded(2 * kept, 16)), BF16),
    ]
    copied = [jax.ShapeDtypeStruct((side, cols), F32)] + [jax.ShapeDtypeStruct((rows, side), F32)] * count
    here = pl.BlockSpec(memory_space=pl.ANY)
    return pl.pallas_call(
        functools.partial(early_tables_kernel, kept),
        in_specs=[
            pl.BlockSpec(memory_space=pltpu.SMEM), whole_spec(tables.shape), whole_spec(col_tables.shape), here,
        ],
        out_specs=[whole_spec(shape.shape) for shape in shapes] + [here] * len(copied),
        out_shape=shapes + copied,
        scratch_shapes=[
            pltpu.VMEM((side, cols), F32),
            pltpu.VMEM((count, rows, side), F32),
            pltpu.SemaphoreType.DMA((2, count + 1)),
        ],
        compiler_params=params(),
        name="early_tables",
    )(blocks, tables, col_tables, covariance)


def pack_call(blocks, covariance, tables, mats, mats_first, packer, halos, group, chunk, kept):
    rows, cols = covariance.shape
    lons = tables.shape[-1]
    side = 2 * lons
    steps_all = cols // (group * lons)
    first, steps = chunk

    def place(g):
        return lax.rem(first + g, steps_all)

    def mats_place(g):
        return place(g) - mats_first

    specs = [whole_spec(tables.shape)] + mats_specs(group, mats_place, side) + [whole_spec(packer.shape)]
    specs += window_specs(side, lambda b: b[0], group, place, lons, cols // side)
    specs += [pl.BlockSpec((side, side), lambda g, b: (b[0], 0))] * len(halos)
    return pl.pallas_call(
        functools.partial(pack_kernel, group, place, steps_all, len(halos)),
        grid_spec=pltpu.PrefetchScalarGridSpec(
            num_scalar_prefetch=1,
            grid=(steps,),
            in_specs=specs,
            out_specs=pl.BlockSpec((2 * kept, group * lons), lambda g, *_: (0, g)),
            scratch_shapes=[pltpu.VMEM((side, (group + 2) * lons), F32), pltpu.VMEM((side, group * lons), F32)],
        ),
        out_shape=jax.ShapeDtypeStruct((2 * kept, steps * group * lons), F32),
        compiler_params=params(),
        name="pack_edges",
    )(blocks, tables, mats, mats, mats, packer, covariance, covariance, covariance, *halos)


def local_call(blocks, covariance, tables, mats, row_mats, rates, signs, halos, chip_rows, chip_halos, group):
    rows, cols = covariance.shape
    lons = tables.shape[-1]
    side = 2 * lons
    part = largest_part(rows // side, 2) * side

    steps = cols // (group * lons)

    def place(g):
        return g

    specs = [whole_spec(tables.shape)] + mats_specs(group, place, side)
    specs += [whole_spec(row_mats.shape), whole_spec(rates.shape), whole_spec(signs.shape)]
    specs += window_specs(rows, lambda *_: 0, group, place, lons, cols // side)
    specs += window_specs(side, lambda *_: 0, group, place, lons, cols // side)
    specs += [whole_spec(chip_halos.shape)] + [whole_spec((rows, side))] * len(halos)
    args = [blocks, tables, mats, mats, mats, row_mats, rates, signs, covariance, covariance, covariance]
    args += [chip_rows, chip_rows, chip_rows, chip_halos, *halos]
    return pl.pallas_call(
        functools.partial(local_kernel, group, steps, len(halos)),
        grid_spec=pltpu.PrefetchScalarGridSpec(
            num_scalar_prefetch=1,
            grid=(steps,),
            in_specs=specs,
            out_specs=pl.BlockSpec((rows, group * lons), lambda g, *_: (0, place(g))),
            scratch_shapes=[
                pltpu.VMEM((part, (group + 2) * lons), F32),
                pltpu.VMEM((rows + 2 * side, group * lons), F32),
                pltpu.VMEM((rows + side, group * lons), F32),
            ],
        ),
        out_shape=jax.ShapeDtypeStruct((rows, cols), F32),
        compiler_params=params(),
        name="local_forecast",
    )(*args)


def add_call(blocks, forecast, adder, received, chunk, group):
    side = adder.shape[0]
    width = group * side // 2
    first, steps = chunk
    steps_all = forecast.shape[1] // width
    spot = pl.BlockSpec((side, width), lambda g, b: (b[0], lax.rem(first + g, steps_all)))
    return pl.pallas_call(
        add_kernel,
        grid_spec=pltpu.PrefetchScalarGridSpec(
            num_scalar_prefetch=1,
            grid=(steps,),
            in_specs=[
                whole_spec(adder.shape),
                pl.BlockSpec((received.shape[0], width), lambda g, b: (0, g)),
                spot,
            ],
            out_specs=spot,
        ),
        out_shape=jax.ShapeDtypeStruct(forecast.shape, F32),
        input_output_aliases={3: 0},
        compiler_params=params(),
        name="add_edges",
    )(blocks, adder, received, forecast)


def chunks_of(steps_all):
    if steps_all < 4:
        return [(0, steps_all)]
    start = max(1, (steps_all - 2) // 3)
    middle = steps_all - 2 - start
    return [(1, start), (1 + start, middle), (1 + start + middle, steps_all - start - middle)]


def swaps(axis, start):
    count = lax.axis_size(axis)
    pairs = [(i, i + 1) for i in range(start, count - 1, 2)]
    return pairs + [(b, a) for a, b in pairs]


def forecast_with(kept, covariance, blocks, row_part, col_part, first_part, mat_part):
    rows, cols = covariance.shape
    lons = row_part.shape[-1]
    side = 2 * lons
    group = largest_part(cols // lons, 8)
    steps_all = cols // (group * lons)
    chunks = chunks_of(steps_all)
    cross, chip = swaps("row", 1), swaps("row", 0)
    col_swaps = [pairs for pairs in (swaps("col", 0), swaps("col", 1)) if pairs]
    first_mats, row_mats, rates, signs, packer, adder, chip_rows, *sides = early_tables(
        blocks, row_part, first_part, covariance, kept, len(col_swaps)
    )
    halos = [lax.ppermute(sent, "col", pairs) for sent, pairs in zip(sides, col_swaps)]
    arrived = []

    def pack(chunk, mats, mats_first, halos=()):
        return pack_call(blocks, covariance, col_part, mats, mats_first, packer, halos, group, chunk, kept)

    def send(packed):
        arrived.append(lax.ppermute(packed, "row", cross))

    early = len(chunks) > 1
    if early:
        packed = pack(chunks[0], first_mats, chunks[0][0])
        packed, chip_rows, mat_part = lax.optimization_barrier((packed, chip_rows, mat_part))
        send(packed)
    chip_rows = lax.ppermute(chip_rows, "row", chip)
    mats = column_tables(mat_part, lons)
    for chunk in chunks[early:-1]:
        packed, arrived[0], halos = lax.optimization_barrier((pack(chunk, mats, 0), arrived[0], halos))
        send(packed)
    near = [lax.dynamic_slice_in_dim(halo, blocks[1] * side, side, 0) for halo in halos]
    chip_halos = lax.ppermute(jnp.concatenate(near, axis=1), "row", chip)
    packed, row_mats = lax.optimization_barrier((pack(chunks[-1], mats, 0, halos), row_mats))
    send(packed)
    forecast = local_call(
        blocks, covariance, col_part, mats, row_mats, rates, signs, halos, chip_rows, chip_halos, group
    )
    for chunk, received in zip(chunks, arrived):
        forecast = add_call(blocks, forecast, adder, received, chunk, group)
    return forecast


def per_device(covariance, lon_courant, lat_courant, zonal_upwind_sign, lat_sign, cycle_counts):
    rows, cols = covariance.shape
    lons = lon_courant.shape[1]
    row_lats, col_lats = rows // lons, cols // lons
    group = largest_part(col_lats, 8)
    chunk = chunks_of(col_lats // group)[0]
    counts = (row_lats + 4, col_lats + 4, padded(chunk[1] * group + 2, 8), padded(col_lats + 2, 8))
    sources = (lon_courant, lat_courant, zonal_upwind_sign, lat_sign, cycle_counts[None, :])
    *parts, most, blocks = prepare(sources, counts, chunk[0] * group, rows // (2 * lons) - 1)
    sizes = [lons * part // 32 for part in (19, 22, 32)]
    branch = sum((most[0] > size).astype(jnp.int32) for size in sizes[:-1])
    return lax.switch(
        branch, [functools.partial(forecast_with, size) for size in sizes],
        covariance, blocks, *parts,
    )


def solution(mesh):
    placed = (P("row", "col"), P(), P(), P(), P(), P())
    return jax.shard_map(
        per_device, mesh=mesh, in_specs=placed, out_specs=P("row", "col"), check_vma=False
    )
```

```python
import functools

import jax
import jax.numpy as jnp
from jax import lax
from jax.experimental import pallas as pl
from jax.experimental.pallas import tpu as pltpu
from jax.sharding import PartitionSpec as P

SUBCYCLES = 4
F32, BF16 = jnp.float32, jnp.bfloat16
LON_RATE, LAT_RATE, ZONAL, HEADING, COUNTS = range(5)
VMEM_BYTES = 56 * 1024 * 1024
HIGHEST = lax.Precision.HIGHEST


def split(values):
    high = values.astype(BF16)
    return high, (values - high.astype(F32)).astype(BF16)


def dot(left, right):
    return jnp.dot(left, right, preferred_element_type=F32)


def exact_dot(left, right):
    return jnp.dot(left, right, preferred_element_type=F32, precision=HIGHEST)


def blend(center, rate, sign, below, above):
    return center - rate * (center - jnp.where(sign > 0.5, below, above))


def table_row(tables, which, at):
    return tables[which, pl.ds(at, 1), :]


def zonal_bands(rate, sign, count):
    lons = rate.shape[-1]
    zero = jnp.zeros_like(rate)
    bands = {0: jnp.ones_like(rate)}
    for cycle in range(SUBCYCLES):
        cell = jnp.where(count > cycle, rate, 0.0)
        west = {k - 1: pltpu.roll(band, 1, 1) for k, band in bands.items()}
        east = {k + 1: pltpu.roll(band, lons - 1, 1) for k, band in bands.items()}
        bands = {
            k: blend(bands.get(k, zero), cell, sign, west.get(k, zero), east.get(k, zero))
            for k in range(-cycle - 1, cycle + 2)
        }
    return bands


def zonal_matrix(bands, lat):
    lons = bands[0].shape[-1]
    reach = lax.broadcasted_iota(jnp.int32, (lons, lons), 0) - lax.broadcasted_iota(jnp.int32, (lons, lons), 1)
    reach = jnp.where(reach < 0, reach + lons, reach)
    field = jnp.zeros((lons, lons), F32)
    for k, band in bands.items():
        field = jnp.where(reach == k % lons, band[lat:lat + 1, :], field)
    return field


def store_column_mats(bands, out, first, count):
    lons = bands[0].shape[-1]
    for lat in range(count):
        high, low = split(zonal_matrix(bands, lat))
        out[first + lat, :lons, :lons] = high
        out[first + lat, :lons, lons:] = low
        out[first + lat, lons:, :lons] = high
        out[first + lat, lons:, lons:] = jnp.zeros_like(low)


def column_tables_kernel(tables, out):
    bands = zonal_bands(tables[LON_RATE], tables[ZONAL], tables[COUNTS])
    store_column_mats(bands, out, 0, out.shape[0])


def padded(count, least):
    return -(-count // least) * least


def prepare_kernel(first_mat, blocks_last, *refs):
    sources, (row_part, col_part, first_part, mat_part, most, blocks, wide) = refs[:5], refs[5:]
    lats, lons = sources[0].shape
    wide[...] = jnp.zeros_like(wide)
    for which, source in enumerate(sources):
        values = source[...].astype(F32)
        if which == COUNTS:
            values = jnp.broadcast_to(values, (lons, lats)).T
        wide[which, 8:8 + lats, :] = values
    row_lats = row_part.shape[1] - 4
    col_lats = col_part.shape[1] - 4
    row = lax.axis_index("row")
    col_first = lax.axis_index("col") * col_lats
    odd = row % 2
    blocks[0] = odd * blocks_last
    blocks[1] = (1 - odd) * blocks_last
    blocks[2] = lax.axis_index("col") % 2
    for which in range(5):
        for out, first in ((row_part, row * row_lats + 6), (col_part, col_first + 6),
                           (first_part, col_first + first_mat + 7), (mat_part, col_first + 7)):
            out[which] = wide[which, pl.ds(first, out.shape[1]), :]
    heading = (sources[HEADING][...] == 1).astype(F32)
    upward = jnp.sum(heading, axis=1, keepdims=True)
    lat = lax.broadcasted_iota(jnp.int32, (lats, 1), 0)
    place = lat % (2 * row_lats)
    low = (place == 0) & (lat > 0)
    high = (place == 2 * row_lats - 1) & (lat < lats - 1)
    needed = jnp.where(low, upward, jnp.where(high, lons - upward, 0.0))
    most[0] = jnp.max(needed).astype(jnp.int32)


def early_tables_kernel(kept, blocks, tables, col_tables, covariance, col_mats, mats, rates, signs, pack_cross, add_cross,
                        chip_rows, *refs):
    lons = tables.shape[-1]
    side = 2 * lons
    cols = covariance.shape[1]
    *sent, passed, held, done = refs
    from_row = pl.multiple_of(blocks[1] * side, side)
    edges = [jnp.where(blocks[2] == at, cols - side, 0) for at in range(len(sent))]
    places = [(covariance.at[pl.ds(from_row, side), :], passed, chip_rows)]
    for at, edge in enumerate(edges):
        places.append((covariance.at[:, pl.ds(pl.multiple_of(edge, side), side)], held.at[at], sent[at]))
    loads = [pltpu.make_async_copy(source, spot, done.at[0, at]) for at, (source, spot, _) in enumerate(places)]
    stores = [pltpu.make_async_copy(spot, out, done.at[1, at]) for at, (_, spot, out) in enumerate(places)]
    for copy in loads:
        copy.start()

    def one(block, carry):
        first = pl.multiple_of(block * 8, 8)
        rows_here = [col_tables[which, pl.ds(first, 8), :] for which in (LON_RATE, ZONAL, COUNTS)]
        store_column_mats(zonal_bands(*rows_here), col_mats, first, 8)
        return carry

    lax.fori_loop(0, col_mats.shape[0] // 8, one, 0)
    for load, store in zip(loads, stores):
        load.wait()
        store.start()
    lats = mats.shape[0] - 2
    square = (lons, lons)
    down = lax.broadcasted_iota(jnp.int32, square, 0)
    across = lax.broadcasted_iota(jnp.int32, square, 1)

    def spread(which, at):
        return jnp.broadcast_to(table_row(tables, which, at), square).T

    low_mat = high_mat = None
    bands = zonal_bands(tables[LON_RATE], tables[ZONAL], tables[COUNTS])
    for lat in range(lats + 2):
        mat = zonal_matrix(bands, lat + 1).T
        if lat == 1:
            low_mat = mat
        if lat == lats:
            high_mat = mat
        high, low = split(mat)
        mats[lat, :lons, :lons] = high
        mats[lat, :lons, lons:] = high
        mats[lat, lons:, :lons] = low
        mats[lat, lons:, lons:] = jnp.zeros_like(low)
        rates[lat] = spread(LAT_RATE, lat + 1)
        signs[lat] = spread(HEADING, lat + 1)

    def packer(out, size, is_low):
        edge, beyond = (2, 1) if is_low else (lats + 1, lats + 2)
        mat = low_mat if is_low else high_mat
        wanted = not is_low
        rows = padded(2 * size, 16)
        sign = jnp.broadcast_to(table_row(tables, HEADING, beyond), square)
        mask = (sign > 0.5) == wanted
        rank = dot(mask.astype(BF16), (down <= across).astype(BF16))
        rank = jnp.where(mask, rank, 0.0)[:1]
        spot = lax.broadcasted_iota(jnp.int32, (rows, lons), 0)
        first = jnp.where(spot < size, spot, -2).astype(F32) + 1.0
        second = jnp.where((spot >= size) & (spot < 2 * size), spot - size, -2).astype(F32) + 1.0
        moved = exact_dot(jnp.where(rank == first, 1.0, 0.0), mat)
        raw = jnp.where(rank == second, 1.0, 0.0)
        rate = table_row(tables, LAT_RATE, edge)
        toward = (table_row(tables, HEADING, edge) > 0.5) == wanted
        own = moved * (1.0 - rate) + raw
        inner = moved * jnp.where(toward, rate, 0.0)
        high, low = split(jnp.concatenate([own, inner] if is_low else [inner, own], axis=1))
        span = 2 * lons
        extra = padded(size, 16)
        out[:rows, :span] = high
        out[:rows, span:] = high
        out[rows:, :span] = jnp.where(spot_below(size, extra, span), low[:extra].astype(F32), 0.0).astype(BF16)
        out[rows:, span:] = jnp.zeros((extra, span), BF16)

    def spot_below(size, extra, span):
        return lax.broadcasted_iota(jnp.int32, (extra, span), 0) < size

    def adder(out, size, is_low):
        edge, inner = (2, 3) if is_low else (lats + 1, lats)
        mat = low_mat if is_low else high_mat
        columns = padded(2 * size, 16)
        total = 3 * columns

        def wide(which, at):
            tile = spread(which, at)
            return jnp.concatenate([tile] * (-(-total // lons)), axis=1)[:, :total]

        mask = (wide(HEADING, edge) > 0.5) == is_low
        rank = jnp.where(mask, dot((across <= down).astype(BF16), mask.astype(BF16)), 0.0)
        place = lax.broadcasted_iota(jnp.int32, (lons, total), 1)
        spot = jnp.where(place >= columns, place - columns, place)
        spot = jnp.where(spot >= columns, spot - columns, spot)
        first = jnp.where(spot < size, spot, -2).astype(F32) + 1.0
        second = jnp.where((spot >= size) & (spot < 2 * size), spot - size, -2).astype(F32) + 1.0
        partial = jnp.where(rank == first, 1.0, 0.0)
        raw = jnp.where(rank == second, 1.0, 0.0)
        grown = exact_dot(mat * table_row(tables, LAT_RATE, edge), raw)
        rate = wide(LAT_RATE, edge)
        here = (1.0 - rate) * grown + rate * partial
        next_in = jnp.where((wide(HEADING, inner) > 0.5) == is_low, wide(LAT_RATE, inner), 0.0) * grown
        whole = jnp.concatenate([here, next_in] if is_low else [next_in, here], axis=0)
        high = whole.astype(BF16).astype(F32)
        place = lax.broadcasted_iota(jnp.int32, whole.shape, 1)
        middle = (place >= columns) & (place < 2 * columns)
        out[...] = jnp.where(middle, whole - high, high).astype(BF16)

    def sides(cross_low):
        packer(pack_cross, kept, cross_low)
        adder(add_cross, kept, cross_low)

    pl.when(blocks[0] == 0)(lambda: sides(True))
    pl.when(blocks[0] != 0)(lambda: sides(False))
    for copy in stores:
        copy.wait()


def sweep_columns(value, tables, first, mats, held, emit, group):
    lons = tables.shape[-1]

    def rate(k):
        return table_row(tables, LAT_RATE, first + 2 + k)

    def sign(k):
        return table_row(tables, HEADING, first + 2 + k)

    for k in range(-1, group + 1):
        start = blend(value(k), rate(k), sign(k), value(k - 1), value(k + 1))
        both = dot(jnp.concatenate(split(start), axis=1), mats(k + 1))
        held[:, (k + 1) * lons:(k + 2) * lons] = both[:, :lons] + both[:, lons:]
        if k >= 1:
            at = (k - 1) * lons
            below, center, above = (held[:, at + s * lons:at + (s + 1) * lons] for s in range(3))
            emit(k - 1, blend(center, rate(k - 1), sign(k - 1), below, above))


def edge_choice(step, last_step, halos, odd, rows):
    def outside(span, from_pair):
        pair = halos[0][rows, span]
        other = halos[1][rows, span] if len(halos) > 1 else jnp.zeros_like(pair)
        return jnp.where(from_pair, pair, other)

    def take(k, group, lons, low, main, high):
        if k < 0:
            span = slice((k + 2) * lons, (k + 3) * lons)
            inside = low[rows, span]
            return jnp.where(step == 0, outside(span, odd == 1), inside) if halos else inside
        if k < group:
            return main[rows, k * lons:(k + 1) * lons]
        span = slice((k - group) * lons, (k - group + 1) * lons)
        inside = high[rows, span]
        return jnp.where(step == last_step, outside(span, odd == 0), inside) if halos else inside

    return take


def pick_mats(main, first_extra, second_extra, group):
    def mats(at):
        if at < group:
            return main[at]
        return first_extra[0] if at == group else second_extra[0]

    return mats


def pack_kernel(group, place, steps_all, count, blocks, tables, mats, mats_a, mats_b, packer, low, main, high, *refs):
    halos = refs[:count]
    out, held, moved = refs[count:]
    lons = tables.shape[-1]
    step = place(pl.program_id(0))
    choose = edge_choice(step, steps_all - 1, halos, blocks[2], slice(None))

    def emit(k, values):
        moved[:, k * lons:(k + 1) * lons] = values

    sweep_columns(
        lambda k: choose(k, group, lons, low, main, high), tables, step * group,
        pick_mats(mats, mats_a, mats_b, group), held, emit, group,
    )
    sums = dot(packer[...], jnp.concatenate(split(moved[...]), axis=0))
    count = out.shape[0]
    rows = padded(count, 16)
    extra = padded(count // 2, 16)
    out[:extra] = sums[:extra] + sums[rows:]
    out[extra:] = sums[extra:count]


def local_kernel(group, steps_all, count, blocks, tables, mats, mats_a, mats_b, row_mats, rates, signs, low, main, high,
                 chip_low, chip_main, chip_high, chip_halos, *refs):
    halos = refs[:count]
    out, held, moved, stage = refs[-4:]
    lons = tables.shape[-1]
    side = 2 * lons
    step = pl.program_id(0)
    lats = row_mats.shape[0] - 2
    part = held.shape[0]
    weights = pick_mats(mats, mats_a, mats_b, group)
    chip_above = blocks[1] > 0
    top = (lats + 2) * lons

    @pl.when(pl.program_id(0) == 0)
    def _():
        moved[pl.ds(pl.multiple_of(jnp.where(chip_above, 0, top), lons), side), :] = jnp.zeros(
            (side, group * lons), F32
        )

    def sweep(value, held_here, first_row, count):
        def emit(k, values):
            moved[pl.ds(first_row, count), k * lons:(k + 1) * lons] = values

        sweep_columns(value, tables, step * group, weights, held_here, emit, group)

    def one(block, carry):
        first_row = pl.multiple_of(block * part, part)
        choose = edge_choice(step, steps_all - 1, halos, blocks[2], pl.ds(first_row, part))
        sweep(
            lambda k: choose(k, group, lons, low, main, high), held,
            pl.multiple_of(first_row + side, side), part,
        )
        return carry

    lax.fori_loop(0, main.shape[0] // part, one, 0)
    chip_sides = [chip_halos.at[:, at * side:(at + 1) * side] for at in range(count)]
    choose_chip = edge_choice(step, steps_all - 1, chip_sides, blocks[2], slice(None))
    sweep(
        lambda k: choose_chip(k, group, lons, chip_low, chip_main, chip_high), held.at[:side],
        pl.multiple_of(jnp.where(chip_above, top, 0), lons), side,
    )

    def wide(ref, at):
        return jnp.concatenate([ref[at]] * group, axis=1)

    def lat_of(ref, at):
        return ref[at * lons:(at + 1) * lons, :]

    for lat in range(-1, lats + 1):
        near = [lat_of(moved, at) for at in (lat + 1, lat + 2, lat + 3)]
        start = blend(near[1], wide(rates, lat + 1), wide(signs, lat + 1), near[0], near[2])
        both = dot(row_mats[lat + 1], jnp.concatenate(split(start), axis=0))
        stage[(lat + 1) * lons:(lat + 2) * lons, :] = both[:lons] + both[lons:]
        if lat >= 1:
            done = lat - 1
            below, center, above = (lat_of(stage, done + s) for s in range(3))
            out[done * lons:(done + 1) * lons, :] = blend(
                center, wide(rates, done + 1), wide(signs, done + 1), below, above
            )


def add_kernel(blocks, adder, received, before, after):
    columns = adder.shape[1] // 3
    values = received[...]
    if values.shape[0] < columns:
        rest = jnp.zeros((columns - values.shape[0], values.shape[1]), F32)
        values = jnp.concatenate([values, rest], axis=0)
    high, low = split(values)
    after[...] = before[...] + dot(adder[...], jnp.concatenate([high, high, low], axis=0))


def params():
    return pltpu.CompilerParams(vmem_limit_bytes=VMEM_BYTES)


def whole_spec(shape):
    return pl.BlockSpec(shape, lambda *_: (0,) * len(shape))


def mats_specs(group, place, side):
    return [
        pl.BlockSpec((group, side, side), lambda g, *_: (place(g), 0, 0)),
        pl.BlockSpec((1, side, side), lambda g, *_: (place(g) * group + group, 0, 0)),
        pl.BlockSpec((1, side, side), lambda g, *_: (place(g) * group + group + 1, 0, 0)),
    ]


def window_specs(rows, row_block, group, place, lons, col_blocks):
    half = group // 2
    return [
        pl.BlockSpec((rows, 2 * lons), lambda g, *_: (row_block(*_), jnp.maximum(place(g) * half - 1, 0))),
        pl.BlockSpec((rows, group * lons), lambda g, *_: (row_block(*_), place(g))),
        pl.BlockSpec((rows, 2 * lons), lambda g, *_: (row_block(*_), jnp.minimum((place(g) + 1) * half, col_blocks - 1))),
    ]


def largest_part(total, most):
    return max(part for part in range(1, most + 1) if total % part == 0)


def prepare(sources, counts, first_mat, blocks_last):
    lats, lons = sources[0].shape
    shapes = [jax.ShapeDtypeStruct((5, count, lons), F32) for count in counts]
    scalars = [jax.ShapeDtypeStruct((1,), jnp.int32), jax.ShapeDtypeStruct((3,), jnp.int32)]
    return pl.pallas_call(
        functools.partial(prepare_kernel, first_mat, blocks_last),
        in_specs=[whole_spec(t.shape) for t in sources],
        out_specs=[whole_spec(shape.shape) for shape in shapes] + [pl.BlockSpec(memory_space=pltpu.SMEM)] * 2,
        out_shape=shapes + scalars,
        scratch_shapes=[pltpu.VMEM((5, lats + 24, lons), F32)],
        compiler_params=params(),
        name="prepare",
    )(*sources)


def column_tables(tables, lons):
    total = tables.shape[1]
    return pl.pallas_call(
        column_tables_kernel,
        grid=(total // 8,),
        in_specs=[pl.BlockSpec((tables.shape[0], 8, lons), lambda g: (0, g, 0))],
        out_specs=pl.BlockSpec((8, 2 * lons, 2 * lons), lambda g: (g, 0, 0)),
        out_shape=jax.ShapeDtypeStruct((total, 2 * lons, 2 * lons), BF16),
        compiler_params=params(),
        name="column_tables",
    )(tables)


def early_tables(blocks, tables, col_tables, covariance, kept, count):
    rows, cols = covariance.shape
    lons = tables.shape[-1]
    lats = rows // lons
    side = 2 * lons
    shapes = [
        jax.ShapeDtypeStruct((col_tables.shape[1], side, side), BF16),
        jax.ShapeDtypeStruct((lats + 2, side, side), BF16),
        jax.ShapeDtypeStruct((lats + 2, lons, lons), F32),
        jax.ShapeDtypeStruct((lats + 2, lons, lons), F32),
        jax.ShapeDtypeStruct((padded(2 * kept, 16) + padded(kept, 16), 2 * side), BF16),
        jax.ShapeDtypeStruct((side, 3 * padded(2 * kept, 16)), BF16),
    ]
    copied = [jax.ShapeDtypeStruct((side, cols), F32)] + [jax.ShapeDtypeStruct((rows, side), F32)] * count
    here = pl.BlockSpec(memory_space=pl.ANY)
    return pl.pallas_call(
        functools.partial(early_tables_kernel, kept),
        in_specs=[
            pl.BlockSpec(memory_space=pltpu.SMEM), whole_spec(tables.shape), whole_spec(col_tables.shape), here,
        ],
        out_specs=[whole_spec(shape.shape) for shape in shapes] + [here] * len(copied),
        out_shape=shapes + copied,
        scratch_shapes=[
            pltpu.VMEM((side, cols), F32),
            pltpu.VMEM((count, rows, side), F32),
            pltpu.SemaphoreType.DMA((2, count + 1)),
        ],
        compiler_params=params(),
        name="early_tables",
    )(blocks, tables, col_tables, covariance)


def pack_call(blocks, covariance, tables, mats, mats_first, packer, halos, group, chunk, kept):
    rows, cols = covariance.shape
    lons = tables.shape[-1]
    side = 2 * lons
    steps_all = cols // (group * lons)
    first, steps = chunk

    def place(g):
        return lax.rem(first + g, steps_all)

    def mats_place(g):
        return place(g) - mats_first

    specs = [whole_spec(tables.shape)] + mats_specs(group, mats_place, side) + [whole_spec(packer.shape)]
    specs += window_specs(side, lambda b: b[0], group, place, lons, cols // side)
    specs += [pl.BlockSpec((side, side), lambda g, b: (b[0], 0))] * len(halos)
    return pl.pallas_call(
        functools.partial(pack_kernel, group, place, steps_all, len(halos)),
        grid_spec=pltpu.PrefetchScalarGridSpec(
            num_scalar_prefetch=1,
            grid=(steps,),
            in_specs=specs,
            out_specs=pl.BlockSpec((2 * kept, group * lons), lambda g, *_: (0, g)),
            scratch_shapes=[pltpu.VMEM((side, (group + 2) * lons), F32), pltpu.VMEM((side, group * lons), F32)],
        ),
        out_shape=jax.ShapeDtypeStruct((2 * kept, steps * group * lons), F32),
        compiler_params=params(),
        name="pack_edges",
    )(blocks, tables, mats, mats, mats, packer, covariance, covariance, covariance, *halos)


def local_call(blocks, covariance, tables, mats, row_mats, rates, signs, halos, chip_rows, chip_halos, group):
    rows, cols = covariance.shape
    lons = tables.shape[-1]
    side = 2 * lons
    part = largest_part(rows // side, 2) * side

    steps = cols // (group * lons)

    def place(g):
        return g

    specs = [whole_spec(tables.shape)] + mats_specs(group, place, side)
    specs += [whole_spec(row_mats.shape), whole_spec(rates.shape), whole_spec(signs.shape)]
    specs += window_specs(rows, lambda *_: 0, group, place, lons, cols // side)
    specs += window_specs(side, lambda *_: 0, group, place, lons, cols // side)
    specs += [whole_spec(chip_halos.shape)] + [whole_spec((rows, side))] * len(halos)
    args = [blocks, tables, mats, mats, mats, row_mats, rates, signs, covariance, covariance, covariance]
    args += [chip_rows, chip_rows, chip_rows, chip_halos, *halos]
    return pl.pallas_call(
        functools.partial(local_kernel, group, steps, len(halos)),
        grid_spec=pltpu.PrefetchScalarGridSpec(
            num_scalar_prefetch=1,
            grid=(steps,),
            in_specs=specs,
            out_specs=pl.BlockSpec((rows, group * lons), lambda g, *_: (0, place(g))),
            scratch_shapes=[
                pltpu.VMEM((part, (group + 2) * lons), F32),
                pltpu.VMEM((rows + 2 * side, group * lons), F32),
                pltpu.VMEM((rows + side, group * lons), F32),
            ],
        ),
        out_shape=jax.ShapeDtypeStruct((rows, cols), F32),
        compiler_params=params(),
        name="local_forecast",
    )(*args)


def add_call(blocks, forecast, adder, received, chunk, group):
    side = adder.shape[0]
    width = group * side // 4
    first, steps = (2 * count for count in chunk)
    steps_all = forecast.shape[1] // width
    spot = pl.BlockSpec((side, width), lambda g, b: (b[0], lax.rem(first + g, steps_all)))
    return pl.pallas_call(
        add_kernel,
        grid_spec=pltpu.PrefetchScalarGridSpec(
            num_scalar_prefetch=1,
            grid=(steps,),
            in_specs=[
                whole_spec(adder.shape),
                pl.BlockSpec((received.shape[0], width), lambda g, b: (0, g)),
                spot,
            ],
            out_specs=spot,
        ),
        out_shape=jax.ShapeDtypeStruct(forecast.shape, F32),
        input_output_aliases={3: 0},
        compiler_params=params(),
        name="add_edges",
    )(blocks, adder, received, forecast)


def chunks_of(steps_all):
    if steps_all < 4:
        return [(0, steps_all)]
    start = max(1, (steps_all - 2) // 3)
    middle = steps_all - 2 - start
    return [(1, start), (1 + start, middle), (1 + start + middle, steps_all - start - middle)]


def swaps(axis, start):
    count = lax.axis_size(axis)
    pairs = [(i, i + 1) for i in range(start, count - 1, 2)]
    return pairs + [(b, a) for a, b in pairs]


def forecast_with(kept, covariance, blocks, row_part, col_part, first_part, mat_part):
    rows, cols = covariance.shape
    lons = row_part.shape[-1]
    side = 2 * lons
    group = largest_part(cols // lons, 8)
    steps_all = cols // (group * lons)
    chunks = chunks_of(steps_all)
    cross, chip = swaps("row", 1), swaps("row", 0)
    col_swaps = [pairs for pairs in (swaps("col", 0), swaps("col", 1)) if pairs]
    first_mats, row_mats, rates, signs, packer, adder, chip_rows, *sides = early_tables(
        blocks, row_part, first_part, covariance, kept, len(col_swaps)
    )
    halos = [lax.ppermute(sent, "col", pairs) for sent, pairs in zip(sides, col_swaps)]
    arrived = []

    def pack(chunk, mats, mats_first, halos=()):
        return pack_call(blocks, covariance, col_part, mats, mats_first, packer, halos, group, chunk, kept)

    def send(packed):
        arrived.append(lax.ppermute(packed, "row", cross))

    early = len(chunks) > 1
    if early:
        packed = pack(chunks[0], first_mats, chunks[0][0])
        packed, chip_rows, mat_part = lax.optimization_barrier((packed, chip_rows, mat_part))
        send(packed)
    chip_rows = lax.ppermute(chip_rows, "row", chip)
    mats = column_tables(mat_part, lons)
    for chunk in chunks[early:-1]:
        packed, arrived[0], halos = lax.optimization_barrier((pack(chunk, mats, 0), arrived[0], halos))
        send(packed)
    near = [lax.dynamic_slice_in_dim(halo, blocks[1] * side, side, 0) for halo in halos]
    chip_halos = lax.ppermute(jnp.concatenate(near, axis=1), "row", chip)
    packed, row_mats = lax.optimization_barrier((pack(chunks[-1], mats, 0, halos), row_mats))
    send(packed)
    forecast = local_call(
        blocks, covariance, col_part, mats, row_mats, rates, signs, halos, chip_rows, chip_halos, group
    )
    for chunk, received in zip(chunks, arrived):
        forecast = add_call(blocks, forecast, adder, received, chunk, group)
    return forecast


def per_device(covariance, lon_courant, lat_courant, zonal_upwind_sign, lat_sign, cycle_counts):
    rows, cols = covariance.shape
    lons = lon_courant.shape[1]
    row_lats, col_lats = rows // lons, cols // lons
    group = largest_part(col_lats, 8)
    chunk = chunks_of(col_lats // group)[0]
    counts = (row_lats + 4, col_lats + 4, padded(chunk[1] * group + 2, 8), padded(col_lats + 2, 8))
    sources = (lon_courant, lat_courant, zonal_upwind_sign, lat_sign, cycle_counts[None, :])
    *parts, most, blocks = prepare(sources, counts, chunk[0] * group, rows // (2 * lons) - 1)
    sizes = [lons * part // 32 for part in (19, 22, 32)]
    branch = sum((most[0] > size).astype(jnp.int32) for size in sizes[:-1])
    return lax.switch(
        branch, [functools.partial(forecast_with, size) for size in sizes],
        covariance, blocks, *parts,
    )


def solution(mesh):
    placed = (P("row", "col"), P(), P(), P(), P(), P())
    return jax.shard_map(
        per_device, mesh=mesh, in_specs=placed, out_specs=P("row", "col"), check_vma=False
    )
```
